32 devices in a mesh: seq: 4 (over y, core), fsdp: 8 (over z, x).
Axes of the slice: x: 2, y: 2, z: 4, core: 2. Of those that a mesh axis runs over, the one named last changes fastest.
Arguments:
- tokens: bfloat16 [8, 1024, 1024], P('fsdp', 'seq'), may hold values from -6 to 6
- cotangent: bfloat16 [8, 1024, 1024], P('fsdp', 'seq'), may hold values from -6 to 6
- scene_lengths: int32 [8, 3], P('fsdp'), may hold values from 1 to 1022, as said below
- key_mask: int32 [8, 1024], P('fsdp'), may hold values 0 or 1
- project_in: bfloat16 [1024, 3072], P('fsdp'), may hold values from -0.1875 to 0.1875
- project_out: bfloat16 [1024, 1024], P('fsdp'), may hold values from -1.5 to 1.5
- up_weight: bfloat16 [1024, 4096], P('fsdp'), may hold values from -0.1875 to 0.1875
- down_weight: bfloat16 [4096, 1024], P('fsdp'), may hold values from -0.09375 to 0.09375
- in_gain: bfloat16 [1024], P('fsdp'), may hold values from 0.5 to 1.5
- in_shift: bfloat16 [1024], P('fsdp'), may hold values from -2 to 2
- out_shift: bfloat16 [1024], P('fsdp'), may hold values from -2 to 2
- mid_gain: bfloat16 [1024], P('fsdp'), may hold values from 0.5 to 1.5
- mid_shift: bfloat16 [1024], P('fsdp'), may hold values from -2 to 2
- up_shift: bfloat16 [4096], P('fsdp'), may hold values from -3 to 3
- down_shift: bfloat16 [1024], P('fsdp'), may hold values from -2 to 2
Outputs:
- result: bfloat16 [8, 1024, 1024], P('fsdp', 'seq')
- grad_tokens: bfloat16 [8, 1024, 1024], P('fsdp', 'seq')
- grad_project_in: float32 [1024, 3072], P('fsdp')
- grad_project_out: float32 [1024, 1024], P('fsdp')
- grad_up_weight: float32 [1024, 4096], P('fsdp')
- grad_down_weight: float32 [4096, 1024], P('fsdp')
- grad_in_gain: float32 [1024], P('fsdp')
- grad_in_shift: float32 [1024], P('fsdp')
- grad_out_shift: float32 [1024], P('fsdp')
- grad_mid_gain: float32 [1024], P('fsdp')
- grad_mid_shift: float32 [1024], P('fsdp')
- grad_up_shift: float32 [4096], P('fsdp')
- grad_down_shift: float32 [1024], P('fsdp')
The draws below stay inside these ranges and needn't reach their ends.
Inputs may be any that keep to these rules, and one draw needn't show every extreme that they name: `scene_lengths`: A row sums to 1024; its second entry is the longest, the first and the third are at most 64 (the pieces of scenes cut at the group's ends), and in some row the first entry is 64.
All inputs are finite; a program needn't handle non-finite values. No bound on the sum of `key_mask` on one device may be relied on, other than what follows from the above.
Results may differ from the reference program's by a relative error of at most 0.03.
Values may be sent and summed in bfloat16 or wider, within the bound.
No kernel may reach another device: no remote copies, remote signals or barrier semaphores. Data moves between devices by JAX's collectives and lax.ppermute only.
A program may use at most 192 MiB of HBM per device.

```python
import jax
import jax.numpy as jnp
from jax import lax

D = 1024
HEADS = 16
HEAD_DIM = 64
FF = 4096
TOK_DEV = 256
EDGE = 64
GROUPS = 8
GROUP_TOK = 1024
N_SEQ = 4


def draw_scene_lengths(key, part):
    key = jax.random.fold_in(key, 11)
    streams = jax.random.split(key, 3)
    front = jax.random.randint(streams[0], (GROUPS,), 1, EDGE + 1)
    back = jax.random.randint(streams[1], (GROUPS,), 1, EDGE + 1)
    chosen = jax.random.randint(streams[2], (), 0, GROUPS)
    groups = jnp.arange(GROUPS)
    front = jnp.where(groups == chosen, 1, front)
    back = jnp.where(groups == chosen, 1, back)
    front = jnp.where(groups == (chosen + 1) % GROUPS, EDGE, front)
    spanning = GROUP_TOK - front - back
    return jnp.stack([front, spanning, back], axis=1).astype(jnp.int32)


def with_ends(array, own_key, smallest, high):
    extent = array.shape
    place = [jax.random.randint(jax.random.fold_in(own_key, axis), (), 0, extent[axis]) for axis in range(len(extent))]
    array = array.at[tuple(place)].set(smallest)
    longest = extent.index(max(extent))
    place[longest] = (place[longest] + 1) % extent[longest]
    return array.at[tuple(place)].set(high)


def levels(rng, shape, cuts, low, top_value):
    def one(dim, shards_of):
        heights = jax.random.uniform(jax.random.fold_in(jax.random.fold_in(rng, 6), dim), (shards_of,), jnp.float32, low / len(cuts), top_value / len(cuts))
        return jnp.repeat(jnp.exp(heights), shape[dim] // shards_of).reshape((-1,) + (1,) * (len(shape) - dim - 1))

    level = one(*cuts[0])
    for cut in cuts[1:]:
        level = level * one(*cut)
    return level


def centred(rng, extent, deviation, limit, cuts=(), kind=jnp.bfloat16):
    level = levels(rng, extent, cuts, -0.22, 0.18) if cuts else 1.0
    array = jax.random.normal(rng, extent, jnp.float32) * deviation * level
    return jnp.minimum(jnp.maximum(array, -limit), limit).astype(kind)


def setup_inputs(seed: int = 0) -> dict:
    arg_keys = jax.random.split(jax.random.key(seed), 16)
    return {
        "tokens": centred(arg_keys[0], (GROUPS, GROUP_TOK, D), 1.0, 6.0, ((0, 8), (1, 4))),
        "cotangent": centred(arg_keys[1], (GROUPS, GROUP_TOK, D), 1.0, 6.0, ((0, 8), (1, 4))),
        "scene_lengths": draw_scene_lengths(jax.random.fold_in(arg_keys[15], 71), 0),
        "key_mask": with_ends((jax.random.randint(arg_keys[3], (GROUPS, GROUP_TOK), 0, 4) < 3).astype(jnp.int32), jax.random.fold_in(arg_keys[3], 1), 0, 1),
        "project_in": centred(arg_keys[4], (D, 3 * D), D ** -0.5, 0.1875, ((0, 8),)),
        "project_out": centred(arg_keys[5], (D, D), (max(1, D * 16 // (TOK_DEV * N_SEQ))) ** -0.5, 1.5, ((0, 8),)),
        "up_weight": centred(arg_keys[6], (D, FF), D ** -0.5, 0.1875, ((0, 8),)),
        "down_weight": centred(arg_keys[7], (FF, D), FF ** -0.5, 0.09375, ((0, 8),)),
        "in_gain": jnp.clip(1.0 + 0.1 * jax.random.normal(arg_keys[8], (D,), jnp.float32), 0.5, 1.5).astype(jnp.bfloat16),
        "in_shift": centred(arg_keys[9], (D,), 0.3, 2.0, ((0, 8),)),
        "out_shift": centred(arg_keys[10], (D,), 0.3, 2.0, ((0, 8),)),
        "mid_gain": jnp.clip(1.0 + 0.1 * jax.random.normal(arg_keys[11], (D,), jnp.float32), 0.5, 1.5).astype(jnp.bfloat16),
        "mid_shift": centred(arg_keys[12], (D,), 0.3, 2.0, ((0, 8),)),
        "up_shift": centred(arg_keys[13], (FF,), 0.5, 3.0, ((0, 8),)),
        "down_shift": centred(arg_keys[14], (D,), 0.3, 2.0, ((0, 8),)),
    }


@jax.custom_vjp
def low(v):
    return lax.optimization_barrier(v.astype(jnp.bfloat16)).astype(jnp.float32)

@jax.custom_vjp
def low_back(v):
    return v

def low_keep(v):
    return (low(v), None)

def low_pass(kept, grad):
    return (grad,)

def back_keep(v):
    return (v, None)

def back_low(kept, grad):
    return (low(grad),)
low.defvjp(low_keep, low_pass)
low_back.defvjp(back_keep, back_low)
epsilon = 1e-05
masked_score = -1e+30
highest = lax.Precision.HIGHEST

def layer_norm(values, gain, shift):
    center = values - lax.optimization_barrier(jnp.mean(values, axis=-1, keepdims=True))
    spread = lax.optimization_barrier(jnp.mean(center * center, axis=-1, keepdims=True))
    return center * lax.rsqrt(spread + epsilon) * gain + shift

def scene_tables(lengths, key_mask):
    ends = jnp.cumsum(lengths)
    starts = ends - lengths
    places = jnp.arange(key_mask.shape[0], dtype=jnp.int32)
    scene = lax.optimization_barrier(jnp.sum((places[:, None] >= ends[None, :]).astype(jnp.int32), axis=1))
    first = jnp.any(places[:, None] == starts[None, :], axis=1)
    return (scene, (key_mask == 1) | first)

def attend_block(query, query_scene, keys, values, key_scene, keep):
    scores = low_back(jnp.einsum('qhd,khd->hqk', query, keys, precision=highest) * HEAD_DIM ** (-0.5))
    allowed = ((query_scene[:, None] == key_scene[None, :]) & keep[None, :])[None]
    scores = jnp.where(allowed, scores, masked_score)
    top = lax.optimization_barrier(jnp.max(scores, axis=-1, keepdims=True))
    weights = jnp.exp(scores - top)
    total = lax.optimization_barrier(jnp.sum(weights, axis=-1))
    summed = jnp.einsum('hqk,khd->qhd', low(weights), values, precision=highest)
    return summed / jnp.transpose(total)[:, :, None]

def attend_group(parts):
    query, keys, values, scene, keep = parts
    blocks = GROUP_TOK // TOK_DEV

    def one_block(block):
        return attend_block(block[0], block[1], keys, values, scene, keep)
    outcome = lax.map(jax.checkpoint(one_block), (query.reshape(blocks, TOK_DEV, HEADS, HEAD_DIM), scene.reshape(blocks, TOK_DEV)))
    return outcome.reshape(GROUP_TOK, HEADS * HEAD_DIM)

def forward(tokens, project_in, project_out, up_weight, down_weight, in_gain, in_shift, out_shift, mid_gain, mid_shift, up_shift, down_shift, scene, keep):
    normed = low(layer_norm(tokens, in_gain, in_shift))
    mixed = low(low_back(jnp.einsum('gtd,de->gte', normed, project_in, precision=highest)))
    shape = (GROUPS, GROUP_TOK, HEADS, HEAD_DIM)
    query = mixed[:, :, :D].reshape(shape)
    keys = mixed[:, :, D:2 * D].reshape(shape)
    values = mixed[:, :, 2 * D:].reshape(shape)
    attended = lax.map(jax.checkpoint(attend_group), (query, keys, values, scene, keep))
    attended = low(low_back(attended))
    branch = low_back(jnp.einsum('gtd,de->gte', attended, project_out, precision=highest) + out_shift)
    middle = tokens + branch
    normed_mid = low(layer_norm(middle, mid_gain, mid_shift))
    hidden = low_back(jnp.einsum('gtd,df->gtf', normed_mid, up_weight, precision=highest) + up_shift)
    active = low(jax.nn.gelu(hidden, approximate=False))
    return middle + jnp.einsum('gtf,fd->gtd', active, down_weight, precision=highest) + down_shift

def reference(tokens, cotangent, scene_lengths, key_mask, project_in, project_out, up_weight, down_weight, in_gain, in_shift, out_shift, mid_gain, mid_shift, up_shift, down_shift):
    scene, keep = jax.vmap(scene_tables)(scene_lengths, key_mask)
    primals = [item.astype(jnp.float32) for item in (tokens, project_in, project_out, up_weight, down_weight, in_gain, in_shift, out_shift, mid_gain, mid_shift, up_shift, down_shift)]

    def closed(*items):
        return forward(*items, scene, keep)
    result, pull = jax.vjp(closed, *primals)
    grads = pull(cotangent.astype(jnp.float32))
    return (result.astype(jnp.bfloat16), grads[0].astype(jnp.bfloat16), grads[1], grads[2], grads[3], grads[4], grads[5], grads[6], grads[7], grads[8], grads[9], grads[10], grads[11])
```

```python
import functools
import math

import jax
import jax.numpy as jnp
from jax import lax
from jax.experimental import pallas as pl
from jax.experimental.pallas import tpu as pltpu
from jax.sharding import PartitionSpec as P


HEADS = 16
HEAD_DIM = 64
EPSILON = 1e-05
MASKED = -1e30
MIB = 1 << 20
F32 = jnp.float32
BF16 = jnp.bfloat16
LOG2E = math.log2(math.e)
HBM = pl.BlockSpec(memory_space=pl.ANY)


def ring_order(count):
    wide = max(count // 4, 1)
    tall = count // wide
    path = [(row, 0) for row in range(tall)]
    for row in reversed(range(tall)):
        columns = list(range(1, wide))
        if (tall - 1 - row) % 2:
            columns.reverse()
        path += [(row, column) for column in columns]
    return [row * wide + column for row, column in path]


def ring_steps(order):
    onward = list(zip(order, order[1:] + order[:1]))
    return onward, [(target, source) for source, target in onward]


def ring_gather(block, order, cut):
    onward, backward = ring_steps(order)
    count = len(order)
    half = count // 2
    parts = [(0, 0, block)]
    left = right = block
    for step in range(1, half):
        left = lax.ppermute(left, "fsdp", onward)
        right = lax.ppermute(right, "fsdp", backward)
        parts += [(count - step, 0, left), (step, 0, right)]
    parts.append((half, 0, lax.ppermute(left[:cut], "fsdp", onward)))
    if cut < block.shape[0]:
        parts.append((half, cut, lax.ppermute(right[cut:], "fsdp", backward)))
    return parts


def plus(left, right):
    return (left.astype(F32) + right.astype(F32)).astype(BF16)


def ring_scatter(pieces, order, cut):
    onward, backward = ring_steps(order)
    count = len(order)
    half = count // 2
    left = lax.ppermute(pieces[half][:cut], "fsdp", onward)
    if cut < pieces.shape[1]:
        right = lax.ppermute(pieces[half][cut:], "fsdp", backward)
    else:
        right = pieces[half][cut:]
    for step in range(1, half):
        near, far = pieces[half - step], pieces[count - half + step]
        if step == 1:
            left = jnp.concatenate([plus(near[:cut], left), near[cut:]])
            right = jnp.concatenate([far[:cut], plus(far[cut:], right)])
        else:
            left, right = plus(near, left), plus(far, right)
        left = lax.ppermute(left, "fsdp", onward)
        right = lax.ppermute(right, "fsdp", backward)
    return (pieces[0].astype(F32) + left.astype(F32) + right.astype(F32)).astype(BF16)


def swap(value, axis, count, bit):
    return lax.ppermute(value, axis, [(i, i ^ bit) for i in range(count)])


def spread(block, count):
    parts = {0: block}
    bit = count // 2
    while bit:
        parts.update({place | bit: swap(part, "seq", count, bit) for place, part in parts.items()})
        bit //= 2
    return [parts[place] for place in range(count)]


def fold(kept, sent, count):
    addends = [kept]
    bit = 1
    while True:
        got = swap(sent, "seq", count, bit)
        addends.append(got)
        bit *= 2
        if bit == count:
            return addends
        sent = sum(part[1::2].astype(F32) for part in addends).astype(BF16)
        addends = [part[0::2] for part in addends]


def sum_all(value, groups, places):
    for axis, count in (("fsdp", groups), ("seq", places)):
        bit = 1
        while bit < count:
            value = value + swap(value, axis, count, bit)
            bit *= 2
    return value


def run(kernel, outs, *, grid, scalars, specs, arrays, out_specs, scratch=(), flops=0, vmem=48):
    moved = sum(math.prod(a.shape) * a.dtype.itemsize for a in (*arrays, *outs))
    return pl.pallas_call(
        kernel,
        out_shape=[jax.ShapeDtypeStruct(o.shape, o.dtype) for o in outs],
        grid_spec=pltpu.PrefetchScalarGridSpec(
            num_scalar_prefetch=1,
            grid=grid,
            in_specs=specs,
            out_specs=out_specs,
            scratch_shapes=list(scratch),
        ),
        compiler_params=pltpu.CompilerParams(vmem_limit_bytes=vmem * MIB),
        cost_estimate=pl.CostEstimate(flops=flops, bytes_accessed=moved, transcendentals=0),
    )(scalars, *arrays)


def shape(dims, dtype=BF16):
    return jax.ShapeDtypeStruct(dims, dtype)


def whole(dims):
    return pl.BlockSpec(dims, lambda *_: (0,) * len(dims))


def dot(left, right):
    return jnp.dot(left, right, preferred_element_type=F32)


def dot_nt(left, right):
    return lax.dot_general(left, right, (((1,), (1,)), ((), ())), preferred_element_type=F32)


def dot_tn(left, right):
    return lax.dot_general(left, right, (((0,), (0,)), ((), ())), preferred_element_type=F32)


def standard(values):
    center = values - jnp.mean(values, axis=-1, keepdims=True)
    spread_of = jnp.mean(center * center, axis=-1, keepdims=True)
    inverse = lax.rsqrt(spread_of + EPSILON)
    return center * inverse, inverse


def norm_pull(grad, gain, unit, inverse):
    slope = grad * gain
    first = jnp.mean(slope, axis=-1, keepdims=True)
    second = jnp.mean(slope * unit, axis=-1, keepdims=True)
    return inverse * (slope - first - unit * second)


def column_sum(values):
    return jnp.sum(values, axis=0, keepdims=True)


def landing(parts, refs, target, places, sems, first=0):
    rows = sum(part.shape[0] for distance, _, part in parts if distance == 0)
    copies = []
    for number, ((distance, start, part), ref) in enumerate(zip(parts, refs)):
        offset = pl.multiple_of(places[distance] * rows + start, 16)
        copies.append(
            pltpu.make_async_copy(
                ref, target.at[pl.ds(offset, part.shape[0])], sems.at[first + number]
            )
        )
    return copies


def project(scalars, tokens, vectors, parts, rows):
    total, width = tokens.shape
    columns = parts[0][2].shape[1]
    share = columns // 3

    def kernel(places, tokens_ref, vectors_ref, *refs):
        held, (normed, query, keys, values, weight, sems) = refs[: len(parts)], refs[len(parts) :]

        @pl.when(pl.program_id(0) == 0)
        def _():
            copies = landing(parts, held, weight, places, sems)
            for copy in copies:
                copy.start()
            for copy in copies:
                copy.wait()

        unit, _ = standard(tokens_ref[...].astype(F32))
        normed[...] = (unit * vectors_ref[0:1, :] + vectors_ref[1:2, :]).astype(BF16)
        mixed = dot(normed[...], weight[...]).astype(BF16)
        query[...] = mixed[:, :share]
        keys[...] = mixed[:, share : 2 * share]
        values[...] = mixed[:, 2 * share :]

    by_rows = lambda w: pl.BlockSpec((rows, w), lambda i, _: (i, 0))
    return run(
        kernel,
        [shape((total, width))] + [shape((total, share))] * 3 + [shape((width, columns))],
        grid=(total // rows,),
        scalars=scalars,
        specs=[by_rows(width), whole(vectors.shape)] + [HBM] * len(parts),
        arrays=[tokens, vectors] + [part for _, _, part in parts],
        out_specs=[by_rows(width)] + [by_rows(share)] * 3 + [whole((width, columns))],
        scratch=[pltpu.SemaphoreType.DMA((len(parts),))],
        flops=2 * total * width * columns,
    )


def split_three(values):
    high = values.astype(BF16)
    rest = values - high.astype(F32)
    middle = rest.astype(BF16)
    return high, middle, (rest - middle.astype(F32)).astype(BF16)


def attend(scalars, query, keys, values, query_mask, key_mask):
    total, share = query.shape
    wide = min(share, 2 * HEAD_DIM)
    rows = min(total, 256)
    scale = HEAD_DIM**-0.5

    def kernel(_, q_ref, k_ref, v_ref, qm_ref, km_ref, attended, extra):
        ones = jnp.ones((total, HEAD_DIM), BF16)
        place = lax.broadcasted_iota(jnp.int32, (rows, HEAD_DIM), 1)
        outs, extras = [], []
        for head in range(wide // HEAD_DIM):
            lanes = slice(head * HEAD_DIM, (head + 1) * HEAD_DIM)
            q = jnp.concatenate([q_ref[:, lanes], qm_ref[...]], axis=1)
            k = jnp.concatenate([k_ref[:, lanes], km_ref[...]], axis=1)
            v = jnp.concatenate([v_ref[:, lanes], ones], axis=1)
            scores = dot_nt(q, k)
            top = jnp.max(scores, axis=1, keepdims=True)
            weights = jnp.exp2((scores - top) * (LOG2E * scale)).astype(BF16)
            summed = dot(weights, v)
            amount = summed[:, HEAD_DIM : HEAD_DIM + 1]
            outs.append(summed[:, :HEAD_DIM] / amount)
            high, middle, low = split_three(top + jnp.log(amount) / scale)
            extras.append(
                jnp.where(
                    place == 3,
                    high,
                    jnp.where(place == 4, middle, jnp.where(place == 5, low, qm_ref[...])),
                )
            )
        attended[...] = jnp.concatenate(outs, axis=1).astype(BF16)
        extra[...] = jnp.concatenate(extras, axis=1)

    by_rows = pl.BlockSpec((rows, wide), lambda p, i, _: (i, p))
    fixed = pl.BlockSpec((total, wide), lambda p, i, _: (0, p))
    return run(
        kernel,
        [shape((total, share))] * 2,
        grid=(share // wide, total // rows),
        scalars=scalars,
        specs=[
            by_rows,
            fixed,
            fixed,
            pl.BlockSpec((rows, HEAD_DIM), lambda p, i, _: (i, 0)),
            whole((total, HEAD_DIM)),
        ],
        arrays=[query, keys, values, query_mask, key_mask],
        out_specs=[by_rows, by_rows],
        flops=4 * 4 * total * total * share,
    )


def feed(scalars, attended, tokens, cotangent, vectors, up_shift, out_weight, ups, downs, rows):
    places_along = len(attended)
    total, width = tokens.shape
    share = attended[0].shape[1]
    units = up_shift.shape[1]
    count = len(ups) + len(downs)
    own = scalars.shape[0] - 1

    def kernel(places, *refs):
        attended_refs = refs[:places_along]
        tokens_ref, cot_ref, vectors_ref, shift_ref, out_ref = refs[places_along : places_along + 5]
        held = refs[places_along + 5 : places_along + 5 + count]
        (
            gathered,
            normed,
            active,
            grad_hidden,
            middle_own,
            kept,
            sent,
            grad_shift,
            down,
            up,
            sems,
        ) = refs[places_along + 5 + count :]
        step = pl.program_id(0)

        @pl.when(step == 0)
        def _():
            copies = landing(ups, held[: len(ups)], up, places, sems)
            copies += landing(downs, held[len(ups) :], down, places, sems, len(ups))
            for copy in copies:
                copy.start()
            for copy in copies:
                copy.wait()

        branch = vectors_ref[2:3, :]
        for place, ref in enumerate(attended_refs):
            part = ref[...]
            gathered[:, place * share : (place + 1) * share] = part
            start = pl.multiple_of((places[own] ^ place) * share, share)
            branch = branch + dot(part, out_ref[pl.ds(start, share), :])
        middle = tokens_ref[...].astype(F32) + branch

        @pl.when(step == 0)
        def _():
            middle_own[...] = middle
            grad_shift[...] = jnp.zeros_like(grad_shift)

        unit, _ = standard(middle)
        normed[...] = (unit * vectors_ref[3:4, :] + vectors_ref[4:5, :]).astype(BF16)
        hidden = dot(normed[...], up[...]) + shift_ref[...]
        share_of = 0.5 + 0.5 * lax.erf(hidden * (0.5**0.5))
        active[...] = (hidden * share_of).astype(BF16)
        slope = share_of + hidden * (
            jnp.exp2(hidden * hidden * (-0.5 * LOG2E)) * ((2 * math.pi) ** -0.5)
        )
        grad = (slope * dot_nt(cot_ref[...], down[...])).astype(BF16)
        grad_hidden[...] = grad
        grad_shift[...] += column_sum(grad.astype(F32))
        grad_normed = dot_nt(grad, up[...]).astype(BF16)

        @pl.when(step % 2 == 0)
        def _():
            kept[step // 2] = grad_normed

        @pl.when(step % 2 == 1)
        def _():
            sent[step // 2] = grad_normed

    by_rows = lambda w: pl.BlockSpec((rows, w), lambda i, _: (i, 0))
    part_of = lambda x: pl.BlockSpec((rows, share), lambda i, _: (i ^ x, 0))
    halves = (places_along // 2, rows, width)
    return run(
        kernel,
        [
            shape((total, width)),
            shape((total, width)),
            shape((total, units)),
            shape((total, units)),
            shape((rows, width), F32),
            shape(halves),
            shape(halves),
            shape((1, units), F32),
            shape((units, width)),
        ],
        grid=(places_along,),
        scalars=scalars,
        specs=[part_of(x) for x in range(places_along)]
        + [
            by_rows(width),
            by_rows(width),
            whole(vectors.shape),
            whole(up_shift.shape),
            whole(out_weight.shape),
        ]
        + [HBM] * count,
        arrays=[*attended, tokens, cotangent, vectors, up_shift, out_weight]
        + [part for _, _, part in (*ups, *downs)],
        out_specs=[
            by_rows(width),
            by_rows(width),
            by_rows(units),
            by_rows(units),
            whole((rows, width)),
            whole(halves),
            whole(halves),
            whole((1, units)),
            whole((units, width)),
        ],
        scratch=[pltpu.VMEM((width, units), BF16), pltpu.SemaphoreType.DMA((count,))],
        flops=2 * total * width * (width + 3 * units),
        vmem=56,
    )


def descend(scalars, active, down, rows):
    total, units = active.shape
    width = down.shape[1]

    def kernel(_, active_ref, down_ref, kept, sent):
        step = pl.program_id(0)
        part = dot(active_ref[...], down_ref[...]).astype(BF16)

        @pl.when(step % 2 == 0)
        def _():
            kept[step // 2] = part

        @pl.when(step % 2 == 1)
        def _():
            sent[step // 2] = part

    halves = (total // rows // 2, rows, width)
    return run(
        kernel,
        [shape(halves)] * 2,
        grid=(total // rows,),
        scalars=scalars,
        specs=[pl.BlockSpec((rows, units), lambda i, _: (i, 0)), whole(down.shape)],
        arrays=[active, down],
        out_specs=[whole(halves)] * 2,
        flops=2 * total * units * width,
    )


def outer(scalars, left, right, count):
    total, height = left.shape
    width = right.shape[1]
    rows = min(height, 256)
    piece = height // count

    def kernel(places, left_ref, right_ref, out):
        product = dot_tn(left_ref[...], right_ref[...]).astype(BF16)
        for part in range(rows // piece):
            number = pl.program_id(0) * (rows // piece) + part
            out[places[count + number]] = product[part * piece : (part + 1) * piece]

    return run(
        kernel,
        [shape((count, piece, width))],
        grid=(height // rows,),
        scalars=scalars,
        specs=[pl.BlockSpec((total, rows), lambda i, _: (0, i)), whole(right.shape)],
        arrays=[left, right],
        out_specs=[whole((count, piece, width))],
        flops=2 * total * height * width,
    )[0]


def middle_back(scalars, addends, middle, cotangent, vectors):
    rows, width = middle.shape
    block = min(rows, 128)

    def kernel(_, *refs):
        parts = refs[: len(addends)]
        middle_ref, cot_ref, vectors_ref, grad_middle, grad_branch, sums = refs[len(addends) :]
        grad = sum(part[0].astype(F32) for part in parts)
        cot = cot_ref[...].astype(F32)
        unit, inverse = standard(middle_ref[...])
        total = cot + norm_pull(grad, vectors_ref[3:4, :], unit, inverse)
        grad_middle[...] = total
        branch = total.astype(BF16)
        grad_branch[...] = branch

        @pl.when(pl.program_id(0) == 0)
        def _():
            sums[...] = jnp.zeros_like(sums)

        sums[0:1, :] += column_sum(branch.astype(F32))
        sums[1:2, :] += column_sum(grad * unit)
        sums[2:3, :] += column_sum(grad)
        sums[3:4, :] += column_sum(cot)

    by_rows = pl.BlockSpec((block, width), lambda i, _: (i, 0))
    return run(
        kernel,
        [shape((rows, width), F32), shape((rows, width)), shape((8, width), F32)],
        grid=(rows // block,),
        scalars=scalars,
        specs=[pl.BlockSpec((1, block, width), lambda i, _: (0, i, 0))] * len(addends)
        + [by_rows, by_rows, whole(vectors.shape)],
        arrays=[*addends, middle, cotangent, vectors],
        out_specs=[by_rows, by_rows, whole((8, width))],
    )


def attended_back(scalars, branches, out_weight, attended):
    count = len(branches)
    total, share = attended.shape
    rows, width = branches[0].shape
    own = scalars.shape[0] - 1

    def kernel(_, *refs):
        parts = refs[:count]
        out_ref, attended_ref, grads, extras = refs[count:]
        place = lax.broadcasted_iota(jnp.int32, (rows, HEAD_DIM), 1)
        for number, part in enumerate(parts):
            span = slice(number * rows, (number + 1) * rows)
            grad = dot_nt(part[...], out_ref[...]).astype(BF16)
            grads[span, :] = grad
            product = grad.astype(F32) * attended_ref[span, :].astype(F32)
            columns = []
            for head in range(share // HEAD_DIM):
                lanes = slice(head * HEAD_DIM, (head + 1) * HEAD_DIM)
                delta = jnp.sum(product[:, lanes], axis=1, keepdims=True)
                high, middle, low = split_three(delta)
                zero = jnp.zeros((rows, HEAD_DIM), BF16)
                columns.append(
                    jnp.where(
                        place == 3,
                        high,
                        jnp.where(place == 4, middle, jnp.where(place == 5, low, zero)),
                    )
                )
            extras[span, :] = jnp.concatenate(columns, axis=1)

    return run(
        kernel,
        [shape((total, share))] * 2,
        grid=(1,),
        scalars=scalars,
        specs=[whole((rows, width))] * count
        + [pl.BlockSpec((share, width), lambda i, w: (w[own], 0)), whole((total, share))],
        arrays=[*branches, out_weight, attended],
        out_specs=[whole((total, share))] * 2,
        flops=2 * total * width * share,
    )


def attend_back(scalars, query, extra, keys, key_mask, values, grads, grad_extra):
    total, share = query.shape
    wide = min(share, 2 * HEAD_DIM)
    rows = min(total, 256)
    scale = HEAD_DIM**-0.5

    def kernel(_, q_ref, qx_ref, k_ref, km_ref, v_ref, g_ref, gx_ref, dq_ref, dk_ref, dv_ref, held):
        step = pl.program_id(1)
        grad_keys, grad_values = [], []
        for head in range(wide // HEAD_DIM):
            lanes = slice(head * HEAD_DIM, (head + 1) * HEAD_DIM)
            query_part, key_part, grad_part = q_ref[:, lanes], k_ref[:, lanes], g_ref[:, lanes]
            q = jnp.concatenate([query_part, qx_ref[:, lanes]], axis=1)
            k = jnp.concatenate([key_part, km_ref[...]], axis=1)
            g = jnp.concatenate([grad_part, gx_ref[:, lanes]], axis=1)
            v = jnp.concatenate([v_ref[:, lanes], jnp.maximum(km_ref[...], -1.0)], axis=1)
            shares = jnp.exp2(dot_nt(k, q) * (LOG2E * scale))
            grad_scores = (shares * dot_nt(v, g)).astype(BF16)
            grad_values.append(dot(shares.astype(BF16), grad_part))
            grad_keys.append(dot(grad_scores, query_part) * scale)
            update = dot_tn(key_part, grad_scores) * scale

            @pl.when(step == 0)
            def _():
                held[lanes, :] = update

            @pl.when(step > 0)
            def _():
                held[lanes, :] += update

        dk_ref[...] = jnp.concatenate(grad_keys, axis=1).astype(BF16)
        dv_ref[...] = jnp.concatenate(grad_values, axis=1).astype(BF16)

        @pl.when(step == pl.num_programs(1) - 1)
        def _():
            dq_ref[...] = held[...].T.astype(BF16)

    by_rows = pl.BlockSpec((rows, wide), lambda p, i, _: (i, p))
    fixed = pl.BlockSpec((total, wide), lambda p, i, _: (0, p))
    return run(
        kernel,
        [shape((total, share))] * 3,
        grid=(share // wide, total // rows),
        scalars=scalars,
        specs=[
            fixed,
            fixed,
            by_rows,
            pl.BlockSpec((rows, HEAD_DIM), lambda p, i, _: (i, 0)),
            by_rows,
            fixed,
            fixed,
        ],
        arrays=[query, extra, keys, key_mask, values, grads, grad_extra],
        out_specs=[fixed, by_rows, by_rows],
        scratch=[pltpu.VMEM((wide, total), F32)],
        flops=10 * 4 * total * total * share,
    )


def projection_grads(scalars, normed, mixed, gathered, branches, count):
    total, width = normed.shape
    share = mixed[0].shape[1]
    rows = min(width, 256)
    piece = width // count
    block = branches[0].shape[0]
    own = scalars.shape[0] - 1
    per = share // piece
    column = pl.BlockSpec((block, share), lambda i, w: (0, w[own]))
    if share % 128:
        column = whole((block, share))
        branches = [
            lax.dynamic_slice_in_dim(part, scalars[own] * share, share, 1) for part in branches
        ]

    def kernel(places, normed_ref, gathered_ref, q_ref, k_ref, v_ref, *refs):
        parts, out = refs[: len(branches)], refs[len(branches)]
        step = pl.program_id(0)
        left = normed_ref[...]
        products = [dot_tn(left, ref[...]).astype(BF16) for ref in (q_ref, k_ref, v_ref)]
        branch = 0.0
        for number, part in enumerate(parts):
            branch = branch + dot_tn(
                gathered_ref[number * block : (number + 1) * block, :], part[...]
            )
        branch = branch.astype(BF16)
        for part in range(rows // piece):
            span = slice(part * piece, (part + 1) * piece)
            number = step * (rows // piece) + part
            target = places[count + number]
            for place, product in enumerate(products):
                out[target, :, place * share : (place + 1) * share] = product[span]
            natural = ((number // per) ^ places[own]) * per + number % per
            out[places[count + natural], :, 3 * share :] = branch[span]

    return run(
        kernel,
        [shape((count, piece, 4 * share))],
        grid=(width // rows,),
        scalars=scalars,
        specs=[pl.BlockSpec((total, rows), lambda i, _: (0, i))] * 2
        + [whole((total, share))] * 3
        + [column] * len(branches),
        arrays=[normed, gathered, *mixed, *branches],
        out_specs=[whole((count, piece, 4 * share))],
        flops=2 * total * width * 4 * share,
    )[0]


def normed_back(scalars, mixed, weight, tokens, rows):
    total, width = tokens.shape
    share = mixed[0].shape[1]

    def kernel(_, q_ref, k_ref, v_ref, weight_ref, tokens_ref, kept, sent, sums):
        step = pl.program_id(0)
        grad = 0.0
        for place, ref in enumerate((q_ref, k_ref, v_ref)):
            lanes = slice(place * share, (place + 1) * share)
            grad = grad + dot_nt(ref[...], weight_ref[:, lanes])
        unit, _ = standard(tokens_ref[...].astype(F32))

        @pl.when(step == 0)
        def _():
            sums[...] = jnp.zeros_like(sums)

        sums[0:1, :] += column_sum(grad * unit)
        sums[1:2, :] += column_sum(grad)

        @pl.when(step % 2 == 0)
        def _():
            kept[step // 2] = grad.astype(BF16)

        @pl.when(step % 2 == 1)
        def _():
            sent[step // 2] = grad.astype(BF16)

    by_rows = lambda w: pl.BlockSpec((rows, w), lambda i, _: (i, 0))
    halves = (total // rows // 2, rows, width)
    return run(
        kernel,
        [shape(halves), shape(halves), shape((8, width), F32)],
        grid=(total // rows,),
        scalars=scalars,
        specs=[by_rows(share)] * 3 + [whole(weight.shape), by_rows(width)],
        arrays=[*mixed, weight, tokens],
        out_specs=[whole(halves), whole(halves), whole((8, width))],
        flops=2 * total * width * 3 * share,
    )


def tokens_back(scalars, addends, tokens, grad_middle, vectors):
    rows, width = tokens.shape
    block = min(rows, 128)

    def kernel(_, *refs):
        parts = refs[: len(addends)]
        tokens_ref, middle_ref, vectors_ref, out = refs[len(addends) :]
        grad = sum(part[0].astype(F32) for part in parts)
        unit, inverse = standard(tokens_ref[...].astype(F32))
        pulled = norm_pull(grad, vectors_ref[0:1, :], unit, inverse)
        out[...] = (middle_ref[...] + pulled).astype(BF16)

    by_rows = pl.BlockSpec((block, width), lambda i, _: (i, 0))
    return run(
        kernel,
        [shape((rows, width))],
        grid=(rows // block,),
        scalars=scalars,
        specs=[pl.BlockSpec((1, block, width), lambda i, _: (0, i, 0))] * len(addends)
        + [by_rows, by_rows, whole(vectors.shape)],
        arrays=[*addends, tokens, grad_middle, vectors],
        out_specs=[by_rows],
    )[0]


def natural(parts, mine):
    return jnp.take(jnp.stack(parts), mine ^ jnp.arange(len(parts)), axis=0)


def scene_tables(lengths, key_mask):
    ends = jnp.cumsum(lengths)
    starts = ends - lengths
    places = jnp.arange(key_mask.shape[0], dtype=jnp.int32)
    scene = jnp.sum((places[:, None] >= ends[None, :]).astype(jnp.int32), axis=1)
    first = jnp.any(places[:, None] == starts[None, :], axis=1)
    return (scene, (key_mask == 1) | first)


def local(
    groups,
    along,
    tokens,
    cotangent,
    scene_lengths,
    key_mask,
    project_in,
    project_out,
    up_weight,
    down_weight,
    in_gain,
    in_shift,
    out_shift,
    mid_gain,
    mid_shift,
    up_shift,
    down_shift,
):
    rows, width = tokens.shape[1:]
    total = rows * along
    hidden_units = up_weight.shape[1]
    strip = width // groups
    share = width // along
    unit_strip = hidden_units // groups // along
    units = unit_strip * groups
    mine, group = lax.axis_index("seq"), lax.axis_index("fsdp")
    order = ring_order(groups)
    spot = jnp.array([order.index(i) for i in range(groups)], jnp.int32)
    near = (spot[group] + jnp.arange(groups)) % groups
    scalars = jnp.concatenate(
        [
            jnp.array(order, jnp.int32)[near],
            (spot - spot[group]) % groups,
            mine[None],
        ]
    ).astype(jnp.int32)

    pick = lambda array, start: lax.dynamic_slice_in_dim(array, start + mine * share, share, 1)
    in_part = jnp.concatenate([pick(project_in, place * width) for place in range(3)], axis=1)
    out_part = pick(project_out, 0)
    up_part = lax.dynamic_index_in_dim(
        up_weight.reshape(strip, groups, along, unit_strip), mine, 2, keepdims=False
    ).reshape(strip, units)
    down_part = lax.dynamic_index_in_dim(
        down_weight.reshape(along, unit_strip, width), mine, 0, keepdims=False
    )
    up_shift_part = lax.dynamic_slice_in_dim(up_shift, mine * unit_strip, unit_strip)

    cut = max(unit_strip // 2 // 16, 1) * 16

    in_parts = ring_gather(in_part, order, strip // 2)
    own_tokens = tokens[0]
    own_cot = cotangent[0]
    all_tokens = jnp.concatenate(spread(own_tokens, along))

    vectors = jnp.stack(
        [in_gain, in_shift, out_shift, mid_gain, mid_shift, down_shift]
        + [jnp.pad(up_shift_part, (0, strip - unit_strip)), jnp.zeros_like(in_gain)]
    )[None]
    bit = 1
    while bit < groups:
        vectors = jnp.concatenate([vectors, swap(vectors, "fsdp", groups, bit)])
        bit *= 2
    vectors = jnp.take(vectors, group ^ jnp.arange(groups), axis=0).astype(F32)
    up_shift_all = vectors[:, 6, :unit_strip].reshape(1, units)
    vectors = jnp.transpose(vectors, (1, 0, 2)).reshape(8, width)

    scene, keep = scene_tables(scene_lengths[0], key_mask[0])
    nearby = mine ^ jnp.arange(along)
    scene = jnp.take(scene.reshape(along, rows), nearby, axis=0).reshape(total, 1)
    keep = jnp.take(keep.reshape(along, rows), nearby, axis=0).reshape(total, 1)
    place = jnp.arange(HEAD_DIM)[None, :]
    same = scene == place
    query_mask = same.astype(BF16)
    key_table = jnp.where(
        place < 3,
        jnp.where(same & keep, 0.0, MASKED),
        jnp.where(place < 6, -1.0, 0.0),
    ).astype(BF16)

    out_parts = ring_gather(out_part, order, strip // 2)
    up_parts = ring_gather(up_part, order, strip // 2)
    down_parts = ring_gather(down_part, order, cut)

    normed, query, keys, values, in_weight = project(scalars, all_tokens, vectors, in_parts, rows)
    attended, extra = attend(scalars, query, keys, values, query_mask, key_table)
    all_attended = spread(attended, along)

    by_distance = sorted(((d, r, a) for d, r, a in out_parts), key=lambda item: item[:2])
    out_columns = spread(jnp.concatenate([a for _, _, a in by_distance]), along)
    out_weight = natural(out_columns, mine).reshape(along, groups, strip, share)
    out_weight = jnp.take(out_weight, scalars[groups : 2 * groups], axis=1)
    out_weight = jnp.transpose(out_weight, (1, 2, 0, 3)).reshape(width, width)

    all_cot = jnp.concatenate(spread(own_cot, along))
    (gathered, normed_mid, active, grad_hidden, middle, kept, sent, grad_up_shift, down_all) = feed(
        scalars,
        all_attended,
        all_tokens,
        all_cot,
        vectors,
        up_shift_all,
        out_weight,
        up_parts,
        down_parts,
        rows,
    )
    addends = fold(kept, sent, along)
    down_pieces = outer(scalars, active, all_cot, groups)
    up_pieces = outer(scalars, normed_mid, grad_hidden, groups)
    grad_down = ring_scatter(down_pieces, order, cut)
    grad_up = ring_scatter(up_pieces, order, strip // 2)

    grad_middle, grad_branch, middle_sums = middle_back(scalars, addends, middle, own_cot, vectors)
    branches = spread(grad_branch, along)
    grads, grad_extra = attended_back(scalars, branches, out_weight, attended)
    mixed = attend_back(scalars, query, extra, keys, key_table, values, grads, grad_extra)
    pieces = projection_grads(scalars, normed, mixed, gathered, branches, groups)
    grad_both = ring_scatter(pieces, order, strip // 2)
    in_kept, in_sent, in_sums = normed_back(scalars, mixed, in_weight, all_tokens, rows)
    grad_tokens = tokens_back(
        scalars, fold(in_kept, in_sent, along), own_tokens, grad_middle, vectors
    )

    result_kept, result_sent = descend(scalars, active, down_all, rows)
    result = middle + vectors[5:6] + sum(
        part[0].astype(F32) for part in fold(result_kept, result_sent, along)
    )

    up_shift_grad = jnp.zeros((groups, along, unit_strip), F32)
    up_shift_grad = lax.dynamic_update_slice_in_dim(
        up_shift_grad, grad_up_shift.reshape(groups, 1, unit_strip), mine, axis=1
    )
    sums = jnp.concatenate([in_sums[:2], middle_sums[:4]]).reshape(6, groups, strip)
    sums = jnp.concatenate(
        [jnp.transpose(sums, (1, 0, 2)).reshape(groups, -1), up_shift_grad.reshape(groups, -1)],
        axis=1,
    )
    sums = lax.dynamic_index_in_dim(sum_all(sums, groups, along), group, 0, keepdims=False)
    small = [sums[i * strip : (i + 1) * strip] for i in range(6)]

    both = natural(spread(grad_both, along), mine).astype(F32)
    grad_in = jnp.transpose(
        both[:, :, : 3 * share].reshape(along, strip, 3, share), (1, 2, 0, 3)
    ).reshape(strip, 3 * width)
    grad_out = jnp.transpose(both[:, :, 3 * share :], (1, 0, 2)).reshape(strip, width)
    ups = natural(spread(grad_up, along), mine).astype(F32)
    grad_up = jnp.transpose(
        ups.reshape(along, strip, groups, unit_strip), (1, 2, 0, 3)
    ).reshape(strip, hidden_units)
    grad_down = natural(spread(grad_down, along), mine).astype(F32)
    grad_down = grad_down.reshape(along * unit_strip, width)
    return (
        result.astype(BF16)[None],
        grad_tokens[None],
        grad_in,
        grad_out,
        grad_up,
        grad_down,
        small[0],
        small[1],
        small[2],
        small[3],
        small[4],
        sums[6 * strip :],
        small[5],
    )


def solution(mesh):
    by_token = P("fsdp", "seq", None)
    by_row, by_part = P("fsdp", None), P("fsdp")
    return jax.shard_map(
        functools.partial(local, mesh.shape["fsdp"], mesh.shape["seq"]),
        mesh=mesh,
        in_specs=(by_token,) * 2 + (by_row,) * 6 + (by_part,) * 7,
        out_specs=(by_token,) * 2 + (by_row,) * 4 + (by_part,) * 7,
        check_vma=False,
    )
```

```python
import functools
import math

import jax
import jax.numpy as jnp
from jax import lax
from jax.experimental import pallas as pl
from jax.experimental.pallas import tpu as pltpu
from jax.sharding import PartitionSpec as P


HEADS = 16
HEAD_DIM = 64
EPSILON = 1e-05
MASKED = -1e30
MIB = 1 << 20
F32 = jnp.float32
BF16 = jnp.bfloat16
LOG2E = math.log2(math.e)
HBM = pl.BlockSpec(memory_space=pl.ANY)


def ring_order(count):
    wide = max(count // 4, 1)
    tall = count // wide
    path = [(row, 0) for row in range(tall)]
    for row in reversed(range(tall)):
        columns = list(range(1, wide))
        if (tall - 1 - row) % 2:
            columns.reverse()
        path += [(row, column) for column in columns]
    return [row * wide + column for row, column in path]


def order_table(order):
    count = len(order)
    rows = []
    for device in range(count):
        spot = order.index(device)
        rows.append(
            [order[(spot + i) % count] for i in range(count)]
            + [(order.index(i) - spot) % count for i in range(count)]
            + [device]
        )
    return rows


def ring_steps(order):
    onward = list(zip(order, order[1:] + order[:1]))
    return onward, [(target, source) for source, target in onward]


def after(value, *others):
    return lax.optimization_barrier((value, *others))[0] if others else value


def ring_gather(block, order, cut, waits=()):
    onward, backward = ring_steps(order)
    count = len(order)
    half = count // 2
    parts = [(0, 0, block)]
    left = right = block
    waits = dict(enumerate(waits, 2))
    for step in range(1, half):
        if step in waits:
            left, right = lax.optimization_barrier((left, right, *waits[step]))[:2]
        left = lax.ppermute(left, "fsdp", onward)
        right = lax.ppermute(right, "fsdp", backward)
        parts += [(count - step, 0, left), (step, 0, right)]
    if half in waits:
        left, right = lax.optimization_barrier((left, right, *waits[half]))[:2]
    parts.append((half, 0, lax.ppermute(left[:cut], "fsdp", onward)))
    if cut < block.shape[0]:
        parts.append((half, cut, lax.ppermute(right[cut:], "fsdp", backward)))
    return parts


class RingSum:
    def __init__(self, scalars, pieces, order, cut):
        self.scalars, self.pieces = scalars, pieces
        self.onward, self.backward = ring_steps(order)
        self.count, self.step = len(order), 1
        far = [part[self.count // 2] for part in pieces]
        if len(far) == 2 and far[0].shape[0] == cut:
            self.left, self.right = far
        else:
            far = jnp.concatenate(far)
            self.left, self.right = far[:cut], far[cut:]
        self.send()

    def send(self):
        self.left = lax.ppermute(self.left, "fsdp", self.onward)
        if self.right is not None and self.right.shape[0]:
            self.right = lax.ppermute(self.right, "fsdp", self.backward)
        else:
            self.right = None

    def advance(self, *waits):
        if self.step == self.count // 2:
            return []
        left = after(self.left, *waits)
        near, far = self.count // 2 - self.step, self.count // 2 + self.step
        self.left, self.right = merge(self.scalars, self.pieces, near, far, left, self.right)
        sent = [self.left, self.right]
        self.send()
        self.step += 1
        return sent

    def finish(self):
        while self.step < self.count // 2:
            self.advance()
        return merge(self.scalars, self.pieces, 0, None, self.left, self.right)


def swap(value, axis, count, bit):
    return lax.ppermute(value, axis, [(i, i ^ bit) for i in range(count)])


def spread(block, count):
    parts = {0: block}
    bit = count // 2
    while bit:
        parts.update({place | bit: swap(part, "seq", count, bit) for place, part in parts.items()})
        bit //= 2
    return [parts[place] for place in range(count)]


def fold(kept, sent, count):
    addends, sends = [kept], [sent]
    bit = 1
    while True:
        addends.append(swap(sends[-1], "seq", count, bit))
        bit *= 2
        if bit == count:
            return addends, sends
        sends.append(sum(part[1::2].astype(F32) for part in addends).astype(BF16))
        addends = [part[0::2] for part in addends]


def run(kernel, outs, *, grid, scalars, specs, arrays, out_specs, scratch=(), flops=0, vmem=20, kept=None):
    return pl.pallas_call(
        kernel,
        out_shape=[jax.ShapeDtypeStruct(o.shape, o.dtype) for o in outs],
        grid_spec=pltpu.PrefetchScalarGridSpec(
            num_scalar_prefetch=1,
            grid=grid,
            in_specs=specs,
            out_specs=out_specs,
            scratch_shapes=list(scratch),
        ),
        input_output_aliases=kept or {},
        compiler_params=pltpu.CompilerParams(vmem_limit_bytes=vmem * MIB),
        cost_estimate=pl.CostEstimate(flops=0, bytes_accessed=1024, transcendentals=0),
    )(scalars, *arrays)


def shape(dims, dtype=BF16):
    return jax.ShapeDtypeStruct(dims, dtype)


def whole(dims):
    return pl.BlockSpec(dims, lambda *_: (0,) * len(dims))


def dot(left, right):
    return jnp.dot(left, right, preferred_element_type=F32)


def dot_nt(left, right):
    return lax.dot_general(left, right, (((1,), (1,)), ((), ())), preferred_element_type=F32)


def dot_tn(left, right):
    return lax.dot_general(left, right, (((0,), (0,)), ((), ())), preferred_element_type=F32)


def standard(values):
    center = values - jnp.mean(values, axis=-1, keepdims=True)
    spread_of = jnp.mean(center * center, axis=-1, keepdims=True)
    inverse = lax.rsqrt(spread_of + EPSILON)
    return center * inverse, inverse


def norm_pull(grad, gain, unit, inverse):
    slope = grad * gain
    first = jnp.mean(slope, axis=-1, keepdims=True)
    second = jnp.mean(slope * unit, axis=-1, keepdims=True)
    return inverse * (slope - first - unit * second)


def column_sum(values):
    return jnp.sum(values, axis=0, keepdims=True)


def landing(parts, refs, fields, places, sems):
    height = sum(part.shape[0] for distance, _, part in parts if distance == 0)
    copies = []
    for (distance, start, part), ref in zip(parts, refs):
        for (low, high), columns, target in fields:
            high = high or height
            begin, end = max(low, start), min(high, start + part.shape[0])
            if begin >= end:
                continue
            offset = places[distance] * (high - low) + (begin - low)
            source = ref.at[pl.ds(begin - start, end - begin)]
            if columns is not None:
                source = ref.at[pl.ds(begin - start, end - begin), pl.ds(*columns)]
            target = target.at[pl.ds(pl.multiple_of(offset, 16), end - begin)]
            copies.append(pltpu.make_async_copy(source, target, sems.at[len(copies)]))
    return copies


def landings(parts, fields):
    return len(parts) * fields


def wait_all(copies):
    for copy in copies:
        copy.start()
    for copy in copies:
        copy.wait()


def merge(scalars, pieces, near, far, left, right):
    heights = [part.shape[1] for part in pieces]
    height, width = sum(heights), pieces[0].shape[2]
    arrays, specs = [], []
    for distance in (near,) if far is None else (near, far):
        for part, rows in zip(pieces, heights):
            arrays.append(part)
            specs.append(pl.BlockSpec((1, rows, width), lambda i, _, d=distance: (d, 0, 0)))
    sums = [part for part in (left, right) if part is not None]

    def kernel(_, *refs):
        held = refs[: len(arrays)]
        sums_refs = list(refs[len(arrays) : len(arrays) + len(sums)])
        outs = refs[len(arrays) + len(sums) :]
        first = left.shape[0]
        for side, out in enumerate(outs):
            start = 0
            for ref, rows in zip(held[side * len(pieces) :], heights):
                own = ref[0].astype(F32)
                span = slice(start, start + rows)
                if far is None:
                    for part in sums_refs:
                        own = own + part[span, :].astype(F32)
                    out[span, :] = own.astype(BF16)
                elif side < len(sums) and sums[side].shape[0] == height:
                    out[span, :] = (own + sums_refs[side][span, :].astype(F32)).astype(BF16)
                else:
                    out[span, :] = own.astype(BF16)
                start += rows
            if far is not None and side < len(sums) and sums[side].shape[0] < height:
                base = 0 if side == 0 else first
                rows = sums[side].shape[0]
                span = slice(base, base + rows)
                total = out[span, :].astype(F32) + sums_refs[side][...].astype(F32)
                out[span, :] = total.astype(BF16)

    whole_out = whole((height, width))
    count = 1 if far is None else 2
    outs = run(
        kernel,
        [shape((height, width))] * count,
        grid=(1,),
        scalars=scalars,
        specs=specs + [whole(part.shape) for part in sums],
        arrays=arrays + sums,
        out_specs=[whole_out] * count,
    )
    return outs[0] if far is None else outs


def select(scalars, arrays, starts, columns, fields=()):
    rows = arrays[0].shape[0]
    own = scalars.shape[0] - 1
    width = len(starts) * columns
    height = rows + (16 if fields else 0)
    if columns % 128:
        pick = lambda array, start, size: lax.dynamic_slice_in_dim(
            array, (start + scalars[own]) * size, size, 1
        )
        parts = [pick(array, start, columns) for array, start in zip(arrays, starts)]
        parts = jnp.concatenate(parts, axis=1)
        if not fields:
            return parts
        line = lax.dynamic_slice_in_dim(fields[-1], scalars[own], 1, 0)
        below = jnp.concatenate([*fields[:-1], line], axis=1)
        below = jnp.pad(below, ((0, 0), (0, 16 * width - below.shape[1])))
        return jnp.concatenate([parts, below.reshape(16, width)])

    def kernel(places, *refs):
        held = refs[: len(arrays) + len(fields)]
        out, sems, *lines = refs[len(held) :]
        copies = []
        for number, (ref, start) in enumerate(zip(held, starts)):
            begin = pl.multiple_of((start + places[own]) * columns, 128)
            target = out.at[pl.ds(0, rows), pl.ds(number * columns, columns)]
            copies.append((ref.at[:, pl.ds(begin, columns)], target))
        for number, ref in enumerate(held[len(arrays) :]):
            copies.append((ref, lines[number]))
        wait_all(
            [
                pltpu.make_async_copy(source, target, sems.at[number])
                for number, (source, target) in enumerate(copies)
            ]
        )
        if not fields:
            return
        size = lines[0].shape[1]
        per = width // size
        row = lax.broadcasted_iota(jnp.int32, (16, size), 0)
        values = [line[...].astype(F32) for line in lines]
        mine = lax.broadcasted_iota(jnp.int32, values[-1].shape, 0) == places[own]
        values[-1] = column_sum(jnp.where(mine, values[-1], 0.0))
        for start in range(per):
            value = jnp.zeros(row.shape, F32)
            for number in range(start, len(lines), per):
                value = jnp.where(row == number // per, values[number], value)
            out[rows:, start * size : (start + 1) * size] = value.astype(BF16)

    return run(
        kernel,
        [shape((height, width))],
        grid=(1,),
        scalars=scalars,
        specs=[pl.BlockSpec(memory_space=pltpu.HBM)] * (len(arrays) + len(fields)),
        arrays=[*arrays, *fields],
        out_specs=[whole((height, width))],
        scratch=[pltpu.SemaphoreType.DMA((len(arrays) + len(fields),))]
        + [pltpu.VMEM(field.shape, BF16) for field in fields],
        vmem=60 if fields else 20,
    )[0]


def tables(scalars, lengths, key_mask, along):
    total = key_mask.shape[1]
    rows = total // along
    scenes = lengths.shape[1]
    own = scalars.shape[0] - 1

    def kernel(places, lengths_ref, mask_ref, query_table, key_table):
        row = lax.broadcasted_iota(jnp.int32, (HEAD_DIM, rows), 0)
        for number in range(along):
            start = pl.multiple_of((places[own] ^ number) * rows, 128)
            spot = start + lax.broadcasted_iota(jnp.int32, (1, rows), 1)
            keep = mask_ref[:, pl.ds(start, rows)] == 1
            keep = jnp.where(keep, 1.0, 0.0)
            scene = jnp.zeros((1, rows), jnp.int32)
            edge = 0
            for part in range(scenes):
                keep = jnp.where(spot == edge, 1.0, keep)
                edge = edge + lengths_ref[0, part]
                scene = scene + jnp.where(spot >= edge, 1, 0)
            same = jnp.where(row == scene, 1.0, 0.0)
            keys = jnp.where(same * keep > 0.5, 0.0, MASKED)
            keys = jnp.where(row < scenes, keys, jnp.where(row < scenes + 3, -1.0, 0.0))
            span = slice(number * rows, (number + 1) * rows)
            query_table[span, :] = same.T.astype(BF16)
            key_table[span, :] = keys.T.astype(BF16)

    return run(
        kernel,
        [shape((total, HEAD_DIM))] * 2,
        grid=(1,),
        scalars=scalars,
        specs=[pl.BlockSpec(memory_space=pltpu.SMEM), whole(key_mask.shape)],
        arrays=[lengths, key_mask],
        out_specs=[whole((total, HEAD_DIM))] * 2,
    )


def standardize(scalars, tokens):
    rows, width = tokens[0].shape
    total = rows * len(tokens)

    def kernel(_, *refs):
        parts, (unit, joined) = refs[: len(tokens)], refs[len(tokens) :]
        for number, part in enumerate(parts):
            span = slice(number * rows, (number + 1) * rows)
            joined[span, :] = part[...]
            unit[span, :], _ = standard(part[...].astype(F32))

    return run(
        kernel,
        [shape((total, width), F32), shape((total, width))],
        grid=(1,),
        scalars=scalars,
        specs=[whole((rows, width))] * len(tokens),
        arrays=tokens,
        out_specs=[whole((total, width))] * 2,
    )


def field_at(number, strip, columns):
    per = columns // strip
    return number // per, number % per * strip


def project(scalars, unit, parts, rows, strip, unit_strip):
    total, width = unit.shape
    columns = parts[0][2].shape[1]
    share = columns // 4
    groups = width // strip
    count = landings(parts, 3)

    def kernel(places, unit_ref, *refs):
        held = refs[: len(parts)]
        normed, query, keys, values, weight, out_weight, vectors, tail, extra, sems, *joint = refs[
            len(parts) :
        ]

        @pl.when(pl.program_id(0) == 0)
        def _():
            fields = [((strip, strip + 16), None, extra)]
            if joint:
                fields.append(((0, strip), None, joint[0]))
            else:
                fields.append(((0, strip), (0, 3 * share), weight))
                fields.append(((0, strip), (3 * share, share), out_weight))
            wait_all(landing(parts, held, fields, places, sems))
            if joint:
                weight[...] = joint[0][:, : 3 * share]
                out_weight[...] = joint[0][:, 3 * share :]
            for number in range(groups):
                block = extra[number * 16 : (number + 1) * 16, :].astype(F32)
                for field in range(7):
                    row, start = field_at(field, strip, columns)
                    part = block[row : row + 1, start : start + strip]
                    vectors[field : field + 1, number * strip : (number + 1) * strip] = part
                tail[:, number * unit_strip : (number + 1) * unit_strip] = part[:, :unit_strip]

        normed[...] = (unit_ref[...] * vectors[0:1, :] + vectors[1:2, :]).astype(BF16)
        mixed = dot(normed[...], weight[...]).astype(BF16)
        query[...] = mixed[:, :share]
        keys[...] = mixed[:, share : 2 * share]
        values[...] = mixed[:, 2 * share :]

    by_rows = lambda w: pl.BlockSpec((rows, w), lambda i, _: (i, 0))
    return run(
        kernel,
        [shape((total, width))]
        + [shape((total, share))] * 3
        + [shape((width, 3 * share)), shape((width, share))]
        + [shape((8, width), F32), shape((1, groups * unit_strip), F32)],
        grid=(total // rows,),
        scalars=scalars,
        specs=[by_rows(width)] + [HBM] * len(parts),
        arrays=[unit] + [part for _, _, part in parts],
        out_specs=[by_rows(width)]
        + [by_rows(share)] * 3
        + [whole((width, 3 * share)), whole((width, share))]
        + [whole((8, width)), whole((1, groups * unit_strip))],
        scratch=[pltpu.VMEM((groups * 16, columns), BF16), pltpu.SemaphoreType.DMA((count,))]
        + [pltpu.VMEM((width, columns), BF16)] * (share % 128 > 0),
        flops=2 * total * width * 3 * share,
    )


def split_three(values):
    high = values.astype(BF16)
    rest = values - high.astype(F32)
    middle = rest.astype(BF16)
    return high, middle, (rest - middle.astype(F32)).astype(BF16)


def head_pairs(share):
    wide = min(share, 2 * HEAD_DIM)
    return share // wide, wide


def attend(scalars, query, keys, values, query_mask, key_mask, pair, before=()):
    total, share = query.shape
    wide = head_pairs(share)[1]
    rows = min(total, 256)
    scale = HEAD_DIM**-0.5

    def kernel(_, q_ref, k_ref, v_ref, qm_ref, km_ref, *refs):
        attended, extra = refs[len(before) :]
        ones = jnp.ones((total, HEAD_DIM), BF16)
        place = lax.broadcasted_iota(jnp.int32, (rows, HEAD_DIM), 1)
        outs, extras = [], []
        for head in range(wide // HEAD_DIM):
            lanes = slice(head * HEAD_DIM, (head + 1) * HEAD_DIM)
            q = jnp.concatenate([q_ref[:, lanes], qm_ref[...]], axis=1)
            k = jnp.concatenate([k_ref[:, lanes], km_ref[...]], axis=1)
            v = jnp.concatenate([v_ref[:, lanes], ones], axis=1)
            scores = dot_nt(q, k)
            top = jnp.max(scores, axis=1, keepdims=True)
            weights = jnp.exp2((scores - top) * (LOG2E * scale)).astype(BF16)
            summed = dot(weights, v)
            amount = summed[:, HEAD_DIM : HEAD_DIM + 1]
            outs.append(summed[:, :HEAD_DIM] / amount)
            high, middle, low = split_three(top + jnp.log(amount) / scale)
            extras.append(
                jnp.where(
                    place == 3,
                    high,
                    jnp.where(place == 4, middle, jnp.where(place == 5, low, qm_ref[...])),
                )
            )
        attended[...] = jnp.concatenate(outs, axis=1).astype(BF16)
        extra[...] = jnp.concatenate(extras, axis=1)

    by_rows = pl.BlockSpec((rows, wide), lambda i, _: (i, pair))
    fixed = pl.BlockSpec((total, wide), lambda i, _: (0, pair))
    return run(
        kernel,
        [shape((total, share))] * 2,
        grid=(total // rows,),
        scalars=scalars,
        specs=[
            by_rows,
            fixed,
            fixed,
            pl.BlockSpec((rows, HEAD_DIM), lambda i, _: (i, 0)),
            whole((total, HEAD_DIM)),
        ]
        + [HBM] * len(before),
        arrays=[query, keys, values, query_mask, key_mask, *before],
        out_specs=[by_rows, by_rows],
        kept={6 + number: number for number in range(len(before))},
        flops=4 * 4 * total * total * share,
    )


def column_copies(places, refs, target, sems, rows):
    own = places.shape[0] - 1
    if len(refs) == 1:
        return [pltpu.make_async_copy(refs[0].at[rows], target, sems.at[0])]
    columns = refs[0].shape[1]
    return [
        pltpu.make_async_copy(
            ref.at[rows],
            target.at[:, pl.ds(pl.multiple_of((places[own] ^ place) * columns, 128), columns)],
            sems.at[place],
        )
        for place, ref in enumerate(refs)
    ]


def attend_out(scalars, attended, tokens, vectors, outs, rows):
    places_along = len(attended)
    total, width = tokens.shape
    share = attended[0].shape[1]
    own = scalars.shape[0] - 1

    def kernel(places, *refs):
        attended_refs, refs = refs[:places_along], refs[places_along:]
        tokens_ref, vectors_ref = refs[:2]
        held, (gathered, normed, middle_own, out_ref, sems) = (
            refs[2 : 2 + len(outs)],
            refs[2 + len(outs) :],
        )
        step = pl.program_id(0)

        @pl.when(step == 0)
        def _():
            wait_all(column_copies(places, held, out_ref, sems, pl.ds(0, width)))

        for place, ref in enumerate(attended_refs):
            gathered[:, place * share : (place + 1) * share] = ref[...]
        branch = vectors_ref[2:3, :]
        for place in range(places_along):
            start = pl.multiple_of((places[own] ^ place) * share, share)
            branch = branch + dot(attended_refs[place][...], out_ref[pl.ds(start, share), :])
        middle = tokens_ref[...].astype(F32) + branch

        @pl.when(step == 0)
        def _():
            middle_own[...] = middle

        unit, _ = standard(middle)
        normed[...] = (unit * vectors_ref[3:4, :] + vectors_ref[4:5, :]).astype(BF16)

    by_rows = pl.BlockSpec((rows, width), lambda i, _: (i, 0))
    part_of = lambda x: pl.BlockSpec((rows, share), lambda i, _: (i ^ x, 0))
    return run(
        kernel,
        [shape((total, width)), shape((total, width)), shape((rows, width), F32)],
        grid=(places_along,),
        scalars=scalars,
        specs=[part_of(x) for x in range(places_along)]
        + [by_rows, whole(vectors.shape)]
        + [HBM] * len(outs),
        arrays=[*attended, tokens, vectors, *outs],
        out_specs=[by_rows, by_rows, whole((rows, width))],
        scratch=[pltpu.VMEM((width, width), BF16), pltpu.SemaphoreType.DMA((len(outs),))],
        flops=2 * total * width * width,
    )


def feed(scalars, normed, cotangent, up_shift, rings, rows, strip):
    total, width = normed.shape
    units = up_shift.shape[1]
    steps = total // rows
    parts = [part for ring in rings for part in ring]
    signals = 2 * len(parts)

    def kernel(places, *refs):
        normed_ref, cot_ref, shift_ref = refs[:3]
        held = refs[3 : 3 + len(parts)]
        active, grad_hidden, kept, sent, grad_shift, down, up, sems = refs[3 + len(parts) :]
        step = pl.program_id(0)

        @pl.when(step == 0)
        def _():
            if len(rings) == 1:
                fields = [((0, strip), None, up), ((strip, None), None, down)]
                copies = landing(rings[0], held, fields, places, sems)
            else:
                first, second = held[: len(rings[0])], held[len(rings[0]) :]
                copies = landing(rings[0], first, [((0, None), None, up)], places, sems)
                left = sems.at[pl.ds(len(copies), signals - len(copies))]
                copies += landing(rings[1], second, [((0, None), None, down)], places, left)
            wait_all(copies)
            grad_shift[...] = jnp.zeros_like(grad_shift)

        hidden = dot(normed_ref[...], up[...]) + shift_ref[...]
        share_of = 0.5 + 0.5 * lax.erf(hidden * (0.5**0.5))
        active[...] = (hidden * share_of).astype(BF16)
        slope = share_of + hidden * (
            jnp.exp2(hidden * hidden * (-0.5 * LOG2E)) * ((2 * math.pi) ** -0.5)
        )
        grad = (slope * dot_nt(cot_ref[...], down[...])).astype(BF16)
        grad_hidden[...] = grad
        grad_shift[...] += column_sum(grad.astype(F32))
        grad_normed = dot_nt(grad, up[...]).astype(BF16)

        @pl.when(step % 2 == 0)
        def _():
            kept[step // 2] = grad_normed

        @pl.when(step % 2 == 1)
        def _():
            sent[step // 2] = grad_normed

    by_rows = lambda w: pl.BlockSpec((rows, w), lambda i, _: (i, 0))
    halves = (steps // 2, rows, width)
    return run(
        kernel,
        [
            shape((total, units)),
            shape((total, units)),
            shape(halves),
            shape(halves),
            shape((1, units), F32),
            shape((units, width)),
        ],
        grid=(steps,),
        scalars=scalars,
        specs=[by_rows(width), by_rows(width), whole(up_shift.shape)] + [HBM] * len(parts),
        arrays=[normed, cotangent, up_shift] + [part for _, _, part in parts],
        out_specs=[
            by_rows(units),
            by_rows(units),
            whole(halves),
            whole(halves),
            whole((1, units)),
            whole((units, width)),
        ],
        scratch=[pltpu.VMEM((width, units), BF16), pltpu.SemaphoreType.DMA((signals,))],
        flops=6 * total * width * units,
        vmem=32,
    )


def descend(scalars, active, down, rows):
    total, units = active.shape
    width = down.shape[1]

    def kernel(_, active_ref, down_ref, kept, sent):
        step = pl.program_id(0)
        part = dot(active_ref[...], down_ref[...]).astype(BF16)

        @pl.when(step % 2 == 0)
        def _():
            kept[step // 2] = part

        @pl.when(step % 2 == 1)
        def _():
            sent[step // 2] = part

    halves = (total // rows // 2, rows, width)
    return run(
        kernel,
        [shape(halves)] * 2,
        grid=(total // rows,),
        scalars=scalars,
        specs=[pl.BlockSpec((rows, units), lambda i, _: (i, 0)), whole(down.shape)],
        arrays=[active, down],
        out_specs=[whole(halves)] * 2,
        flops=2 * total * units * width,
    )


def outer(scalars, left, right, count):
    total, height = left.shape
    width = right.shape[1]
    rows = min(height, 256)
    piece = height // count

    def kernel(places, left_ref, right_ref, out):
        product = dot_tn(left_ref[...], right_ref[...]).astype(BF16)
        for part in range(rows // piece):
            number = pl.program_id(0) * (rows // piece) + part
            out[places[count + number]] = product[part * piece : (part + 1) * piece]

    return run(
        kernel,
        [shape((count, piece, width))],
        grid=(height // rows,),
        scalars=scalars,
        specs=[pl.BlockSpec((total, rows), lambda i, _: (0, i)), whole(right.shape)],
        arrays=[left, right],
        out_specs=[whole((count, piece, width))],
        flops=2 * total * height * width,
    )[0]


def middle_back(scalars, addends, middle, cotangent, vectors):
    rows, width = middle.shape
    block = min(rows, 128)

    def kernel(_, *refs):
        parts = refs[: len(addends)]
        middle_ref, cot_ref, vectors_ref, grad_middle, grad_branch, sums = refs[len(addends) :]
        grad = sum(part[0].astype(F32) for part in parts)
        cot = cot_ref[...].astype(F32)
        unit, inverse = standard(middle_ref[...])
        total = cot + norm_pull(grad, vectors_ref[3:4, :], unit, inverse)
        grad_middle[...] = total
        branch = total.astype(BF16)
        grad_branch[...] = branch

        @pl.when(pl.program_id(0) == 0)
        def _():
            sums[...] = jnp.zeros_like(sums)

        sums[0:1, :] += column_sum(branch.astype(F32))
        sums[1:2, :] += column_sum(grad * unit)
        sums[2:3, :] += column_sum(grad)
        sums[3:4, :] += column_sum(cot)

    by_rows = pl.BlockSpec((block, width), lambda i, _: (i, 0))
    return run(
        kernel,
        [shape((rows, width), F32), shape((rows, width)), shape((8, width), F32)],
        grid=(rows // block,),
        scalars=scalars,
        specs=[pl.BlockSpec((1, block, width), lambda i, _: (0, i, 0))] * len(addends)
        + [by_rows, by_rows, whole(vectors.shape)],
        arrays=[*addends, middle, cotangent, vectors],
        out_specs=[by_rows, by_rows, whole((8, width))],
    )


def attended_back(scalars, branches, outs, attended):
    count = len(branches)
    total, share = attended.shape
    rows, width = branches[0].shape
    own = scalars.shape[0] - 1

    def kernel(places, *refs):
        parts, held = refs[:count], refs[count : count + len(outs)]
        attended_ref, grads, extras, out_ref, sems = refs[count + len(outs) :]
        start = pl.multiple_of(places[own] * share, 16)
        wait_all(column_copies(places, held, out_ref, sems, pl.ds(start, share)))
        place = lax.broadcasted_iota(jnp.int32, (rows, HEAD_DIM), 1)
        for number, part in enumerate(parts):
            span = slice(number * rows, (number + 1) * rows)
            grad = dot_nt(part[...], out_ref[...]).astype(BF16)
            grads[span, :] = grad
            product = grad.astype(F32) * attended_ref[span, :].astype(F32)
            columns = []
            for head in range(share // HEAD_DIM):
                lanes = slice(head * HEAD_DIM, (head + 1) * HEAD_DIM)
                delta = jnp.sum(product[:, lanes], axis=1, keepdims=True)
                high, middle, low = split_three(delta)
                zero = jnp.zeros((rows, HEAD_DIM), BF16)
                columns.append(
                    jnp.where(
                        place == 3,
                        high,
                        jnp.where(place == 4, middle, jnp.where(place == 5, low, zero)),
                    )
                )
            extras[span, :] = jnp.concatenate(columns, axis=1)

    return run(
        kernel,
        [shape((total, share))] * 2,
        grid=(1,),
        scalars=scalars,
        specs=[whole((rows, width))] * count
        + [HBM] * len(outs)
        + [whole((total, share))],
        arrays=[*branches, *outs, attended],
        out_specs=[whole((total, share))] * 2,
        scratch=[pltpu.VMEM((share, width), BF16), pltpu.SemaphoreType.DMA((len(outs),))],
        flops=2 * total * width * share,
    )


def attend_back(scalars, query, extra, keys, key_mask, values, grads, grad_extra, pair, before=()):
    total, share = query.shape
    wide = head_pairs(share)[1]
    rows = min(total, 256)
    scale = HEAD_DIM**-0.5

    def kernel(_, q_ref, qx_ref, k_ref, km_ref, v_ref, g_ref, gx_ref, *refs):
        dq_ref, dk_ref, dv_ref, held = refs[len(before) :]
        step = pl.program_id(0)
        grad_keys, grad_values = [], []
        for head in range(wide // HEAD_DIM):
            lanes = slice(head * HEAD_DIM, (head + 1) * HEAD_DIM)
            query_part, key_part, grad_part = q_ref[:, lanes], k_ref[:, lanes], g_ref[:, lanes]
            q = jnp.concatenate([query_part, qx_ref[:, lanes]], axis=1)
            k = jnp.concatenate([key_part, km_ref[...]], axis=1)
            g = jnp.concatenate([grad_part, gx_ref[:, lanes]], axis=1)
            v = jnp.concatenate([v_ref[:, lanes], jnp.maximum(km_ref[...], -1.0)], axis=1)
            shares = jnp.exp2(dot_nt(k, q) * (LOG2E * scale))
            grad_scores = (shares * dot_nt(v, g)).astype(BF16)
            grad_values.append(dot(shares.astype(BF16), grad_part))
            grad_keys.append(dot(grad_scores, query_part) * scale)
            update = dot_tn(key_part, grad_scores) * scale

            @pl.when(step == 0)
            def _():
                held[lanes, :] = update

            @pl.when(step > 0)
            def _():
                held[lanes, :] += update

        dk_ref[...] = jnp.concatenate(grad_keys, axis=1).astype(BF16)
        dv_ref[...] = jnp.concatenate(grad_values, axis=1).astype(BF16)

        @pl.when(step == pl.num_programs(0) - 1)
        def _():
            dq_ref[...] = held[...].T.astype(BF16)

    by_rows = pl.BlockSpec((rows, wide), lambda i, _: (i, pair))
    fixed = pl.BlockSpec((total, wide), lambda i, _: (0, pair))
    return run(
        kernel,
        [shape((total, share))] * 3,
        grid=(total // rows,),
        scalars=scalars,
        specs=[
            fixed,
            fixed,
            by_rows,
            pl.BlockSpec((rows, HEAD_DIM), lambda i, _: (i, 0)),
            by_rows,
            fixed,
            fixed,
        ]
        + [HBM] * len(before),
        arrays=[query, extra, keys, key_mask, values, grads, grad_extra, *before],
        out_specs=[fixed, by_rows, by_rows],
        kept={8 + number: number for number in range(len(before))},
        scratch=[pltpu.VMEM((wide, total), F32)],
        flops=10 * 4 * total * total * share,
    )


def projection_grads(
    scalars, normed, mixed, gathered, branches, weight, vectors, middle_sums, up_sums, count
):
    total, width = normed.shape
    share = mixed[0].shape[1]
    rows = min(width, 256)
    piece = width // count
    units = up_sums.shape[1] // count
    block = branches[0].shape[0]
    own = scalars.shape[0] - 1
    per = share // piece
    column = pl.BlockSpec((block, share), lambda i, w: (0, w[own]))
    if share % 128:
        column = whole((block, share))
        branches = [
            lax.dynamic_slice_in_dim(part, scalars[own] * share, share, 1) for part in branches
        ]

    def to_row(values):
        if values.shape[1] % 128 == 0:
            values = sum(
                values[:, start : start + 128] for start in range(0, values.shape[1], 128)
            )
        return jnp.sum(values.T, axis=0, keepdims=True)

    def kernel(places, normed_ref, gathered_ref, weight_ref, vectors_ref, sums_ref, up_ref, *refs):
        mixed_refs, parts = refs[:3], refs[3 : 3 + len(branches)]
        out, totals, fields = refs[3 + len(branches) :]
        step = pl.program_id(0)

        @pl.when(step == 0)
        def _():
            for place, ref in enumerate(mixed_refs):
                totals[place : place + 1, :] = column_sum(ref[...].astype(F32))
            for number in range(count):
                span = slice(number * piece, (number + 1) * piece)
                fields[number, 2:6, :] = sums_ref[0:4, span]
                fields[number, 6:7, :units] = up_ref[:, number * units : (number + 1) * units]

        left = normed_ref[...]
        products, gain, shift = [], 0.0, 0.0
        for place, ref in enumerate(mixed_refs):
            product = dot_tn(left, ref[...])
            products.append(product.astype(BF16))
            part = weight_ref[:, place * share : (place + 1) * share].astype(F32)
            gain = gain + to_row(product * part)
            shift = shift + to_row(part * totals[place : place + 1, :])
        gain = (gain - vectors_ref[1:2, :] * shift) / vectors_ref[0:1, :]
        branch = 0.0
        for number, part in enumerate(parts):
            branch = branch + dot_tn(
                gathered_ref[number * block : (number + 1) * block, :], part[...]
            )
        branch = branch.astype(BF16)
        for part in range(rows // piece):
            span = slice(part * piece, (part + 1) * piece)
            number = step * (rows // piece) + part
            target = places[count + number]
            for place, product in enumerate(products):
                out[target, :piece, place * share : (place + 1) * share] = product[span]
            held = fields[number]
            entries = [gain[:, span], shift[:, span]] + [held[i : i + 1] for i in range(2, 7)]
            row = lax.broadcasted_iota(jnp.int32, (16, piece), 0)
            spots = [field_at(number, piece, 4 * share) for number in range(7)]
            for start in range(0, 4 * share, piece):
                value = jnp.zeros((16, piece), F32)
                for entry, (line, begin) in zip(entries, spots):
                    if begin == start:
                        value = jnp.where(row == line, entry, value)
                out[target, piece:, start : start + piece] = value.astype(BF16)
            natural = ((number // per) ^ places[own]) * per + number % per
            out[places[count + natural], :piece, 3 * share :] = branch[span]

    return run(
        kernel,
        [shape((count, piece + 16, 4 * share))],
        grid=(width // rows,),
        scalars=scalars,
        specs=[pl.BlockSpec((total, rows), lambda i, _: (0, i))] * 2
        + [pl.BlockSpec((rows, 3 * share), lambda i, _: (i, 0))]
        + [pl.BlockSpec((8, rows), lambda i, _: (0, i))]
        + [whole(middle_sums.shape), whole(up_sums.shape)]
        + [whole((total, share))] * 3
        + [column] * len(branches),
        arrays=[normed, gathered, weight, vectors, middle_sums, up_sums, *mixed, *branches],
        out_specs=[whole((count, piece + 16, 4 * share))],
        scratch=[pltpu.VMEM((8, share), F32), pltpu.VMEM((count, 8, piece), F32)],
        flops=2 * total * width * 4 * share,
    )[0]


def normed_back(scalars, mixed, weight, rows):
    total, share = mixed[0].shape
    width = weight.shape[0]

    def kernel(_, q_ref, k_ref, v_ref, weight_ref, kept, sent):
        step = pl.program_id(0)
        grad = 0.0
        for place, ref in enumerate((q_ref, k_ref, v_ref)):
            lanes = slice(place * share, (place + 1) * share)
            grad = grad + dot_nt(ref[...], weight_ref[:, lanes])

        @pl.when(step % 2 == 0)
        def _():
            kept[step // 2] = grad.astype(BF16)

        @pl.when(step % 2 == 1)
        def _():
            sent[step // 2] = grad.astype(BF16)

    by_rows = pl.BlockSpec((rows, share), lambda i, _: (i, 0))
    halves = (total // rows // 2, rows, width)
    return run(
        kernel,
        [shape(halves), shape(halves)],
        grid=(total // rows,),
        scalars=scalars,
        specs=[by_rows] * 3 + [whole(weight.shape)],
        arrays=[*mixed, weight],
        out_specs=[whole(halves), whole(halves)],
        flops=2 * total * width * 3 * share,
    )


def tokens_back(scalars, addends, tokens, grad_middle, vectors):
    rows, width = tokens.shape
    block = min(rows, 128)

    def kernel(_, *refs):
        parts = refs[: len(addends)]
        tokens_ref, middle_ref, vectors_ref, out = refs[len(addends) :]
        grad = sum(part[0].astype(F32) for part in parts)
        unit, inverse = standard(tokens_ref[...].astype(F32))
        pulled = norm_pull(grad, vectors_ref[0:1, :], unit, inverse)
        out[...] = (middle_ref[...] + pulled).astype(BF16)

    by_rows = pl.BlockSpec((block, width), lambda i, _: (i, 0))
    return run(
        kernel,
        [shape((rows, width))],
        grid=(rows // block,),
        scalars=scalars,
        specs=[pl.BlockSpec((1, block, width), lambda i, _: (0, i, 0))] * len(addends)
        + [by_rows, by_rows, whole(vectors.shape)],
        arrays=[*addends, tokens, grad_middle, vectors],
        out_specs=[by_rows],
    )[0]


def place_attention(scalars, parts, strip, unit_strip):
    columns = parts[0].shape[1]
    share = columns // 4
    along = len(parts)
    own = scalars.shape[0] - 1

    def kernel(places, *refs):
        held, grad_in, grad_out, small, tail = refs[:along], *refs[along : along + 2], *refs[-2:]
        total = 0.0
        for number, ref in enumerate(held):
            spot = places[own] ^ number
            for place in range(4):
                part = ref[:strip, place * share : (place + 1) * share].astype(F32)
                target = grad_out if place == 3 else grad_in
                start = pl.multiple_of((place % 3 * along + spot) * share, 128)
                target[:, pl.ds(start, share)] = part
            extra = ref[strip:, :].astype(F32)
            total = total + extra
            row, start = field_at(6, strip, columns)
            target = pl.multiple_of(spot * unit_strip, 128)
            tail[:, pl.ds(target, unit_strip)] = extra[row : row + 1, start : start + unit_strip]
        for field in range(6):
            row, start = field_at(field, strip, columns)
            small[field : field + 1, :] = total[row : row + 1, start : start + strip]

    outs = [(strip, 3 * share * along), (strip, share * along), (8, strip), (1, along * unit_strip)]
    return run(
        kernel,
        [shape(out, F32) for out in outs],
        grid=(1,),
        scalars=scalars,
        specs=[whole(part.shape) for part in parts],
        arrays=parts,
        out_specs=[whole(out) for out in outs],
    )


def place_feed(scalars, parts, strip, unit_strip, groups):
    width = parts[0].shape[1]
    along = len(parts)
    own = scalars.shape[0] - 1

    def kernel(places, *refs):
        held, (grad_up, grad_down) = refs[:along], refs[along:]
        for number, ref in enumerate(held):
            spot = places[own] ^ number
            for group in range(groups):
                start = pl.multiple_of((group * along + spot) * unit_strip, 128)
                lanes = slice(group * unit_strip, (group + 1) * unit_strip)
                grad_up[:, pl.ds(start, unit_strip)] = ref[:strip, lanes].astype(F32)
            start = pl.multiple_of(spot * unit_strip, 16)
            grad_down[pl.ds(start, unit_strip), :] = ref[strip:, :].astype(F32)

    outs = [(strip, groups * along * unit_strip), (along * unit_strip, width)]
    return run(
        kernel,
        [shape(out, F32) for out in outs],
        grid=(1,),
        scalars=scalars,
        specs=[whole(part.shape) for part in parts],
        arrays=parts,
        out_specs=[whole(out) for out in outs],
    )


def natural(parts, mine):
    return jnp.take(jnp.stack(parts), mine ^ jnp.arange(len(parts)), axis=0)


def local(
    groups,
    along,
    tokens,
    cotangent,
    scene_lengths,
    key_mask,
    project_in,
    project_out,
    up_weight,
    down_weight,
    in_gain,
    in_shift,
    out_shift,
    mid_gain,
    mid_shift,
    up_shift,
    down_shift,
):
    rows, width = tokens.shape[1:]
    total = rows * along
    hidden_units = up_weight.shape[1]
    strip = width // groups
    share = width // along
    unit_strip = hidden_units // groups // along
    units = unit_strip * groups
    mine, group = lax.axis_index("seq"), lax.axis_index("fsdp")
    order = ring_order(groups)
    rings = []
    for device in order_table(order):
        rings += [[*device, place] for place in range(along)]
    scalars = lax.dynamic_index_in_dim(
        jnp.array(rings, jnp.int32), group * along + mine, 0, keepdims=False
    )
    cut = max(unit_strip // 2 // 16, 1) * 16
    own_tokens = tokens[0]
    own_cot = cotangent[0]

    fields = [in_gain, in_shift, out_shift, mid_gain, mid_shift, down_shift]
    in_part = select(
        scalars,
        [project_in] * 3 + [project_out],
        [0, along, 2 * along, 0],
        share,
        [field.reshape(1, strip) for field in fields] + [up_shift.reshape(along, -1)],
    )
    token_parts = spread(after(own_tokens, in_part), along)
    unit, all_tokens = standardize(scalars, token_parts)
    in_parts = ring_gather(in_part, order, strip // 2, [[], [*token_parts[1 : along - 1]], [unit]])
    hops = [[part for d, _, part in in_parts if d in (i, groups - i)] for i in range(1, groups // 2 + 1)]

    cot_parts = spread(after(own_cot, token_parts[-2], *hops[0]), along)
    up_weight, down_weight, key_mask = lax.optimization_barrier(
        (up_weight, down_weight, key_mask, *hops[0])
    )[:3]
    up_part = select(scalars, [up_weight] * groups, [along * i for i in range(groups)], unit_strip)
    down_part = lax.dynamic_slice_in_dim(down_weight, mine * unit_strip, unit_strip, 0)
    query_mask, key_table = tables(scalars, scene_lengths, key_mask, along)
    up_part = after(up_part, key_table)
    all_cot = jnp.concatenate(cot_parts)
    joined = up_part.shape[1] == down_part.shape[1]
    if joined:
        feed_part = after(jnp.concatenate([up_part, down_part]), *hops[-1], all_cot)
        rings = [ring_gather(feed_part, order, strip)]
    else:
        rings = [ring_gather(up_part, order, strip // 2), ring_gather(down_part, order, cut)]
    first_hop = [part for d, _, part in rings[0] if d in (1, groups - 1)]

    normed, query, keys, values, in_weight, out_columns, vectors, up_shift_all = project(
        scalars, unit, in_parts, rows, strip, unit_strip
    )
    outs = spread(out_columns, along)
    pairs = head_pairs(share)[0]
    attended = ()
    for pair in range(pairs):
        attended = attend(
            scalars, query, keys, values, query_mask, key_table, pair, attended
        )
        query = after(query, outs[1], attended[0], *first_hop)
    attended, extra = attended
    all_attended = spread(attended, along)
    if share % 128:
        outs = [jnp.transpose(natural(outs, mine), (1, 0, 2)).reshape(width, width)]

    gathered, normed_mid, middle = attend_out(
        scalars, all_attended, all_tokens, vectors, outs, rows
    )
    active, grad_hidden, kept, sent, grad_up_shift, down_all = feed(
        scalars, normed_mid, all_cot, up_shift_all, rings, rows, strip
    )
    addends, sends = fold(kept, sent, along)
    active, normed_mid = lax.optimization_barrier((active, normed_mid, sends[-1]))[:2]
    up_pieces = outer(scalars, normed_mid, grad_hidden, groups)
    down_pieces = outer(scalars, active, all_cot, groups)
    if joined:
        sums = [RingSum(scalars, [up_pieces, down_pieces], order, strip)]
    else:
        sums = [
            RingSum(scalars, [up_pieces], order, strip // 2),
            RingSum(scalars, [down_pieces], order, cut),
        ]
    feed_sum = sums[0]
    grad_middle, grad_branch, middle_sums = middle_back(
        scalars, addends, middle, own_cot, vectors
    )
    branches = spread(grad_branch, along)
    active = after(active, *feed_sum.advance(grad_branch))
    result_addends, result_sends = fold(*descend(scalars, active, down_all, rows), along)
    ready = after(attended, *feed_sum.advance())
    grads, grad_extra = attended_back(scalars, branches, outs, ready)
    mixed = ()
    for pair in range(pairs):
        mixed = attend_back(
            scalars, query, extra, keys, key_table, values, grads, grad_extra, pair, mixed
        )
        if pair == 0:
            grads = after(grads, result_sends[-1], *feed_sum.advance(mixed[0]))
    pieces = projection_grads(
        scalars,
        after(normed, result_addends[-1]),
        mixed,
        gathered,
        branches,
        in_weight,
        vectors,
        middle_sums,
        grad_up_shift,
        groups,
    )
    feed_grads = [ring.finish() for ring in sums]
    pieces = after(pieces, feed_grads[0])
    attention_sum = RingSum(scalars, [pieces], order, strip // 2)
    feed_parts = spread(feed_grads[0], along)
    mixed = lax.optimization_barrier((*mixed, *attention_sum.advance(feed_parts[-2])))[:3]
    addends, sends = fold(*normed_back(scalars, mixed, in_weight, rows), along)
    attention_sum.advance(sends[-1])
    grad_tokens = tokens_back(scalars, addends, own_tokens, grad_middle, vectors)
    result = middle + vectors[5:6] + sum(part[0].astype(F32) for part in result_addends)
    attention_grads = after(attention_sum.finish(), addends[-1])

    parts = spread(attention_grads, along)
    if joined and not (share % 128 or unit_strip % 128):
        grad_in, grad_out, small, tail = place_attention(scalars, parts, strip, unit_strip)
        grad_up, grad_down = place_feed(scalars, feed_parts, strip, unit_strip, groups)
    else:
        both = natural(parts, mine).astype(F32)
        grad_in = jnp.transpose(
            both[:, :strip, : 3 * share].reshape(along, strip, 3, share), (1, 2, 0, 3)
        ).reshape(strip, 3 * width)
        grad_out = jnp.transpose(both[:, :strip, 3 * share :], (1, 0, 2)).reshape(strip, width)
        small = jnp.sum(both[:, strip:], axis=0).reshape(-1, strip)
        tail = both[:, strip:].reshape(along, -1, strip)[:, 6, :unit_strip]
        ups = natural(feed_parts, mine).astype(F32)
        ups = ups.reshape(along, strip, groups, unit_strip)
        grad_up = jnp.transpose(ups, (1, 2, 0, 3)).reshape(strip, hidden_units)
        grad_down = natural(spread(feed_grads[1], along), mine).astype(F32)
        grad_down = grad_down.reshape(along * unit_strip, width)
    small = [small[i] for i in range(6)]
    return (
        result.astype(BF16)[None],
        grad_tokens[None],
        grad_in,
        grad_out,
        grad_up,
        grad_down,
        small[0],
        small[1],
        small[2],
        small[3],
        small[4],
        tail.reshape(-1),
        small[5],
    )


def solution(mesh):
    by_token = P("fsdp", "seq", None)
    by_row, by_part = P("fsdp", None), P("fsdp")
    return jax.shard_map(
        functools.partial(local, mesh.shape["fsdp"], mesh.shape["seq"]),
        mesh=mesh,
        in_specs=(by_token,) * 2 + (by_row,) * 6 + (by_part,) * 7,
        out_specs=(by_token,) * 2 + (by_row,) * 4 + (by_part,) * 7,
        check_vma=False,
    )
```

```python
import functools
import math

import jax
import jax.numpy as jnp
from jax import lax
from jax.experimental import pallas as pl
from jax.experimental.pallas import tpu as pltpu
from jax.sharding import PartitionSpec as P


HEADS = 16
HEAD_DIM = 64
EPSILON = 1e-05
MASKED = -1e30
MIB = 1 << 20
F32 = jnp.float32
BF16 = jnp.bfloat16
LOG2E = math.log2(math.e)
HBM = pl.BlockSpec(memory_space=pl.ANY)
STEP = 1024


def ring_order(count):
    wide = max(count // 4, 1)
    tall = count // wide
    path = [(row, 0) for row in range(tall)]
    for row in reversed(range(tall)):
        columns = list(range(1, wide))
        if (tall - 1 - row) % 2:
            columns.reverse()
        path += [(row, column) for column in columns]
    return [row * wide + column for row, column in path]


def order_table(order):
    count = len(order)
    rows = []
    for device in range(count):
        spot = order.index(device)
        rows.append(
            [order[(spot + i) % count] for i in range(count)]
            + [(order.index(i) - spot) % count for i in range(count)]
            + [device]
        )
    return rows


def ring_steps(order):
    onward = list(zip(order, order[1:] + order[:1]))
    return onward, [(target, source) for source, target in onward]


def after(value, *others):
    return lax.optimization_barrier((value, *others))[0] if others else value


def ring_gather(block, order, cut, waits=()):
    onward, backward = ring_steps(order)
    count = len(order)
    half = count // 2
    parts = [(0, 0, block)]
    left = right = block
    waits = dict(enumerate(waits, 2))
    for step in range(1, half):
        if step in waits:
            left, right = lax.optimization_barrier((left, right, *waits[step]))[:2]
        left = lax.ppermute(left, "fsdp", onward)
        right = lax.ppermute(right, "fsdp", backward)
        parts += [(count - step, 0, left), (step, 0, right)]
    if half in waits:
        left, right = lax.optimization_barrier((left, right, *waits[half]))[:2]
    parts.append((half, 0, lax.ppermute(left[:cut], "fsdp", onward)))
    if cut < block.shape[0]:
        parts.append((half, cut, lax.ppermute(right[cut:], "fsdp", backward)))
    return parts


class RingSum:
    def __init__(self, scalars, pieces, order, cut):
        self.scalars, self.pieces = scalars, pieces
        self.onward, self.backward = ring_steps(order)
        self.count, self.step = len(order), 1
        far = [part[self.count // 2] for part in pieces]
        if len(far) == 2 and far[0].shape[0] == cut:
            self.left, self.right = far
        else:
            far = jnp.concatenate(far)
            self.left, self.right = far[:cut], far[cut:]
        self.send()

    def send(self):
        self.left = lax.ppermute(self.left, "fsdp", self.onward)
        if self.right is not None and self.right.shape[0]:
            self.right = lax.ppermute(self.right, "fsdp", self.backward)
        else:
            self.right = None

    def advance(self, *waits):
        if self.step == self.count // 2:
            return []
        left = after(self.left, *waits)
        near, far = self.count // 2 - self.step, self.count // 2 + self.step
        self.left, self.right = merge(self.scalars, self.pieces, near, far, left, self.right)
        sent = [self.left, self.right]
        self.send()
        self.step += 1
        return sent

    def finish(self):
        while self.step < self.count // 2:
            self.advance()
        return merge(self.scalars, self.pieces, 0, None, self.left, self.right)


def swap(value, axis, count, bit):
    return lax.ppermute(value, axis, [(i, i ^ bit) for i in range(count)])


def spread(block, count):
    parts = {0: block}
    bit = count // 2
    while bit:
        parts.update({place | bit: swap(part, "seq", count, bit) for place, part in parts.items()})
        bit //= 2
    return [parts[place] for place in range(count)]


def fold(kept, sent, count):
    addends, sends = [kept], [sent]
    bit = 1
    while True:
        addends.append(swap(sends[-1], "seq", count, bit))
        bit *= 2
        if bit == count:
            return addends, sends
        sends.append(sum(part[1::2].astype(F32) for part in addends).astype(BF16))
        addends = [part[0::2] for part in addends]


def run(kernel, outs, *, grid, scalars, specs, arrays, out_specs, scratch=(), flops=0, vmem=20, kept=None):
    return pl.pallas_call(
        kernel,
        out_shape=[jax.ShapeDtypeStruct(o.shape, o.dtype) for o in outs],
        grid_spec=pltpu.PrefetchScalarGridSpec(
            num_scalar_prefetch=1,
            grid=grid,
            in_specs=specs,
            out_specs=out_specs,
            scratch_shapes=list(scratch),
        ),
        input_output_aliases=kept or {},
        compiler_params=pltpu.CompilerParams(vmem_limit_bytes=vmem * MIB),
        cost_estimate=pl.CostEstimate(flops=0, bytes_accessed=1024, transcendentals=0),
    )(scalars, *arrays)


def shape(dims, dtype=BF16):
    return jax.ShapeDtypeStruct(dims, dtype)


def whole(dims):
    return pl.BlockSpec(dims, lambda *_: (0,) * len(dims))


def dot(left, right):
    return jnp.dot(left, right, preferred_element_type=F32)


def dot_nt(left, right):
    return lax.dot_general(left, right, (((1,), (1,)), ((), ())), preferred_element_type=F32)


def dot_tn(left, right):
    return lax.dot_general(left, right, (((0,), (0,)), ((), ())), preferred_element_type=F32)


def blocks_of(total, rows):
    return min(total, 1024) // rows


def standard(values):
    center = values - jnp.mean(values, axis=-1, keepdims=True)
    spread_of = jnp.mean(center * center, axis=-1, keepdims=True)
    inverse = lax.rsqrt(spread_of + EPSILON)
    return center * inverse, inverse


def norm_pull(grad, gain, unit, inverse):
    slope = grad * gain
    first = jnp.mean(slope, axis=-1, keepdims=True)
    second = jnp.mean(slope * unit, axis=-1, keepdims=True)
    return inverse * (slope - first - unit * second)


def column_sum(values):
    return jnp.sum(values, axis=0, keepdims=True)


def landing(parts, refs, fields, places, sems):
    height = sum(part.shape[0] for distance, _, part in parts if distance == 0)
    copies = []
    for (distance, start, part), ref in zip(parts, refs):
        for (low, high), columns, target in fields:
            high = high or height
            begin, end = max(low, start), min(high, start + part.shape[0])
            if begin >= end:
                continue
            offset = places[distance] * (high - low) + (begin - low)
            source = ref.at[pl.ds(begin - start, end - begin)]
            if columns is not None:
                source = ref.at[pl.ds(begin - start, end - begin), pl.ds(*columns)]
            target = target.at[pl.ds(pl.multiple_of(offset, 16), end - begin)]
            copies.append(pltpu.make_async_copy(source, target, sems.at[len(copies)]))
    return copies


def landings(parts, fields):
    return len(parts) * fields


def wait_all(copies):
    for copy in copies:
        copy.start()
    for copy in copies:
        copy.wait()


def merge(scalars, pieces, near, far, left, right):
    heights = [part.shape[1] for part in pieces]
    height, width = sum(heights), pieces[0].shape[2]
    arrays, specs = [], []
    for distance in (near,) if far is None else (near, far):
        for part, rows in zip(pieces, heights):
            arrays.append(part)
            specs.append(pl.BlockSpec((1, rows, width), lambda i, _, d=distance: (d, 0, 0)))
    sums = [part for part in (left, right) if part is not None]

    def kernel(_, *refs):
        held = refs[: len(arrays)]
        sums_refs = list(refs[len(arrays) : len(arrays) + len(sums)])
        outs = refs[len(arrays) + len(sums) :]
        first = left.shape[0]
        for side, out in enumerate(outs):
            start = 0
            for ref, rows in zip(held[side * len(pieces) :], heights):
                own = ref[0].astype(F32)
                span = slice(start, start + rows)
                if far is None:
                    for part in sums_refs:
                        own = own + part[span, :].astype(F32)
                    out[span, :] = own.astype(BF16)
                elif side < len(sums) and sums[side].shape[0] == height:
                    out[span, :] = (own + sums_refs[side][span, :].astype(F32)).astype(BF16)
                else:
                    out[span, :] = own.astype(BF16)
                start += rows
            if far is not None and side < len(sums) and sums[side].shape[0] < height:
                base = 0 if side == 0 else first
                rows = sums[side].shape[0]
                span = slice(base, base + rows)
                total = out[span, :].astype(F32) + sums_refs[side][...].astype(F32)
                out[span, :] = total.astype(BF16)

    whole_out = whole((height, width))
    count = 1 if far is None else 2
    outs = run(
        kernel,
        [shape((height, width))] * count,
        grid=(1,),
        scalars=scalars,
        specs=specs + [whole(part.shape) for part in sums],
        arrays=arrays + sums,
        out_specs=[whole_out] * count,
    )
    return outs[0] if far is None else outs


def select(scalars, arrays, starts, columns, fields=()):
    rows = arrays[0].shape[0]
    own = scalars.shape[0] - 1
    width = len(starts) * columns
    height = rows + (16 if fields else 0)
    if columns % 128:
        pick = lambda array, start, size: lax.dynamic_slice_in_dim(
            array, (start + scalars[own]) * size, size, 1
        )
        parts = [pick(array, start, columns) for array, start in zip(arrays, starts)]
        parts = jnp.concatenate(parts, axis=1)
        if not fields:
            return parts
        line = lax.dynamic_slice_in_dim(fields[-1], scalars[own], 1, 0)
        below = jnp.concatenate([*fields[:-1], line], axis=1)
        below = jnp.pad(below, ((0, 0), (0, 16 * width - below.shape[1])))
        return jnp.concatenate([parts, below.reshape(16, width)])

    def kernel(_, *refs):
        held = refs[: len(arrays) + len(fields)]
        out, sems, *lines = refs[len(held) :]
        mine = lax.axis_index("seq")
        copies = []
        for number, (ref, start) in enumerate(zip(held, starts)):
            begin = pl.multiple_of((start + mine) * columns, 128)
            target = out.at[pl.ds(0, rows), pl.ds(number * columns, columns)]
            copies.append((ref.at[:, pl.ds(begin, columns)], target))
        for number, ref in enumerate(held[len(arrays) :]):
            copies.append((ref, lines[number]))
        wait_all(
            [
                pltpu.make_async_copy(source, target, sems.at[number])
                for number, (source, target) in enumerate(copies)
            ]
        )
        if not fields:
            return
        size = lines[0].shape[1]
        per = width // size
        row = lax.broadcasted_iota(jnp.int32, (16, size), 0)
        values = [line[...].astype(F32) for line in lines]
        chosen = lax.broadcasted_iota(jnp.int32, values[-1].shape, 0) == mine
        values[-1] = column_sum(jnp.where(chosen, values[-1], 0.0))
        for start in range(per):
            value = jnp.zeros(row.shape, F32)
            for number in range(start, len(lines), per):
                value = jnp.where(row == number // per, values[number], value)
            out[rows:, start * size : (start + 1) * size] = value.astype(BF16)

    return run(
        kernel,
        [shape((height, width))],
        grid=(1,),
        scalars=jnp.zeros((1,), jnp.int32),
        specs=[pl.BlockSpec(memory_space=pltpu.HBM)] * (len(arrays) + len(fields)),
        arrays=[*arrays, *fields],
        out_specs=[whole((height, width))],
        scratch=[pltpu.SemaphoreType.DMA((len(arrays) + len(fields),))]
        + [pltpu.VMEM(field.shape, BF16) for field in fields],
        vmem=60 if fields else 20,
    )[0]


def tables(scalars, lengths, key_mask, along):
    total = key_mask.shape[1]
    rows = total // along
    scenes = lengths.shape[1]
    own = scalars.shape[0] - 1

    def kernel(places, lengths_ref, mask_ref, query_table, key_table):
        row = lax.broadcasted_iota(jnp.int32, (HEAD_DIM, rows), 0)
        for number in range(along):
            start = pl.multiple_of((places[own] ^ number) * rows, 128)
            spot = start + lax.broadcasted_iota(jnp.int32, (1, rows), 1)
            keep = mask_ref[:, pl.ds(start, rows)] == 1
            keep = jnp.where(keep, 1.0, 0.0)
            scene = jnp.zeros((1, rows), jnp.int32)
            edge = 0
            for part in range(scenes):
                keep = jnp.where(spot == edge, 1.0, keep)
                edge = edge + lengths_ref[0, part]
                scene = scene + jnp.where(spot >= edge, 1, 0)
            same = jnp.where(row == scene, 1.0, 0.0)
            keys = jnp.where(same * keep > 0.5, 0.0, MASKED)
            keys = jnp.where(row < scenes, keys, jnp.where(row < scenes + 3, -1.0, 0.0))
            span = slice(number * rows, (number + 1) * rows)
            query_table[span, :] = same.T.astype(BF16)
            key_table[span, :] = keys.T.astype(BF16)

    return run(
        kernel,
        [shape((total, HEAD_DIM))] * 2,
        grid=(1,),
        scalars=scalars,
        specs=[pl.BlockSpec(memory_space=pltpu.SMEM), whole(key_mask.shape)],
        arrays=[lengths, key_mask],
        out_specs=[whole((total, HEAD_DIM))] * 2,
    )


def standardize(scalars, tokens):
    rows, width = tokens[0].shape
    total = rows * len(tokens)

    def kernel(_, *refs):
        parts, (unit, joined) = refs[: len(tokens)], refs[len(tokens) :]
        for number, part in enumerate(parts):
            span = slice(number * rows, (number + 1) * rows)
            joined[span, :] = part[...]
            unit[span, :], _ = standard(part[...].astype(F32))

    return run(
        kernel,
        [shape((total, width), F32), shape((total, width))],
        grid=(1,),
        scalars=scalars,
        specs=[whole((rows, width))] * len(tokens),
        arrays=tokens,
        out_specs=[whole((total, width))] * 2,
    )


def field_at(number, strip, columns):
    per = columns // strip
    return number // per, number % per * strip


def project(scalars, unit, parts, rows, strip, unit_strip):
    total, width = unit.shape
    columns = parts[0][2].shape[1]
    share = columns // 4
    groups = width // strip
    count = landings(parts, 3)
    blocks = blocks_of(total, rows)

    def kernel(places, unit_ref, *refs):
        held = refs[: len(parts)]
        normed, query, keys, values, weight, out_weight, vectors, tail, extra, sems, *joint = refs[
            len(parts) :
        ]

        @pl.when(pl.program_id(0) == 0)
        def _():
            fields = [((strip, strip + 16), None, extra)]
            if joint:
                fields.append(((0, strip), None, joint[0]))
            else:
                fields.append(((0, strip), (0, 3 * share), weight))
                fields.append(((0, strip), (3 * share, share), out_weight))
            wait_all(landing(parts, held, fields, places, sems))
            if joint:
                weight[...] = joint[0][:, : 3 * share]
                out_weight[...] = joint[0][:, 3 * share :]
            for number in range(groups):
                block = extra[number * 16 : (number + 1) * 16, :].astype(F32)
                for field in range(7):
                    row, start = field_at(field, strip, columns)
                    part = block[row : row + 1, start : start + strip]
                    vectors[field : field + 1, number * strip : (number + 1) * strip] = part
                tail[:, number * unit_strip : (number + 1) * unit_strip] = part[:, :unit_strip]

        for block in range(blocks):
            span = slice(block * rows, (block + 1) * rows)
            part = (unit_ref[span, :] * vectors[0:1, :] + vectors[1:2, :]).astype(BF16)
            normed[span, :] = part
            mixed = dot(part, weight[...]).astype(BF16)
            query[span, :] = mixed[:, :share]
            keys[span, :] = mixed[:, share : 2 * share]
            values[span, :] = mixed[:, 2 * share :]

    by_rows = lambda w: pl.BlockSpec((rows * blocks, w), lambda i, _: (i, 0))
    return run(
        kernel,
        [shape((total, width))]
        + [shape((total, share))] * 3
        + [shape((width, 3 * share)), shape((width, share))]
        + [shape((8, width), F32), shape((1, groups * unit_strip), F32)],
        grid=(total // rows // blocks,),
        scalars=scalars,
        specs=[by_rows(width)] + [HBM] * len(parts),
        arrays=[unit] + [part for _, _, part in parts],
        out_specs=[by_rows(width)]
        + [by_rows(share)] * 3
        + [whole((width, 3 * share)), whole((width, share))]
        + [whole((8, width)), whole((1, groups * unit_strip))],
        scratch=[pltpu.VMEM((groups * 16, columns), BF16), pltpu.SemaphoreType.DMA((count,))]
        + [pltpu.VMEM((width, columns), BF16)] * (share % 128 > 0),
        flops=2 * total * width * 3 * share,
    )


def split_three(values):
    high = values.astype(BF16)
    rest = values - high.astype(F32)
    middle = rest.astype(BF16)
    return high, middle, (rest - middle.astype(F32)).astype(BF16)


def head_pairs(share):
    wide = min(share, 2 * HEAD_DIM)
    return share // wide, wide


def attend(scalars, query, keys, values, query_mask, key_mask, pair, before=()):
    total, share = query.shape
    wide = head_pairs(share)[1]
    rows = min(total, 512 * STEP // total)
    scale = HEAD_DIM**-0.5

    def kernel(_, q_ref, k_ref, v_ref, qm_ref, km_ref, *refs):
        attended, extra = refs[len(before) :]
        ones = jnp.ones((total, HEAD_DIM), BF16)
        place = lax.broadcasted_iota(jnp.int32, (rows, HEAD_DIM), 1)
        outs, extras = [], []
        for head in range(wide // HEAD_DIM):
            lanes = slice(head * HEAD_DIM, (head + 1) * HEAD_DIM)
            q = jnp.concatenate([q_ref[:, lanes], qm_ref[...]], axis=1)
            k = jnp.concatenate([k_ref[:, lanes], km_ref[...]], axis=1)
            v = jnp.concatenate([v_ref[:, lanes], ones], axis=1)
            scores = dot_nt(q, k)
            top = jnp.max(scores, axis=1, keepdims=True)
            weights = jnp.exp2((scores - top) * (LOG2E * scale)).astype(BF16)
            summed = dot(weights, v)
            amount = summed[:, HEAD_DIM : HEAD_DIM + 1]
            outs.append(summed[:, :HEAD_DIM] / amount)
            high, middle, low = split_three(top + jnp.log(amount) / scale)
            extras.append(
                jnp.where(
                    place == 3,
                    high,
                    jnp.where(place == 4, middle, jnp.where(place == 5, low, qm_ref[...])),
                )
            )
        attended[...] = jnp.concatenate(outs, axis=1).astype(BF16)
        extra[...] = jnp.concatenate(extras, axis=1)

    by_rows = pl.BlockSpec((rows, wide), lambda i, _: (i, pair))
    fixed = pl.BlockSpec((total, wide), lambda i, _: (0, pair))
    return run(
        kernel,
        [shape((total, share))] * 2,
        grid=(total // rows,),
        scalars=scalars,
        specs=[
            by_rows,
            fixed,
            fixed,
            pl.BlockSpec((rows, HEAD_DIM), lambda i, _: (i, 0)),
            whole((total, HEAD_DIM)),
        ]
        + [HBM] * len(before),
        arrays=[query, keys, values, query_mask, key_mask, *before],
        out_specs=[by_rows, by_rows],
        kept={6 + number: number for number in range(len(before))},
        flops=4 * 4 * total * total * share,
    )


def column_copies(places, refs, target, sems, rows):
    own = places.shape[0] - 1
    if len(refs) == 1:
        return [pltpu.make_async_copy(refs[0].at[rows], target, sems.at[0])]
    columns = refs[0].shape[1]
    return [
        pltpu.make_async_copy(
            ref.at[rows],
            target.at[:, pl.ds(pl.multiple_of((places[own] ^ place) * columns, 128), columns)],
            sems.at[place],
        )
        for place, ref in enumerate(refs)
    ]


def attend_out(scalars, attended, tokens, vectors, outs, rows):
    places_along = len(attended)
    total, width = tokens.shape
    share = attended[0].shape[1]
    own = scalars.shape[0] - 1

    def kernel(places, *refs):
        attended_refs, refs = refs[:places_along], refs[places_along:]
        tokens_ref, vectors_ref = refs[:2]
        held, (gathered, normed, middle_own, out_ref, sems) = (
            refs[2 : 2 + len(outs)],
            refs[2 + len(outs) :],
        )
        step = pl.program_id(0)

        @pl.when(step == 0)
        def _():
            wait_all(column_copies(places, held, out_ref, sems, pl.ds(0, width)))

        for place, ref in enumerate(attended_refs):
            gathered[:, place * share : (place + 1) * share] = ref[...]
        branch = vectors_ref[2:3, :]
        for place in range(places_along):
            start = pl.multiple_of((places[own] ^ place) * share, share)
            branch = branch + dot(attended_refs[place][...], out_ref[pl.ds(start, share), :])
        middle = tokens_ref[...].astype(F32) + branch

        @pl.when(step == 0)
        def _():
            middle_own[...] = middle

        unit, _ = standard(middle)
        normed[...] = (unit * vectors_ref[3:4, :] + vectors_ref[4:5, :]).astype(BF16)

    by_rows = pl.BlockSpec((rows, width), lambda i, _: (i, 0))
    part_of = lambda x: pl.BlockSpec((rows, share), lambda i, _: (i ^ x, 0))
    return run(
        kernel,
        [shape((total, width)), shape((total, width)), shape((rows, width), F32)],
        grid=(places_along,),
        scalars=scalars,
        specs=[part_of(x) for x in range(places_along)]
        + [by_rows, whole(vectors.shape)]
        + [HBM] * len(outs),
        arrays=[*attended, tokens, vectors, *outs],
        out_specs=[by_rows, by_rows, whole((rows, width))],
        scratch=[pltpu.VMEM((width, width), BF16), pltpu.SemaphoreType.DMA((len(outs),))],
        flops=2 * total * width * width,
    )


def feed(scalars, normed, cotangent, up_shift, rings, rows, strip):
    total, width = normed.shape
    units = up_shift.shape[1]
    steps, blocks = total // rows, blocks_of(total, rows)
    parts = [part for ring in rings for part in ring]
    signals = 2 * len(parts)

    def kernel(places, *refs):
        normed_ref, cot_ref, shift_ref = refs[:3]
        held = refs[3 : 3 + len(parts)]
        active, grad_hidden, kept, sent, grad_shift, down, up, sems = refs[3 + len(parts) :]
        step = pl.program_id(0)

        @pl.when(step == 0)
        def _():
            if len(rings) == 1:
                fields = [((0, strip), None, up), ((strip, None), None, down)]
                copies = landing(rings[0], held, fields, places, sems)
            else:
                first, second = held[: len(rings[0])], held[len(rings[0]) :]
                copies = landing(rings[0], first, [((0, None), None, up)], places, sems)
                left = sems.at[pl.ds(len(copies), signals - len(copies))]
                copies += landing(rings[1], second, [((0, None), None, down)], places, left)
            wait_all(copies)
            grad_shift[...] = jnp.zeros_like(grad_shift)

        for block in range(blocks):
            span = slice(block * rows, (block + 1) * rows)
            hidden = dot(normed_ref[span, :], up[...]) + shift_ref[...]
            share_of = 0.5 + 0.5 * lax.erf(hidden * (0.5**0.5))
            active[span, :] = (hidden * share_of).astype(BF16)
            slope = share_of + hidden * (
                jnp.exp2(hidden * hidden * (-0.5 * LOG2E)) * ((2 * math.pi) ** -0.5)
            )
            grad = (slope * dot_nt(cot_ref[span, :], down[...])).astype(BF16)
            grad_hidden[span, :] = grad
            grad_shift[...] += column_sum(grad.astype(F32))
            grad_normed = dot_nt(grad, up[...]).astype(BF16)
            (sent if block % 2 else kept)[step * (blocks // 2) + block // 2] = grad_normed

    by_rows = lambda w: pl.BlockSpec((rows * blocks, w), lambda i, _: (i, 0))
    halves = (steps // 2, rows, width)
    return run(
        kernel,
        [
            shape((total, units)),
            shape((total, units)),
            shape(halves),
            shape(halves),
            shape((1, units), F32),
            shape((units, width)),
        ],
        grid=(steps // blocks,),
        scalars=scalars,
        specs=[by_rows(width), by_rows(width), whole(up_shift.shape)] + [HBM] * len(parts),
        arrays=[normed, cotangent, up_shift] + [part for _, _, part in parts],
        out_specs=[
            by_rows(units),
            by_rows(units),
            whole(halves),
            whole(halves),
            whole((1, units)),
            whole((units, width)),
        ],
        scratch=[pltpu.VMEM((width, units), BF16), pltpu.SemaphoreType.DMA((signals,))],
        flops=6 * total * width * units,
        vmem=32,
    )


def descend(scalars, active, down, rows):
    total, units = active.shape
    width = down.shape[1]

    blocks = blocks_of(total, rows)

    def kernel(_, active_ref, down_ref, kept, sent):
        for block in range(blocks):
            span = slice(block * rows, (block + 1) * rows)
            part = dot(active_ref[span, :], down_ref[...]).astype(BF16)
            number = pl.program_id(0) * (blocks // 2) + block // 2
            (sent if block % 2 else kept)[number] = part

    halves = (total // rows // 2, rows, width)
    return run(
        kernel,
        [shape(halves)] * 2,
        grid=(total // rows // blocks,),
        scalars=scalars,
        specs=[pl.BlockSpec((rows * blocks, units), lambda i, _: (i, 0)), whole(down.shape)],
        arrays=[active, down],
        out_specs=[whole(halves)] * 2,
        flops=2 * total * units * width,
    )


def outer(scalars, left, right, count):
    total, height = left.shape
    width = right.shape[1]
    rows = min(height, 1024)
    part_rows = min(rows, 256)
    piece = height // count

    def kernel(places, left_ref, right_ref, out):
        for start in range(0, rows, part_rows):
            product = dot_tn(left_ref[:, start : start + part_rows], right_ref[...]).astype(BF16)
            for part in range(part_rows // piece):
                number = pl.program_id(0) * (rows // piece) + start // piece + part
                out[places[count + number]] = product[part * piece : (part + 1) * piece]

    return run(
        kernel,
        [shape((count, piece, width))],
        grid=(height // rows,),
        scalars=scalars,
        specs=[pl.BlockSpec((total, rows), lambda i, _: (0, i)), whole(right.shape)],
        arrays=[left, right],
        out_specs=[whole((count, piece, width))],
        flops=2 * total * height * width,
    )[0]


def middle_back(scalars, addends, middle, cotangent, vectors):
    rows, width = middle.shape
    block = min(rows, 128)

    def kernel(_, *refs):
        parts = refs[: len(addends)]
        middle_ref, cot_ref, vectors_ref, grad_middle, grad_branch, sums = refs[len(addends) :]
        grad = sum(part[0].astype(F32) for part in parts)
        cot = cot_ref[...].astype(F32)
        unit, inverse = standard(middle_ref[...])
        total = cot + norm_pull(grad, vectors_ref[3:4, :], unit, inverse)
        grad_middle[...] = total
        branch = total.astype(BF16)
        grad_branch[...] = branch

        @pl.when(pl.program_id(0) == 0)
        def _():
            sums[...] = jnp.zeros_like(sums)

        sums[0:1, :] += column_sum(branch.astype(F32))
        sums[1:2, :] += column_sum(grad * unit)
        sums[2:3, :] += column_sum(grad)
        sums[3:4, :] += column_sum(cot)

    by_rows = pl.BlockSpec((block, width), lambda i, _: (i, 0))
    return run(
        kernel,
        [shape((rows, width), F32), shape((rows, width)), shape((8, width), F32)],
        grid=(rows // block,),
        scalars=scalars,
        specs=[pl.BlockSpec((1, block, width), lambda i, _: (0, i, 0))] * len(addends)
        + [by_rows, by_rows, whole(vectors.shape)],
        arrays=[*addends, middle, cotangent, vectors],
        out_specs=[by_rows, by_rows, whole((8, width))],
    )


def attended_back(scalars, branches, outs, attended):
    count = len(branches)
    total, share = attended.shape
    rows, width = branches[0].shape
    own = scalars.shape[0] - 1

    def kernel(places, *refs):
        parts, held = refs[:count], refs[count : count + len(outs)]
        attended_ref, grads, extras, out_ref, sems = refs[count + len(outs) :]
        start = pl.multiple_of(places[own] * share, 16)
        wait_all(column_copies(places, held, out_ref, sems, pl.ds(start, share)))
        line = lax.broadcasted_iota(jnp.int32, (share, share), 0) // HEAD_DIM
        lane = lax.broadcasted_iota(jnp.int32, (share, share), 1) // HEAD_DIM
        over_head = jnp.where(line == lane, 1.0, 0.0).astype(BF16)
        place = lax.broadcasted_iota(jnp.int32, (rows, share), 1) % HEAD_DIM
        for number, part in enumerate(parts):
            span = slice(number * rows, (number + 1) * rows)
            grad = dot_nt(part[...], out_ref[...]).astype(BF16)
            grads[span, :] = grad
            product = grad.astype(F32) * attended_ref[span, :].astype(F32)
            delta = sum(dot(piece, over_head) for piece in split_three(product))
            high, middle, low = (piece.astype(F32) for piece in split_three(delta))
            extra = jnp.where(place == 4, middle, jnp.where(place == 5, low, 0.0))
            extras[span, :] = jnp.where(place == 3, high, extra).astype(BF16)

    return run(
        kernel,
        [shape((total, share))] * 2,
        grid=(1,),
        scalars=scalars,
        specs=[whole((rows, width))] * count
        + [HBM] * len(outs)
        + [whole((total, share))],
        arrays=[*branches, *outs, attended],
        out_specs=[whole((total, share))] * 2,
        scratch=[pltpu.VMEM((share, width), BF16), pltpu.SemaphoreType.DMA((len(outs),))],
        flops=2 * total * width * share,
    )


def attend_back(scalars, query, extra, keys, key_mask, values, grads, grad_extra, pair, before=()):
    total, share = query.shape
    wide = head_pairs(share)[1]
    rows = min(total, 512 * STEP // total)
    scale = HEAD_DIM**-0.5

    def kernel(_, q_ref, qx_ref, k_ref, km_ref, v_ref, g_ref, gx_ref, *refs):
        dq_ref, dk_ref, dv_ref, held = refs[len(before) :]
        step = pl.program_id(0)
        grad_keys, grad_values = [], []
        for head in range(wide // HEAD_DIM):
            lanes = slice(head * HEAD_DIM, (head + 1) * HEAD_DIM)
            query_part, key_part, grad_part = q_ref[:, lanes], k_ref[:, lanes], g_ref[:, lanes]
            q = jnp.concatenate([query_part, qx_ref[:, lanes]], axis=1)
            k = jnp.concatenate([key_part, km_ref[...]], axis=1)
            g = jnp.concatenate([grad_part, gx_ref[:, lanes]], axis=1)
            v = jnp.concatenate([v_ref[:, lanes], jnp.maximum(km_ref[...], -1.0)], axis=1)
            shares = jnp.exp2(dot_nt(k, q) * (LOG2E * scale))
            grad_scores = (shares * dot_nt(v, g)).astype(BF16)
            grad_values.append(dot(shares.astype(BF16), grad_part))
            grad_keys.append(dot(grad_scores, query_part) * scale)
            update = dot_tn(key_part, grad_scores) * scale

            @pl.when(step == 0)
            def _():
                held[lanes, :] = update

            @pl.when(step > 0)
            def _():
                held[lanes, :] += update

        dk_ref[...] = jnp.concatenate(grad_keys, axis=1).astype(BF16)
        dv_ref[...] = jnp.concatenate(grad_values, axis=1).astype(BF16)

        @pl.when(step == pl.num_programs(0) - 1)
        def _():
            dq_ref[...] = held[...].T.astype(BF16)

    by_rows = pl.BlockSpec((rows, wide), lambda i, _: (i, pair))
    fixed = pl.BlockSpec((total, wide), lambda i, _: (0, pair))
    return run(
        kernel,
        [shape((total, share))] * 3,
        grid=(total // rows,),
        scalars=scalars,
        specs=[
            fixed,
            fixed,
            by_rows,
            pl.BlockSpec((rows, HEAD_DIM), lambda i, _: (i, 0)),
            by_rows,
            fixed,
            fixed,
        ]
        + [HBM] * len(before),
        arrays=[query, extra, keys, key_mask, values, grads, grad_extra, *before],
        out_specs=[fixed, by_rows, by_rows],
        kept={8 + number: number for number in range(len(before))},
        scratch=[pltpu.VMEM((wide, total), F32)],
        flops=10 * 4 * total * total * share,
    )


def projection_grads(
    scalars, normed, mixed, gathered, branches, weight, vectors, middle_sums, up_sums, count
):
    total, width = normed.shape
    share = mixed[0].shape[1]
    rows = min(width, 1024 * STEP // total)
    piece = width // count
    units = up_sums.shape[1] // count
    block = branches[0].shape[0]
    own = scalars.shape[0] - 1
    per = share // piece
    column = pl.BlockSpec((block, share), lambda i, w: (0, w[own]))
    if share % 128:
        column = whole((block, share))
        branches = [
            lax.dynamic_slice_in_dim(part, scalars[own] * share, share, 1) for part in branches
        ]

    def to_row(values):
        if values.shape[1] % 128 == 0:
            values = sum(
                values[:, start : start + 128] for start in range(0, values.shape[1], 128)
            )
        return jnp.sum(values.T, axis=0, keepdims=True)

    def kernel(places, normed_ref, gathered_ref, weight_ref, vectors_ref, sums_ref, up_ref, *refs):
        mixed_refs, parts = refs[:3], refs[3 : 3 + len(branches)]
        out, totals, fields = refs[3 + len(branches) :]
        step = pl.program_id(0)

        @pl.when(step == 0)
        def _():
            for place, ref in enumerate(mixed_refs):
                totals[place : place + 1, :] = column_sum(ref[...].astype(F32))
            for number in range(count):
                span = slice(number * piece, (number + 1) * piece)
                fields[number, 2:6, :] = sums_ref[0:4, span]
                fields[number, 6:7, :units] = up_ref[:, number * units : (number + 1) * units]

        left = normed_ref[...]
        products, gain, shift = [], 0.0, 0.0
        for place, ref in enumerate(mixed_refs):
            product = dot_tn(left, ref[...])
            products.append(product.astype(BF16))
            part = weight_ref[:, place * share : (place + 1) * share].astype(F32)
            gain = gain + to_row(product * part)
            shift = shift + to_row(part * totals[place : place + 1, :])
        gain = (gain - vectors_ref[1:2, :] * shift) / vectors_ref[0:1, :]
        branch = 0.0
        for number, part in enumerate(parts):
            branch = branch + dot_tn(
                gathered_ref[number * block : (number + 1) * block, :], part[...]
            )
        branch = branch.astype(BF16)
        for part in range(rows // piece):
            span = slice(part * piece, (part + 1) * piece)
            number = step * (rows // piece) + part
            target = places[count + number]
            for place, product in enumerate(products):
                out[target, :piece, place * share : (place + 1) * share] = product[span]
            held = fields[number]
            entries = [gain[:, span], shift[:, span]] + [held[i : i + 1] for i in range(2, 7)]
            row = lax.broadcasted_iota(jnp.int32, (16, piece), 0)
            spots = [field_at(number, piece, 4 * share) for number in range(7)]
            for start in range(0, 4 * share, piece):
                value = jnp.zeros((16, piece), F32)
                for entry, (line, begin) in zip(entries, spots):
                    if begin == start:
                        value = jnp.where(row == line, entry, value)
                out[target, piece:, start : start + piece] = value.astype(BF16)
            natural = ((number // per) ^ places[own]) * per + number % per
            out[places[count + natural], :piece, 3 * share :] = branch[span]

    return run(
        kernel,
        [shape((count, piece + 16, 4 * share))],
        grid=(width // rows,),
        scalars=scalars,
        specs=[pl.BlockSpec((total, rows), lambda i, _: (0, i))] * 2
        + [pl.BlockSpec((rows, 3 * share), lambda i, _: (i, 0))]
        + [pl.BlockSpec((8, rows), lambda i, _: (0, i))]
        + [whole(middle_sums.shape), whole(up_sums.shape)]
        + [whole((total, share))] * 3
        + [column] * len(branches),
        arrays=[normed, gathered, weight, vectors, middle_sums, up_sums, *mixed, *branches],
        out_specs=[whole((count, piece + 16, 4 * share))],
        scratch=[pltpu.VMEM((8, share), F32), pltpu.VMEM((count, 8, piece), F32)],
        flops=2 * total * width * 4 * share,
    )[0]


def normed_back(scalars, mixed, weight, rows):
    total, share = mixed[0].shape
    width = weight.shape[0]

    blocks = blocks_of(total, rows)

    def kernel(_, q_ref, k_ref, v_ref, weight_ref, kept, sent):
        for block in range(blocks):
            span = slice(block * rows, (block + 1) * rows)
            grad = 0.0
            for place, ref in enumerate((q_ref, k_ref, v_ref)):
                lanes = slice(place * share, (place + 1) * share)
                grad = grad + dot_nt(ref[span, :], weight_ref[:, lanes])
            number = pl.program_id(0) * (blocks // 2) + block // 2
            (sent if block % 2 else kept)[number] = grad.astype(BF16)

    by_rows = pl.BlockSpec((rows * blocks, share), lambda i, _: (i, 0))
    halves = (total // rows // 2, rows, width)
    return run(
        kernel,
        [shape(halves), shape(halves)],
        grid=(total // rows // blocks,),
        scalars=scalars,
        specs=[by_rows] * 3 + [whole(weight.shape)],
        arrays=[*mixed, weight],
        out_specs=[whole(halves), whole(halves)],
        flops=2 * total * width * 3 * share,
    )


def tokens_back(scalars, addends, tokens, grad_middle, vectors):
    rows, width = tokens.shape
    block = min(rows, 128)

    def kernel(_, *refs):
        parts = refs[: len(addends)]
        tokens_ref, middle_ref, vectors_ref, out = refs[len(addends) :]
        grad = sum(part[0].astype(F32) for part in parts)
        unit, inverse = standard(tokens_ref[...].astype(F32))
        pulled = norm_pull(grad, vectors_ref[0:1, :], unit, inverse)
        out[...] = (middle_ref[...] + pulled).astype(BF16)

    by_rows = pl.BlockSpec((block, width), lambda i, _: (i, 0))
    return run(
        kernel,
        [shape((rows, width))],
        grid=(rows // block,),
        scalars=scalars,
        specs=[pl.BlockSpec((1, block, width), lambda i, _: (0, i, 0))] * len(addends)
        + [by_rows, by_rows, whole(vectors.shape)],
        arrays=[*addends, tokens, grad_middle, vectors],
        out_specs=[by_rows],
    )[0]


def place_attention(scalars, parts, strip, unit_strip):
    columns = parts[0].shape[1]
    share = columns // 4
    along = len(parts)
    own = scalars.shape[0] - 1

    def kernel(places, *refs):
        held, grad_in, grad_out, small, tail = refs[:along], *refs[along : along + 2], *refs[-2:]
        total = 0.0
        for number, ref in enumerate(held):
            spot = places[own] ^ number
            for place in range(4):
                part = ref[:strip, place * share : (place + 1) * share].astype(F32)
                target = grad_out if place == 3 else grad_in
                start = pl.multiple_of((place % 3 * along + spot) * share, 128)
                target[:, pl.ds(start, share)] = part
            extra = ref[strip:, :].astype(F32)
            total = total + extra
            row, start = field_at(6, strip, columns)
            target = pl.multiple_of(spot * unit_strip, 128)
            tail[:, pl.ds(target, unit_strip)] = extra[row : row + 1, start : start + unit_strip]
        for field in range(6):
            row, start = field_at(field, strip, columns)
            small[field : field + 1, :] = total[row : row + 1, start : start + strip]

    outs = [(strip, 3 * share * along), (strip, share * along), (8, strip), (1, along * unit_strip)]
    return run(
        kernel,
        [shape(out, F32) for out in outs],
        grid=(1,),
        scalars=scalars,
        specs=[whole(part.shape) for part in parts],
        arrays=parts,
        out_specs=[whole(out) for out in outs],
    )


def place_feed(scalars, parts, strip, unit_strip, groups):
    width = parts[0].shape[1]
    along = len(parts)
    own = scalars.shape[0] - 1

    def kernel(places, *refs):
        held, (grad_up, grad_down) = refs[:along], refs[along:]
        for number, ref in enumerate(held):
            spot = places[own] ^ number
            for group in range(groups):
                start = pl.multiple_of((group * along + spot) * unit_strip, 128)
                lanes = slice(group * unit_strip, (group + 1) * unit_strip)
                grad_up[:, pl.ds(start, unit_strip)] = ref[:strip, lanes].astype(F32)
            start = pl.multiple_of(spot * unit_strip, 16)
            grad_down[pl.ds(start, unit_strip), :] = ref[strip:, :].astype(F32)

    outs = [(strip, groups * along * unit_strip), (along * unit_strip, width)]
    return run(
        kernel,
        [shape(out, F32) for out in outs],
        grid=(1,),
        scalars=scalars,
        specs=[whole(part.shape) for part in parts],
        arrays=parts,
        out_specs=[whole(out) for out in outs],
    )


def natural(parts, mine):
    return jnp.take(jnp.stack(parts), mine ^ jnp.arange(len(parts)), axis=0)


def local(
    groups,
    along,
    tokens,
    cotangent,
    scene_lengths,
    key_mask,
    project_in,
    project_out,
    up_weight,
    down_weight,
    in_gain,
    in_shift,
    out_shift,
    mid_gain,
    mid_shift,
    up_shift,
    down_shift,
):
    rows, width = tokens.shape[1:]
    total = rows * along
    hidden_units = up_weight.shape[1]
    strip = width // groups
    share = width // along
    unit_strip = hidden_units // groups // along
    units = unit_strip * groups
    mine, group = lax.axis_index("seq"), lax.axis_index("fsdp")
    order = ring_order(groups)
    rings = []
    for device in order_table(order):
        rings += [[*device, place] for place in range(along)]
    scalars = lax.dynamic_index_in_dim(
        jnp.array(rings, jnp.int32), group * along + mine, 0, keepdims=False
    )
    cut = max(unit_strip // 2 // 16, 1) * 16
    own_tokens = tokens[0]
    own_cot = cotangent[0]

    fields = [in_gain, in_shift, out_shift, mid_gain, mid_shift, down_shift]
    in_part = select(
        scalars,
        [project_in] * 3 + [project_out],
        [0, along, 2 * along, 0],
        share,
        [field.reshape(1, strip) for field in fields] + [up_shift.reshape(along, -1)],
    )
    token_parts = spread(after(own_tokens, in_part), along)
    unit, all_tokens = standardize(scalars, token_parts)
    in_parts = ring_gather(in_part, order, strip // 2, [[], [*token_parts[1 : along - 1]]])
    hops = [[part for d, _, part in in_parts if d in (i, groups - i)] for i in range(1, groups // 2 + 1)]

    cot_parts = spread(after(own_cot, token_parts[-2], *hops[2]), along)
    up_weight, down_weight, key_mask = lax.optimization_barrier(
        (up_weight, down_weight, key_mask, *hops[0])
    )[:3]
    up_part = select(scalars, [up_weight] * groups, [along * i for i in range(groups)], unit_strip)
    down_part = lax.dynamic_slice_in_dim(down_weight, mine * unit_strip, unit_strip, 0)
    query_mask, key_table = tables(scalars, scene_lengths, key_mask, along)
    up_part = after(up_part, key_table)
    all_cot = jnp.concatenate(cot_parts)
    joined = up_part.shape[1] == down_part.shape[1]
    normed, query, keys, values, in_weight, out_columns, vectors, up_shift_all = project(
        scalars, unit, in_parts, rows, strip, unit_strip
    )
    outs = spread(out_columns, along)
    pairs = head_pairs(share)[0]
    attended = attend(scalars, query, keys, values, query_mask, key_table, 0)
    if joined:
        feed_part = after(jnp.concatenate([up_part, down_part]), *hops[-1])
        rings = [ring_gather(feed_part, order, strip, [[attended[0]]])]
    else:
        rings = [ring_gather(up_part, order, strip // 2), ring_gather(down_part, order, cut)]
    first_hop = [part for d, _, part in rings[0] if d in (1, groups - 1)]
    for pair in range(1, pairs):
        query = after(query, outs[1], attended[0], all_cot, *first_hop)
        attended = attend(scalars, query, keys, values, query_mask, key_table, pair, attended)
    attended, extra = attended
    all_attended = spread(attended, along)
    if share % 128:
        outs = [jnp.transpose(natural(outs, mine), (1, 0, 2)).reshape(width, width)]

    gathered, normed_mid, middle = attend_out(
        scalars, all_attended, all_tokens, vectors, outs, rows
    )
    active, grad_hidden, kept, sent, grad_up_shift, down_all = feed(
        scalars, normed_mid, all_cot, up_shift_all, rings, rows, strip
    )
    addends, sends = fold(kept, sent, along)
    active, normed_mid = lax.optimization_barrier((active, normed_mid, sends[-1]))[:2]
    up_pieces = outer(scalars, normed_mid, grad_hidden, groups)
    down_pieces = outer(scalars, active, all_cot, groups)
    if joined:
        sums = [RingSum(scalars, [up_pieces, down_pieces], order, strip)]
    else:
        sums = [
            RingSum(scalars, [up_pieces], order, strip // 2),
            RingSum(scalars, [down_pieces], order, cut),
        ]
    feed_sum = sums[0]
    grad_middle, grad_branch, middle_sums = middle_back(
        scalars, addends, middle, own_cot, vectors
    )
    branches = spread(grad_branch, along)
    active = after(active, *feed_sum.advance(grad_branch))
    result_addends, result_sends = fold(*descend(scalars, active, down_all, rows), along)
    ready = after(attended, *feed_sum.advance())
    grads, grad_extra = attended_back(scalars, branches, outs, ready)
    mixed = ()
    for pair in range(pairs):
        mixed = attend_back(
            scalars, query, extra, keys, key_table, values, grads, grad_extra, pair, mixed
        )
        if pair == 0:
            grads = after(grads, result_sends[-1], *feed_sum.advance(mixed[0]))
    pieces = projection_grads(
        scalars,
        after(normed, result_addends[-1]),
        mixed,
        gathered,
        branches,
        in_weight,
        vectors,
        middle_sums,
        grad_up_shift,
        groups,
    )
    feed_grads = [ring.finish() for ring in sums]
    pieces = after(pieces, feed_grads[0])
    attention_sum = RingSum(scalars, [pieces], order, strip // 2)
    feed_parts = spread(feed_grads[0], along)
    mixed = lax.optimization_barrier((*mixed, *attention_sum.advance(feed_parts[-2])))[:3]
    addends, sends = fold(*normed_back(scalars, mixed, in_weight, rows), along)
    fits = joined and not (share % 128 or unit_strip % 128)
    result = middle + vectors[5:6] + sum(part[0].astype(F32) for part in result_addends)
    result = result.astype(BF16)
    done = [result]
    if fits:
        grad_up, grad_down = place_feed(scalars, feed_parts, strip, unit_strip, groups)
        done += [grad_up, grad_down]
    attention_sum.advance(sends[-1], *done)
    grad_tokens = tokens_back(scalars, addends, own_tokens, grad_middle, vectors)
    attention_grads = after(attention_sum.finish(), grad_tokens)

    parts = spread(attention_grads, along)
    if fits:
        grad_in, grad_out, small, tail = place_attention(scalars, parts, strip, unit_strip)
    else:
        both = natural(parts, mine).astype(F32)
        grad_in = jnp.transpose(
            both[:, :strip, : 3 * share].reshape(along, strip, 3, share), (1, 2, 0, 3)
        ).reshape(strip, 3 * width)
        grad_out = jnp.transpose(both[:, :strip, 3 * share :], (1, 0, 2)).reshape(strip, width)
        small = jnp.sum(both[:, strip:], axis=0).reshape(-1, strip)
        tail = both[:, strip:].reshape(along, -1, strip)[:, 6, :unit_strip]
        ups = natural(feed_parts, mine).astype(F32)
        ups = ups.reshape(along, strip, groups, unit_strip)
        grad_up = jnp.transpose(ups, (1, 2, 0, 3)).reshape(strip, hidden_units)
        grad_down = natural(spread(feed_grads[1], along), mine).astype(F32)
        grad_down = grad_down.reshape(along * unit_strip, width)
    small = [small[i] for i in range(6)]
    return (
        result[None],
        grad_tokens[None],
        grad_in,
        grad_out,
        grad_up,
        grad_down,
        small[0],
        small[1],
        small[2],
        small[3],
        small[4],
        tail.reshape(-1),
        small[5],
    )


def solution(mesh):
    by_token = P("fsdp", "seq", None)
    by_row, by_part = P("fsdp", None), P("fsdp")
    return jax.shard_map(
        functools.partial(local, mesh.shape["fsdp"], mesh.shape["seq"]),
        mesh=mesh,
        in_specs=(by_token,) * 2 + (by_row,) * 6 + (by_part,) * 7,
        out_specs=(by_token,) * 2 + (by_row,) * 4 + (by_part,) * 7,
        check_vma=False,
    )
```

```python
import functools
import math

import jax
import jax.numpy as jnp
from jax import lax
from jax.experimental import pallas as pl
from jax.experimental.pallas import tpu as pltpu
from jax.sharding import PartitionSpec as P


HEADS = 16
HEAD_DIM = 64
EPSILON = 1e-05
MASKED = -1e30
MIB = 1 << 20
F32 = jnp.float32
BF16 = jnp.bfloat16
LOG2E = math.log2(math.e)
HBM = pl.BlockSpec(memory_space=pl.ANY)
STEP = 1024


def ring_order(count):
    wide = max(count // 4, 1)
    tall = count // wide
    path = [(row, 0) for row in range(tall)]
    for row in reversed(range(tall)):
        columns = list(range(1, wide))
        if (tall - 1 - row) % 2:
            columns.reverse()
        path += [(row, column) for column in columns]
    return [row * wide + column for row, column in path]


def order_table(order):
    count = len(order)
    rows = []
    for device in range(count):
        spot = order.index(device)
        rows.append(
            [order[(spot + i) % count] for i in range(count)]
            + [(order.index(i) - spot) % count for i in range(count)]
            + [device]
        )
    return rows


def ring_steps(order):
    onward = list(zip(order, order[1:] + order[:1]))
    return onward, [(target, source) for source, target in onward]


def after(value, *others):
    return lax.optimization_barrier((value, *others))[0] if others else value


def ring_gather(block, order, cut, waits=()):
    onward, backward = ring_steps(order)
    count = len(order)
    half = count // 2
    parts = [(0, 0, block)]
    left = right = block
    waits = dict(enumerate(waits, 2))
    for step in range(1, half):
        if step in waits:
            left, right = lax.optimization_barrier((left, right, *waits[step]))[:2]
        left = lax.ppermute(left, "fsdp", onward)
        right = lax.ppermute(right, "fsdp", backward)
        parts += [(count - step, 0, left), (step, 0, right)]
    if half in waits:
        left, right = lax.optimization_barrier((left, right, *waits[half]))[:2]
    parts.append((half, 0, lax.ppermute(left[:cut], "fsdp", onward)))
    if cut < block.shape[0]:
        parts.append((half, cut, lax.ppermute(right[cut:], "fsdp", backward)))
    return parts


class RingSum:
    def __init__(self, scalars, pieces, order, cut):
        self.scalars, self.pieces = scalars, pieces
        self.onward, self.backward = ring_steps(order)
        self.count, self.step = len(order), 1
        far = [part[self.count // 2] for part in pieces]
        if len(far) == 2 and far[0].shape[0] == cut:
            self.left, self.right = far
        else:
            far = jnp.concatenate(far)
            self.left, self.right = far[:cut], far[cut:]
        self.send()

    def send(self):
        self.left = lax.ppermute(self.left, "fsdp", self.onward)
        if self.right is not None and self.right.shape[0]:
            self.right = lax.ppermute(self.right, "fsdp", self.backward)
        else:
            self.right = None

    def advance(self, *waits):
        if self.step == self.count // 2:
            return []
        left = after(self.left, *waits)
        near, far = self.count // 2 - self.step, self.count // 2 + self.step
        self.left, self.right = merge(self.scalars, self.pieces, near, far, left, self.right)
        sent = [self.left, self.right]
        self.send()
        self.step += 1
        return sent

    def finish(self):
        while self.step < self.count // 2:
            self.advance()
        return merge(self.scalars, self.pieces, 0, None, self.left, self.right)


def swap(value, axis, count, bit):
    return lax.ppermute(value, axis, [(i, i ^ bit) for i in range(count)])


def spread(block, count):
    parts = {0: block}
    bit = count // 2
    while bit:
        parts.update({place | bit: swap(part, "seq", count, bit) for place, part in parts.items()})
        bit //= 2
    return [parts[place] for place in range(count)]


def fold(kept, sent, count):
    addends, sends = [kept], [sent]
    bit = 1
    while True:
        addends.append(swap(sends[-1], "seq", count, bit))
        bit *= 2
        if bit == count:
            return addends, sends
        sends.append(sum(part[1::2].astype(F32) for part in addends).astype(BF16))
        addends = [part[0::2] for part in addends]


def run(kernel, outs, *, grid, scalars, specs, arrays, out_specs, scratch=(), flops=0, vmem=20, kept=None):
    return pl.pallas_call(
        kernel,
        out_shape=[jax.ShapeDtypeStruct(o.shape, o.dtype) for o in outs],
        grid_spec=pltpu.PrefetchScalarGridSpec(
            num_scalar_prefetch=1,
            grid=grid,
            in_specs=specs,
            out_specs=out_specs,
            scratch_shapes=list(scratch),
        ),
        input_output_aliases=kept or {},
        compiler_params=pltpu.CompilerParams(vmem_limit_bytes=vmem * MIB),
        cost_estimate=pl.CostEstimate(flops=0, bytes_accessed=1024, transcendentals=0),
    )(scalars, *arrays)


def shape(dims, dtype=BF16):
    return jax.ShapeDtypeStruct(dims, dtype)


def whole(dims):
    return pl.BlockSpec(dims, lambda *_: (0,) * len(dims))


def dot(left, right):
    return jnp.dot(left, right, preferred_element_type=F32)


def dot_nt(left, right):
    return lax.dot_general(left, right, (((1,), (1,)), ((), ())), preferred_element_type=F32)


def dot_tn(left, right):
    return lax.dot_general(left, right, (((0,), (0,)), ((), ())), preferred_element_type=F32)


def each(count, body):
    if count == 1:
        body(0)
    else:
        lax.fori_loop(0, count, lambda number, carry: (body(number), carry)[1], 0)


def blocks_of(total, rows):
    return min(total, 1024) // rows


def standard(values):
    center = values - jnp.mean(values, axis=-1, keepdims=True)
    spread_of = jnp.mean(center * center, axis=-1, keepdims=True)
    inverse = lax.rsqrt(spread_of + EPSILON)
    return center * inverse, inverse


def norm_pull(grad, gain, unit, inverse):
    slope = grad * gain
    first = jnp.mean(slope, axis=-1, keepdims=True)
    second = jnp.mean(slope * unit, axis=-1, keepdims=True)
    return inverse * (slope - first - unit * second)


def column_sum(values):
    return jnp.sum(values, axis=0, keepdims=True)


def landing(parts, refs, fields, places, sems):
    height = sum(part.shape[0] for distance, _, part in parts if distance == 0)
    copies = []
    for (distance, start, part), ref in zip(parts, refs):
        for (low, high), columns, target in fields:
            high = high or height
            begin, end = max(low, start), min(high, start + part.shape[0])
            if begin >= end:
                continue
            offset = places[distance] * (high - low) + (begin - low)
            source = ref.at[pl.ds(begin - start, end - begin)]
            if columns is not None:
                source = ref.at[pl.ds(begin - start, end - begin), pl.ds(*columns)]
            target = target.at[pl.ds(pl.multiple_of(offset, 16), end - begin)]
            copies.append(pltpu.make_async_copy(source, target, sems.at[len(copies)]))
    return copies


def landings(parts, fields):
    return len(parts) * fields


def wait_all(copies):
    for copy in copies:
        copy.start()
    for copy in copies:
        copy.wait()


def merge(scalars, pieces, near, far, left, right):
    heights = [part.shape[1] for part in pieces]
    height, width = sum(heights), pieces[0].shape[2]
    arrays, specs = [], []
    for distance in (near,) if far is None else (near, far):
        for part, rows in zip(pieces, heights):
            arrays.append(part)
            specs.append(pl.BlockSpec((1, rows, width), lambda i, _, d=distance: (d, 0, 0)))
    sums = [part for part in (left, right) if part is not None]

    def kernel(_, *refs):
        held = refs[: len(arrays)]
        sums_refs = list(refs[len(arrays) : len(arrays) + len(sums)])
        outs = refs[len(arrays) + len(sums) :]
        first = left.shape[0]
        for side, out in enumerate(outs):
            start = 0
            for ref, rows in zip(held[side * len(pieces) :], heights):
                own = ref[0].astype(F32)
                span = slice(start, start + rows)
                if far is None:
                    for part in sums_refs:
                        own = own + part[span, :].astype(F32)
                    out[span, :] = own.astype(BF16)
                elif side < len(sums) and sums[side].shape[0] == height:
                    out[span, :] = (own + sums_refs[side][span, :].astype(F32)).astype(BF16)
                else:
                    out[span, :] = own.astype(BF16)
                start += rows
            if far is not None and side < len(sums) and sums[side].shape[0] < height:
                base = 0 if side == 0 else first
                rows = sums[side].shape[0]
                span = slice(base, base + rows)
                total = out[span, :].astype(F32) + sums_refs[side][...].astype(F32)
                out[span, :] = total.astype(BF16)

    whole_out = whole((height, width))
    count = 1 if far is None else 2
    outs = run(
        kernel,
        [shape((height, width))] * count,
        grid=(1,),
        scalars=scalars,
        specs=specs + [whole(part.shape) for part in sums],
        arrays=arrays + sums,
        out_specs=[whole_out] * count,
    )
    return outs[0] if far is None else outs


def select(scalars, arrays, starts, columns, fields=()):
    rows = arrays[0].shape[0]
    own = scalars.shape[0] - 1
    width = len(starts) * columns
    height = rows + (16 if fields else 0)
    if columns % 128:
        pick = lambda array, start, size: lax.dynamic_slice_in_dim(
            array, (start + scalars[own]) * size, size, 1
        )
        parts = [pick(array, start, columns) for array, start in zip(arrays, starts)]
        parts = jnp.concatenate(parts, axis=1)
        if not fields:
            return parts
        line = lax.dynamic_slice_in_dim(fields[-1], scalars[own], 1, 0)
        below = jnp.concatenate([*fields[:-1], line], axis=1)
        below = jnp.pad(below, ((0, 0), (0, 16 * width - below.shape[1])))
        return jnp.concatenate([parts, below.reshape(16, width)])

    def kernel(_, *refs):
        held = refs[: len(arrays) + len(fields)]
        out, sems, *lines = refs[len(held) :]
        mine = lax.axis_index("seq")
        copies = []
        for number, (ref, start) in enumerate(zip(held, starts)):
            begin = pl.multiple_of((start + mine) * columns, 128)
            target = out.at[pl.ds(0, rows), pl.ds(number * columns, columns)]
            copies.append((ref.at[:, pl.ds(begin, columns)], target))
        for number, ref in enumerate(held[len(arrays) :]):
            copies.append((ref, lines[number]))
        wait_all(
            [
                pltpu.make_async_copy(source, target, sems.at[number])
                for number, (source, target) in enumerate(copies)
            ]
        )
        if not fields:
            return
        size = lines[0].shape[1]
        per = width // size
        row = lax.broadcasted_iota(jnp.int32, (16, size), 0)
        values = [line[...].astype(F32) for line in lines]
        chosen = lax.broadcasted_iota(jnp.int32, values[-1].shape, 0) == mine
        values[-1] = column_sum(jnp.where(chosen, values[-1], 0.0))
        for start in range(per):
            value = jnp.zeros(row.shape, F32)
            for number in range(start, len(lines), per):
                value = jnp.where(row == number // per, values[number], value)
            out[rows:, start * size : (start + 1) * size] = value.astype(BF16)

    return run(
        kernel,
        [shape((height, width))],
        grid=(1,),
        scalars=jnp.zeros((1,), jnp.int32),
        specs=[pl.BlockSpec(memory_space=pltpu.HBM)] * (len(arrays) + len(fields)),
        arrays=[*arrays, *fields],
        out_specs=[whole((height, width))],
        scratch=[pltpu.SemaphoreType.DMA((len(arrays) + len(fields),))]
        + [pltpu.VMEM(field.shape, BF16) for field in fields],
        vmem=60 if fields else 20,
    )[0]


def tables(scalars, lengths, key_mask, along):
    total = key_mask.shape[1]
    rows = total // along
    scenes = lengths.shape[1]
    own = scalars.shape[0] - 1

    def kernel(places, lengths_ref, mask_ref, query_table, key_table):
        row = lax.broadcasted_iota(jnp.int32, (HEAD_DIM, rows), 0)
        for number in range(along):
            start = pl.multiple_of((places[own] ^ number) * rows, 128)
            spot = start + lax.broadcasted_iota(jnp.int32, (1, rows), 1)
            keep = mask_ref[:, pl.ds(start, rows)] == 1
            keep = jnp.where(keep, 1.0, 0.0)
            scene = jnp.zeros((1, rows), jnp.int32)
            edge = 0
            for part in range(scenes):
                keep = jnp.where(spot == edge, 1.0, keep)
                edge = edge + lengths_ref[0, part]
                scene = scene + jnp.where(spot >= edge, 1, 0)
            same = jnp.where(row == scene, 1.0, 0.0)
            keys = jnp.where(same * keep > 0.5, 0.0, MASKED)
            keys = jnp.where(row < scenes, keys, jnp.where(row < scenes + 3, -1.0, 0.0))
            span = slice(number * rows, (number + 1) * rows)
            query_table[span, :] = same.T.astype(BF16)
            key_table[span, :] = keys.T.astype(BF16)

    return run(
        kernel,
        [shape((total, HEAD_DIM))] * 2,
        grid=(1,),
        scalars=scalars,
        specs=[pl.BlockSpec(memory_space=pltpu.SMEM), whole(key_mask.shape)],
        arrays=[lengths, key_mask],
        out_specs=[whole((total, HEAD_DIM))] * 2,
    )


def standardize(scalars, tokens):
    rows, width = tokens[0].shape
    total = rows * len(tokens)

    def kernel(_, *refs):
        parts, (unit, joined) = refs[: len(tokens)], refs[len(tokens) :]
        for number, part in enumerate(parts):
            span = slice(number * rows, (number + 1) * rows)
            joined[span, :] = part[...]
            unit[span, :], _ = standard(part[...].astype(F32))

    return run(
        kernel,
        [shape((total, width), F32), shape((total, width))],
        grid=(1,),
        scalars=scalars,
        specs=[whole((rows, width))] * len(tokens),
        arrays=tokens,
        out_specs=[whole((total, width))] * 2,
    )


def field_at(number, strip, columns):
    per = columns // strip
    return number // per, number % per * strip


def project(scalars, unit, parts, rows, strip, unit_strip):
    total, width = unit.shape
    columns = parts[0][2].shape[1]
    share = columns // 4
    groups = width // strip
    count = landings(parts, 3)
    blocks = blocks_of(total, rows)

    def kernel(places, unit_ref, *refs):
        held = refs[: len(parts)]
        normed, query, keys, values, weight, out_weight, vectors, tail, extra, sems, *joint = refs[
            len(parts) :
        ]

        @pl.when(pl.program_id(0) == 0)
        def _():
            fields = [((strip, strip + 16), None, extra)]
            if joint:
                fields.append(((0, strip), None, joint[0]))
            else:
                fields.append(((0, strip), (0, 3 * share), weight))
                fields.append(((0, strip), (3 * share, share), out_weight))
            wait_all(landing(parts, held, fields, places, sems))
            if joint:
                weight[...] = joint[0][:, : 3 * share]
                out_weight[...] = joint[0][:, 3 * share :]
            for number in range(groups):
                block = extra[number * 16 : (number + 1) * 16, :].astype(F32)
                for field in range(7):
                    row, start = field_at(field, strip, columns)
                    part = block[row : row + 1, start : start + strip]
                    vectors[field : field + 1, number * strip : (number + 1) * strip] = part
                tail[:, number * unit_strip : (number + 1) * unit_strip] = part[:, :unit_strip]

        def block(number):
            span = pl.ds(pl.multiple_of(number * rows, rows), rows)
            part = (unit_ref[span, :] * vectors[0:1, :] + vectors[1:2, :]).astype(BF16)
            normed[span, :] = part
            mixed = dot(part, weight[...]).astype(BF16)
            query[span, :] = mixed[:, :share]
            keys[span, :] = mixed[:, share : 2 * share]
            values[span, :] = mixed[:, 2 * share :]

        each(blocks, block)

    by_rows = lambda w: pl.BlockSpec((rows * blocks, w), lambda i, _: (i, 0))
    return run(
        kernel,
        [shape((total, width))]
        + [shape((total, share))] * 3
        + [shape((width, 3 * share)), shape((width, share))]
        + [shape((8, width), F32), shape((1, groups * unit_strip), F32)],
        grid=(total // rows // blocks,),
        scalars=scalars,
        specs=[by_rows(width)] + [HBM] * len(parts),
        arrays=[unit] + [part for _, _, part in parts],
        out_specs=[by_rows(width)]
        + [by_rows(share)] * 3
        + [whole((width, 3 * share)), whole((width, share))]
        + [whole((8, width)), whole((1, groups * unit_strip))],
        scratch=[pltpu.VMEM((groups * 16, columns), BF16), pltpu.SemaphoreType.DMA((count,))]
        + [pltpu.VMEM((width, columns), BF16)] * (share % 128 > 0),
        flops=2 * total * width * 3 * share,
    )


def split_three(values):
    high = values.astype(BF16)
    rest = values - high.astype(F32)
    middle = rest.astype(BF16)
    return high, middle, (rest - middle.astype(F32)).astype(BF16)


def head_pairs(share):
    wide = min(share, 2 * HEAD_DIM)
    return share // wide, wide


def attend(scalars, query, keys, values, query_mask, key_mask, pair, before=()):
    total, share = query.shape
    wide = head_pairs(share)[1]
    rows = min(total, 256 * STEP // total)
    heads = wide // HEAD_DIM
    scale = HEAD_DIM**-0.5

    def kernel(_, q_ref, k_ref, v_ref, qm_ref, km_ref, *refs):
        attended, extra, k_held, v_held = refs[len(before) :]
        ones = jnp.ones((total, HEAD_DIM), BF16)
        place = lax.broadcasted_iota(jnp.int32, (rows, HEAD_DIM), 1)
        for head in range(heads):
            lanes = slice(head * HEAD_DIM, (head + 1) * HEAD_DIM)
            k_held[head] = jnp.concatenate([k_ref[:, lanes], km_ref[...]], axis=1)
            v_held[head] = jnp.concatenate([v_ref[:, lanes], ones], axis=1)

        def block(number):
            span = pl.ds(pl.multiple_of(number * rows, rows), rows)
            mask = qm_ref[span, :]
            outs, extras = [], []
            for head in range(heads):
                lanes = slice(head * HEAD_DIM, (head + 1) * HEAD_DIM)
                q = jnp.concatenate([q_ref[span, lanes], mask], axis=1)
                scores = dot_nt(q, k_held[head])
                top = jnp.max(scores, axis=1, keepdims=True)
                weights = jnp.exp2((scores - top) * (LOG2E * scale)).astype(BF16)
                summed = dot(weights, v_held[head])
                amount = summed[:, HEAD_DIM : HEAD_DIM + 1]
                outs.append(summed[:, :HEAD_DIM] / amount)
                high, middle, low = split_three(top + jnp.log(amount) / scale)
                tail = jnp.where(place == 4, middle, jnp.where(place == 5, low, mask))
                extras.append(jnp.where(place == 3, high, tail))
            attended[span, :] = jnp.concatenate(outs, axis=1).astype(BF16)
            extra[span, :] = jnp.concatenate(extras, axis=1)

        each(total // rows, block)

    fixed = pl.BlockSpec((total, wide), lambda i, _: (0, pair))
    table = whole((total, HEAD_DIM))
    return run(
        kernel,
        [shape((total, share))] * 2,
        grid=(1,),
        scalars=scalars,
        specs=[fixed, fixed, fixed, table, table] + [HBM] * len(before),
        arrays=[query, keys, values, query_mask, key_mask, *before],
        out_specs=[fixed, fixed],
        scratch=[pltpu.VMEM((heads, total, 2 * HEAD_DIM), BF16)] * 2,
        kept={6 + number: number for number in range(len(before))},
        flops=4 * 4 * total * total * wide,
    )


def column_copies(places, refs, target, sems, rows):
    own = places.shape[0] - 1
    if len(refs) == 1:
        return [pltpu.make_async_copy(refs[0].at[rows], target, sems.at[0])]
    columns = refs[0].shape[1]
    return [
        pltpu.make_async_copy(
            ref.at[rows],
            target.at[:, pl.ds(pl.multiple_of((places[own] ^ place) * columns, 128), columns)],
            sems.at[place],
        )
        for place, ref in enumerate(refs)
    ]


def attend_out(scalars, attended, tokens, vectors, outs, rows):
    places_along = len(attended)
    total, width = tokens.shape
    share = attended[0].shape[1]
    own = scalars.shape[0] - 1

    def kernel(places, *refs):
        attended_refs, refs = refs[:places_along], refs[places_along:]
        tokens_ref, vectors_ref = refs[:2]
        held, (gathered, normed, middle_own, out_ref, sems) = (
            refs[2 : 2 + len(outs)],
            refs[2 + len(outs) :],
        )
        step = pl.program_id(0)

        @pl.when(step == 0)
        def _():
            wait_all(column_copies(places, held, out_ref, sems, pl.ds(0, width)))

        for place, ref in enumerate(attended_refs):
            gathered[:, place * share : (place + 1) * share] = ref[...]
        branch = vectors_ref[2:3, :]
        for place in range(places_along):
            start = pl.multiple_of((places[own] ^ place) * share, share)
            branch = branch + dot(attended_refs[place][...], out_ref[pl.ds(start, share), :])
        middle = tokens_ref[...].astype(F32) + branch

        @pl.when(step == 0)
        def _():
            middle_own[...] = middle

        unit, _ = standard(middle)
        normed[...] = (unit * vectors_ref[3:4, :] + vectors_ref[4:5, :]).astype(BF16)

    by_rows = pl.BlockSpec((rows, width), lambda i, _: (i, 0))
    part_of = lambda x: pl.BlockSpec((rows, share), lambda i, _: (i ^ x, 0))
    return run(
        kernel,
        [shape((total, width)), shape((total, width)), shape((rows, width), F32)],
        grid=(places_along,),
        scalars=scalars,
        specs=[part_of(x) for x in range(places_along)]
        + [by_rows, whole(vectors.shape)]
        + [HBM] * len(outs),
        arrays=[*attended, tokens, vectors, *outs],
        out_specs=[by_rows, by_rows, whole((rows, width))],
        scratch=[pltpu.VMEM((width, width), BF16), pltpu.SemaphoreType.DMA((len(outs),))],
        flops=2 * total * width * width,
    )


def feed(scalars, normed, cotangent, up_shift, rings, rows, strip):
    total, width = normed.shape
    units = up_shift.shape[1]
    steps, blocks = total // rows, blocks_of(total, rows)
    parts = [part for ring in rings for part in ring]
    signals = 2 * len(parts)

    def kernel(places, *refs):
        normed_ref, cot_ref, shift_ref = refs[:3]
        held = refs[3 : 3 + len(parts)]
        active, grad_hidden, kept, sent, grad_shift, down, up, sems = refs[3 + len(parts) :]
        step = pl.program_id(0)

        @pl.when(step == 0)
        def _():
            if len(rings) == 1:
                fields = [((0, strip), None, up), ((strip, None), None, down)]
                copies = landing(rings[0], held, fields, places, sems)
            else:
                first, second = held[: len(rings[0])], held[len(rings[0]) :]
                copies = landing(rings[0], first, [((0, None), None, up)], places, sems)
                left = sems.at[pl.ds(len(copies), signals - len(copies))]
                copies += landing(rings[1], second, [((0, None), None, down)], places, left)
            wait_all(copies)
            grad_shift[...] = jnp.zeros_like(grad_shift)

        def pair(number):
            for half, out in enumerate((kept, sent)):
                span = pl.ds(pl.multiple_of((2 * number + half) * rows, rows), rows)
                hidden = dot(normed_ref[span, :], up[...]) + shift_ref[...]
                share_of = 0.5 + 0.5 * lax.erf(hidden * (0.5**0.5))
                active[span, :] = (hidden * share_of).astype(BF16)
                slope = share_of + hidden * (
                    jnp.exp2(hidden * hidden * (-0.5 * LOG2E)) * ((2 * math.pi) ** -0.5)
                )
                grad = (slope * dot_nt(cot_ref[span, :], down[...])).astype(BF16)
                grad_hidden[span, :] = grad
                grad_shift[...] += column_sum(grad.astype(F32))
                out[step * (blocks // 2) + number] = dot_nt(grad, up[...]).astype(BF16)

        each(blocks // 2, pair)

    by_rows = lambda w: pl.BlockSpec((rows * blocks, w), lambda i, _: (i, 0))
    halves = (steps // 2, rows, width)
    return run(
        kernel,
        [
            shape((total, units)),
            shape((total, units)),
            shape(halves),
            shape(halves),
            shape((1, units), F32),
            shape((units, width)),
        ],
        grid=(steps // blocks,),
        scalars=scalars,
        specs=[by_rows(width), by_rows(width), whole(up_shift.shape)] + [HBM] * len(parts),
        arrays=[normed, cotangent, up_shift] + [part for _, _, part in parts],
        out_specs=[
            by_rows(units),
            by_rows(units),
            whole(halves),
            whole(halves),
            whole((1, units)),
            whole((units, width)),
        ],
        scratch=[pltpu.VMEM((width, units), BF16), pltpu.SemaphoreType.DMA((signals,))],
        flops=6 * total * width * units,
        vmem=32,
    )


def descend(scalars, active, down, rows):
    total, units = active.shape
    width = down.shape[1]

    blocks = blocks_of(total, rows)

    def kernel(_, active_ref, down_ref, kept, sent):
        def pair(number):
            for half, out in enumerate((kept, sent)):
                span = pl.ds(pl.multiple_of((2 * number + half) * rows, rows), rows)
                part = dot(active_ref[span, :], down_ref[...]).astype(BF16)
                out[pl.program_id(0) * (blocks // 2) + number] = part

        each(blocks // 2, pair)

    halves = (total // rows // 2, rows, width)
    return run(
        kernel,
        [shape(halves)] * 2,
        grid=(total // rows // blocks,),
        scalars=scalars,
        specs=[pl.BlockSpec((rows * blocks, units), lambda i, _: (i, 0)), whole(down.shape)],
        arrays=[active, down],
        out_specs=[whole(halves)] * 2,
        flops=2 * total * units * width,
    )


def outer(scalars, left, right, count):
    total, height = left.shape
    width = right.shape[1]
    rows = min(height, 256)
    piece = height // count

    def kernel(places, left_ref, right_ref, out):
        def block(number):
            start = pl.multiple_of(number * rows, rows)
            product = dot_tn(left_ref[:, pl.ds(start, rows)], right_ref[...]).astype(BF16)
            for part in range(rows // piece):
                target = places[count + number * (rows // piece) + part]
                out[target] = product[part * piece : (part + 1) * piece]

        each(height // rows, block)

    return run(
        kernel,
        [shape((count, piece, width))],
        grid=(1,),
        scalars=scalars,
        specs=[whole(left.shape), whole(right.shape)],
        arrays=[left, right],
        out_specs=[whole((count, piece, width))],
        flops=2 * total * height * width,
    )[0]


def middle_back(scalars, addends, middle, cotangent, vectors):
    rows, width = middle.shape
    block = min(rows, 128)

    def kernel(_, *refs):
        parts = refs[: len(addends)]
        middle_ref, cot_ref, vectors_ref, grad_middle, grad_branch, sums = refs[len(addends) :]
        grad = sum(part[0].astype(F32) for part in parts)
        cot = cot_ref[...].astype(F32)
        unit, inverse = standard(middle_ref[...])
        total = cot + norm_pull(grad, vectors_ref[3:4, :], unit, inverse)
        grad_middle[...] = total
        branch = total.astype(BF16)
        grad_branch[...] = branch

        @pl.when(pl.program_id(0) == 0)
        def _():
            sums[...] = jnp.zeros_like(sums)

        sums[0:1, :] += column_sum(branch.astype(F32))
        sums[1:2, :] += column_sum(grad * unit)
        sums[2:3, :] += column_sum(grad)
        sums[3:4, :] += column_sum(cot)

    by_rows = pl.BlockSpec((block, width), lambda i, _: (i, 0))
    return run(
        kernel,
        [shape((rows, width), F32), shape((rows, width)), shape((8, width), F32)],
        grid=(rows // block,),
        scalars=scalars,
        specs=[pl.BlockSpec((1, block, width), lambda i, _: (0, i, 0))] * len(addends)
        + [by_rows, by_rows, whole(vectors.shape)],
        arrays=[*addends, middle, cotangent, vectors],
        out_specs=[by_rows, by_rows, whole((8, width))],
    )


def attended_back(scalars, branches, outs, attended):
    count = len(branches)
    total, share = attended.shape
    rows, width = branches[0].shape
    own = scalars.shape[0] - 1

    def kernel(places, *refs):
        parts, held = refs[:count], refs[count : count + len(outs)]
        attended_ref, grads, extras, out_ref, sems = refs[count + len(outs) :]
        start = pl.multiple_of(places[own] * share, 16)
        wait_all(column_copies(places, held, out_ref, sems, pl.ds(start, share)))
        line = lax.broadcasted_iota(jnp.int32, (share, share), 0) // HEAD_DIM
        lane = lax.broadcasted_iota(jnp.int32, (share, share), 1) // HEAD_DIM
        over_head = jnp.where(line == lane, 1.0, 0.0).astype(BF16)
        place = lax.broadcasted_iota(jnp.int32, (rows, share), 1) % HEAD_DIM
        for number, part in enumerate(parts):
            span = slice(number * rows, (number + 1) * rows)
            grad = dot_nt(part[...], out_ref[...]).astype(BF16)
            grads[span, :] = grad
            product = grad.astype(F32) * attended_ref[span, :].astype(F32)
            delta = sum(dot(piece, over_head) for piece in split_three(product))
            high, middle, low = (piece.astype(F32) for piece in split_three(delta))
            extra = jnp.where(place == 4, middle, jnp.where(place == 5, low, 0.0))
            extras[span, :] = jnp.where(place == 3, high, extra).astype(BF16)

    return run(
        kernel,
        [shape((total, share))] * 2,
        grid=(1,),
        scalars=scalars,
        specs=[whole((rows, width))] * count
        + [HBM] * len(outs)
        + [whole((total, share))],
        arrays=[*branches, *outs, attended],
        out_specs=[whole((total, share))] * 2,
        scratch=[pltpu.VMEM((share, width), BF16), pltpu.SemaphoreType.DMA((len(outs),))],
        flops=2 * total * width * share,
    )


def attend_back(scalars, query, extra, keys, key_mask, values, grads, grad_extra, pair, before=()):
    total, share = query.shape
    wide = head_pairs(share)[1]
    rows = min(total, 256 * STEP // total)
    heads = wide // HEAD_DIM
    scale = HEAD_DIM**-0.5

    def kernel(_, q_ref, qx_ref, k_ref, km_ref, v_ref, g_ref, gx_ref, *refs):
        dq_ref, dk_ref, dv_ref, held, q_held, g_held = refs[len(before) :]
        held[...] = jnp.zeros_like(held)
        for head in range(heads):
            lanes = slice(head * HEAD_DIM, (head + 1) * HEAD_DIM)
            q_held[head] = jnp.concatenate([q_ref[:, lanes], qx_ref[:, lanes]], axis=1)
            g_held[head] = jnp.concatenate([g_ref[:, lanes], gx_ref[:, lanes]], axis=1)

        def block(number):
            span = pl.ds(pl.multiple_of(number * rows, rows), rows)
            mask = km_ref[span, :]
            grad_keys, grad_values = [], []
            for head in range(heads):
                lanes = slice(head * HEAD_DIM, (head + 1) * HEAD_DIM)
                key_part = k_ref[span, lanes]
                k = jnp.concatenate([key_part, mask], axis=1)
                v = jnp.concatenate([v_ref[span, lanes], jnp.maximum(mask, -1.0)], axis=1)
                shares = jnp.exp2(dot_nt(k, q_held[head]) * (LOG2E * scale))
                grad_scores = (shares * dot_nt(v, g_held[head])).astype(BF16)
                grad_values.append(dot(shares.astype(BF16), g_ref[:, lanes]))
                grad_keys.append(dot(grad_scores, q_ref[:, lanes]) * scale)
                held[lanes, :] += dot_tn(key_part, grad_scores) * scale
            dk_ref[span, :] = jnp.concatenate(grad_keys, axis=1).astype(BF16)
            dv_ref[span, :] = jnp.concatenate(grad_values, axis=1).astype(BF16)

        each(total // rows, block)
        dq_ref[...] = held[...].T.astype(BF16)

    fixed = pl.BlockSpec((total, wide), lambda i, _: (0, pair))
    return run(
        kernel,
        [shape((total, share))] * 3,
        grid=(1,),
        scalars=scalars,
        specs=[fixed, fixed, fixed, whole((total, HEAD_DIM)), fixed, fixed, fixed]
        + [HBM] * len(before),
        arrays=[query, extra, keys, key_mask, values, grads, grad_extra, *before],
        out_specs=[fixed, fixed, fixed],
        scratch=[pltpu.VMEM((wide, total), F32)]
        + [pltpu.VMEM((heads, total, 2 * HEAD_DIM), BF16)] * 2,
        kept={8 + number: number for number in range(len(before))},
        flops=10 * 4 * total * total * wide,
    )


def projection_grads(
    scalars, normed, mixed, gathered, branches, weight, vectors, middle_sums, up_sums, count
):
    total, width = normed.shape
    share = mixed[0].shape[1]
    rows = max(min(width, 256 * STEP // total), 128)
    piece = width // count
    units = up_sums.shape[1] // count
    block_rows = branches[0].shape[0]
    own = scalars.shape[0] - 1
    per = share // piece
    column = pl.BlockSpec((block_rows, share), lambda i, w: (0, w[own]))
    if share % 128:
        column = whole((block_rows, share))
        branches = [
            lax.dynamic_slice_in_dim(part, scalars[own] * share, share, 1) for part in branches
        ]

    def to_row(values):
        if values.shape[1] % 128 == 0:
            values = sum(
                values[:, start : start + 128] for start in range(0, values.shape[1], 128)
            )
        return jnp.sum(values.T, axis=0, keepdims=True)

    def kernel(places, normed_ref, gathered_ref, weight_ref, vectors_ref, sums_ref, up_ref, *refs):
        mixed_refs, parts = refs[:3], refs[3 : 3 + len(branches)]
        out, totals, fields = refs[3 + len(branches) :]
        for place, ref in enumerate(mixed_refs):
            totals[place : place + 1, :] = column_sum(ref[...].astype(F32))
        for number in range(count):
            span = slice(number * piece, (number + 1) * piece)
            fields[number, 2:6, :] = sums_ref[0:4, span]
            fields[number, 6:7, :units] = up_ref[:, number * units : (number + 1) * units]

        def block(step):
            begin = pl.ds(pl.multiple_of(step * rows, 128), rows)
            left = normed_ref[:, begin]
            products, gain, shift = [], 0.0, 0.0
            for place, ref in enumerate(mixed_refs):
                product = dot_tn(left, ref[...])
                products.append(product.astype(BF16))
                part = weight_ref[begin, place * share : (place + 1) * share].astype(F32)
                gain = gain + to_row(product * part)
                shift = shift + to_row(part * totals[place : place + 1, :])
            gain = (gain - vectors_ref[1:2, begin] * shift) / vectors_ref[0:1, begin]
            branch = 0.0
            for number, part in enumerate(parts):
                held = gathered_ref[number * block_rows : (number + 1) * block_rows, begin]
                branch = branch + dot_tn(held, part[...])
            branch = branch.astype(BF16)
            for part in range(rows // piece):
                span = slice(part * piece, (part + 1) * piece)
                number = step * (rows // piece) + part
                target = places[count + number]
                for place, product in enumerate(products):
                    out[target, :piece, place * share : (place + 1) * share] = product[span]
                held = fields[number]
                entries = [gain[:, span], shift[:, span]] + [held[i : i + 1] for i in range(2, 7)]
                row = lax.broadcasted_iota(jnp.int32, (16, piece), 0)
                spots = [field_at(number, piece, 4 * share) for number in range(7)]
                for start in range(0, 4 * share, piece):
                    value = jnp.zeros((16, piece), F32)
                    for entry, (line, first) in zip(entries, spots):
                        if first == start:
                            value = jnp.where(row == line, entry, value)
                    out[target, piece:, start : start + piece] = value.astype(BF16)
                natural = ((number // per) ^ places[own]) * per + number % per
                out[places[count + natural], :piece, 3 * share :] = branch[span]

        each(width // rows, block)

    return run(
        kernel,
        [shape((count, piece + 16, 4 * share))],
        grid=(1,),
        scalars=scalars,
        specs=[whole((total, width))] * 2
        + [whole(weight.shape), whole(vectors.shape)]
        + [whole(middle_sums.shape), whole(up_sums.shape)]
        + [whole((total, share))] * 3
        + [column] * len(branches),
        arrays=[normed, gathered, weight, vectors, middle_sums, up_sums, *mixed, *branches],
        out_specs=[whole((count, piece + 16, 4 * share))],
        scratch=[pltpu.VMEM((8, share), F32), pltpu.VMEM((count, 8, piece), F32)],
        flops=2 * total * width * 4 * share,
        vmem=40 if total > STEP else 24,
    )[0]


def normed_back(scalars, mixed, weight, rows):
    total, share = mixed[0].shape
    width = weight.shape[0]

    blocks = blocks_of(total, rows)

    def kernel(_, q_ref, k_ref, v_ref, weight_ref, kept, sent):
        def pair(number):
            for half, out in enumerate((kept, sent)):
                span = pl.ds(pl.multiple_of((2 * number + half) * rows, rows), rows)
                grad = 0.0
                for place, ref in enumerate((q_ref, k_ref, v_ref)):
                    lanes = slice(place * share, (place + 1) * share)
                    grad = grad + dot_nt(ref[span, :], weight_ref[:, lanes])
                out[pl.program_id(0) * (blocks // 2) + number] = grad.astype(BF16)

        each(blocks // 2, pair)

    by_rows = pl.BlockSpec((rows * blocks, share), lambda i, _: (i, 0))
    halves = (total // rows // 2, rows, width)
    return run(
        kernel,
        [shape(halves), shape(halves)],
        grid=(total // rows // blocks,),
        scalars=scalars,
        specs=[by_rows] * 3 + [whole(weight.shape)],
        arrays=[*mixed, weight],
        out_specs=[whole(halves), whole(halves)],
        flops=2 * total * width * 3 * share,
    )


def tokens_back(scalars, addends, tokens, grad_middle, vectors):
    rows, width = tokens.shape
    block = min(rows, 128)

    def kernel(_, *refs):
        parts = refs[: len(addends)]
        tokens_ref, middle_ref, vectors_ref, out = refs[len(addends) :]
        grad = sum(part[0].astype(F32) for part in parts)
        unit, inverse = standard(tokens_ref[...].astype(F32))
        pulled = norm_pull(grad, vectors_ref[0:1, :], unit, inverse)
        out[...] = (middle_ref[...] + pulled).astype(BF16)

    by_rows = pl.BlockSpec((block, width), lambda i, _: (i, 0))
    return run(
        kernel,
        [shape((rows, width))],
        grid=(rows // block,),
        scalars=scalars,
        specs=[pl.BlockSpec((1, block, width), lambda i, _: (0, i, 0))] * len(addends)
        + [by_rows, by_rows, whole(vectors.shape)],
        arrays=[*addends, tokens, grad_middle, vectors],
        out_specs=[by_rows],
    )[0]


def place_attention(scalars, parts, strip, unit_strip):
    columns = parts[0].shape[1]
    share = columns // 4
    along = len(parts)
    own = scalars.shape[0] - 1

    def kernel(places, *refs):
        held, grad_in, grad_out, small, tail = refs[:along], *refs[along : along + 2], *refs[-2:]
        total = 0.0
        for number, ref in enumerate(held):
            spot = places[own] ^ number
            for place in range(4):
                part = ref[:strip, place * share : (place + 1) * share].astype(F32)
                target = grad_out if place == 3 else grad_in
                start = pl.multiple_of((place % 3 * along + spot) * share, 128)
                target[:, pl.ds(start, share)] = part
            extra = ref[strip:, :].astype(F32)
            total = total + extra
            row, start = field_at(6, strip, columns)
            target = pl.multiple_of(spot * unit_strip, 128)
            tail[:, pl.ds(target, unit_strip)] = extra[row : row + 1, start : start + unit_strip]
        for field in range(6):
            row, start = field_at(field, strip, columns)
            small[field : field + 1, :] = total[row : row + 1, start : start + strip]

    outs = [(strip, 3 * share * along), (strip, share * along), (8, strip), (1, along * unit_strip)]
    return run(
        kernel,
        [shape(out, F32) for out in outs],
        grid=(1,),
        scalars=scalars,
        specs=[whole(part.shape) for part in parts],
        arrays=parts,
        out_specs=[whole(out) for out in outs],
    )


def place_feed(scalars, parts, strip, unit_strip, groups):
    width = parts[0].shape[1]
    along = len(parts)
    own = scalars.shape[0] - 1

    def kernel(places, *refs):
        held, (grad_up, grad_down) = refs[:along], refs[along:]
        for number, ref in enumerate(held):
            spot = places[own] ^ number
            for group in range(groups):
                start = pl.multiple_of((group * along + spot) * unit_strip, 128)
                lanes = slice(group * unit_strip, (group + 1) * unit_strip)
                grad_up[:, pl.ds(start, unit_strip)] = ref[:strip, lanes].astype(F32)
            start = pl.multiple_of(spot * unit_strip, 16)
            grad_down[pl.ds(start, unit_strip), :] = ref[strip:, :].astype(F32)

    outs = [(strip, groups * along * unit_strip), (along * unit_strip, width)]
    return run(
        kernel,
        [shape(out, F32) for out in outs],
        grid=(1,),
        scalars=scalars,
        specs=[whole(part.shape) for part in parts],
        arrays=parts,
        out_specs=[whole(out) for out in outs],
    )


def natural(parts, mine):
    return jnp.take(jnp.stack(parts), mine ^ jnp.arange(len(parts)), axis=0)


def local(
    groups,
    along,
    tokens,
    cotangent,
    scene_lengths,
    key_mask,
    project_in,
    project_out,
    up_weight,
    down_weight,
    in_gain,
    in_shift,
    out_shift,
    mid_gain,
    mid_shift,
    up_shift,
    down_shift,
):
    rows, width = tokens.shape[1:]
    total = rows * along
    hidden_units = up_weight.shape[1]
    strip = width // groups
    share = width // along
    unit_strip = hidden_units // groups // along
    units = unit_strip * groups
    mine, group = lax.axis_index("seq"), lax.axis_index("fsdp")
    order = ring_order(groups)
    rings = []
    for device in order_table(order):
        rings += [[*device, place] for place in range(along)]
    scalars = lax.dynamic_index_in_dim(
        jnp.array(rings, jnp.int32), group * along + mine, 0, keepdims=False
    )
    cut = max(unit_strip // 2 // 16, 1) * 16
    own_tokens = tokens[0]
    own_cot = cotangent[0]

    fields = [in_gain, in_shift, out_shift, mid_gain, mid_shift, down_shift]
    in_part = select(
        scalars,
        [project_in] * 3 + [project_out],
        [0, along, 2 * along, 0],
        share,
        [field.reshape(1, strip) for field in fields] + [up_shift.reshape(along, -1)],
    )
    token_parts = spread(after(own_tokens, in_part), along)
    unit, all_tokens = standardize(scalars, token_parts)
    in_parts = ring_gather(in_part, order, strip // 2, [[], [*token_parts[1 : along - 1]]])
    hops = [[part for d, _, part in in_parts if d in (i, groups - i)] for i in range(1, groups // 2 + 1)]

    cot_parts = spread(after(own_cot, token_parts[-2], *hops[2]), along)
    up_weight, down_weight, key_mask = lax.optimization_barrier(
        (up_weight, down_weight, key_mask, *hops[0])
    )[:3]
    up_part = select(scalars, [up_weight] * groups, [along * i for i in range(groups)], unit_strip)
    down_part = lax.dynamic_slice_in_dim(down_weight, mine * unit_strip, unit_strip, 0)
    query_mask, key_table = tables(scalars, scene_lengths, key_mask, along)
    up_part = after(up_part, key_table)
    all_cot = jnp.concatenate(cot_parts)
    joined = up_part.shape[1] == down_part.shape[1]
    normed, query, keys, values, in_weight, out_columns, vectors, up_shift_all = project(
        scalars, unit, in_parts, rows, strip, unit_strip
    )
    outs = spread(out_columns, along)
    pairs = head_pairs(share)[0]
    attended = attend(scalars, query, keys, values, query_mask, key_table, 0)
    if joined:
        feed_part = after(jnp.concatenate([up_part, down_part]), *hops[-1])
        rings = [ring_gather(feed_part, order, strip, [[attended[0]]])]
    else:
        rings = [ring_gather(up_part, order, strip // 2), ring_gather(down_part, order, cut)]
    first_hop = [part for d, _, part in rings[0] if d in (1, groups - 1)]
    for pair in range(1, pairs):
        query = after(query, outs[1], attended[0], all_cot, *first_hop)
        attended = attend(scalars, query, keys, values, query_mask, key_table, pair, attended)
    attended, extra = attended
    all_attended = spread(attended, along)
    if share % 128:
        outs = [jnp.transpose(natural(outs, mine), (1, 0, 2)).reshape(width, width)]

    gathered, normed_mid, middle = attend_out(
        scalars, all_attended, all_tokens, vectors, outs, rows
    )
    active, grad_hidden, kept, sent, grad_up_shift, down_all = feed(
        scalars, normed_mid, all_cot, up_shift_all, rings, rows, strip
    )
    addends, sends = fold(kept, sent, along)
    active, normed_mid = lax.optimization_barrier((active, normed_mid, sends[-1]))[:2]
    up_pieces = outer(scalars, normed_mid, grad_hidden, groups)
    down_pieces = outer(scalars, active, all_cot, groups)
    if joined:
        sums = [RingSum(scalars, [up_pieces, down_pieces], order, strip)]
    else:
        sums = [
            RingSum(scalars, [up_pieces], order, strip // 2),
            RingSum(scalars, [down_pieces], order, cut),
        ]
    feed_sum = sums[0]
    grad_middle, grad_branch, middle_sums = middle_back(
        scalars, addends, middle, own_cot, vectors
    )
    branches = spread(grad_branch, along)
    active = after(active, *feed_sum.advance(grad_branch))
    result_addends, result_sends = fold(*descend(scalars, active, down_all, rows), along)
    ready = after(attended, *feed_sum.advance())
    grads, grad_extra = attended_back(scalars, branches, outs, ready)
    mixed = ()
    for pair in range(pairs):
        mixed = attend_back(
            scalars, query, extra, keys, key_table, values, grads, grad_extra, pair, mixed
        )
        if pair == 0:
            grads = after(grads, result_sends[-1], *feed_sum.advance(mixed[0]))
    pieces = projection_grads(
        scalars,
        after(normed, result_addends[-1]),
        mixed,
        gathered,
        branches,
        in_weight,
        vectors,
        middle_sums,
        grad_up_shift,
        groups,
    )
    feed_grads = [ring.finish() for ring in sums]
    pieces = after(pieces, feed_grads[0])
    attention_sum = RingSum(scalars, [pieces], order, strip // 2)
    feed_parts = spread(feed_grads[0], along)
    mixed = lax.optimization_barrier((*mixed, *attention_sum.advance(feed_parts[-2])))[:3]
    addends, sends = fold(*normed_back(scalars, mixed, in_weight, rows), along)
    fits = joined and not (share % 128 or unit_strip % 128)
    result = middle + vectors[5:6] + sum(part[0].astype(F32) for part in result_addends)
    result = result.astype(BF16)
    done = [result]
    if fits:
        grad_up, grad_down = place_feed(scalars, feed_parts, strip, unit_strip, groups)
        done += [grad_up, grad_down]
    attention_sum.advance(sends[-1], *done)
    grad_tokens = tokens_back(scalars, addends, own_tokens, grad_middle, vectors)
    attention_grads = after(attention_sum.finish(), grad_tokens)

    parts = spread(attention_grads, along)
    if fits:
        grad_in, grad_out, small, tail = place_attention(scalars, parts, strip, unit_strip)
    else:
        both = natural(parts, mine).astype(F32)
        grad_in = jnp.transpose(
            both[:, :strip, : 3 * share].reshape(along, strip, 3, share), (1, 2, 0, 3)
        ).reshape(strip, 3 * width)
        grad_out = jnp.transpose(both[:, :strip, 3 * share :], (1, 0, 2)).reshape(strip, width)
        small = jnp.sum(both[:, strip:], axis=0).reshape(-1, strip)
        tail = both[:, strip:].reshape(along, -1, strip)[:, 6, :unit_strip]
        ups = natural(feed_parts, mine).astype(F32)
        ups = ups.reshape(along, strip, groups, unit_strip)
        grad_up = jnp.transpose(ups, (1, 2, 0, 3)).reshape(strip, hidden_units)
        grad_down = natural(spread(feed_grads[1], along), mine).astype(F32)
        grad_down = grad_down.reshape(along * unit_strip, width)
    small = [small[i] for i in range(6)]
    return (
        result[None],
        grad_tokens[None],
        grad_in,
        grad_out,
        grad_up,
        grad_down,
        small[0],
        small[1],
        small[2],
        small[3],
        small[4],
        tail.reshape(-1),
        small[5],
    )


def solution(mesh):
    by_token = P("fsdp", "seq", None)
    by_row, by_part = P("fsdp", None), P("fsdp")
    return jax.shard_map(
        functools.partial(local, mesh.shape["fsdp"], mesh.shape["seq"]),
        mesh=mesh,
        in_specs=(by_token,) * 2 + (by_row,) * 6 + (by_part,) * 7,
        out_specs=(by_token,) * 2 + (by_row,) * 4 + (by_part,) * 7,
        check_vma=False,
    )
```

```python
import functools
import math

import jax
import jax.numpy as jnp
from jax import lax
from jax.experimental import pallas as pl
from jax.experimental.pallas import tpu as pltpu
from jax.sharding import PartitionSpec as P


HEADS = 16
HEAD_DIM = 64
EPSILON = 1e-05
MASKED = -1e30
MIB = 1 << 20
F32 = jnp.float32
BF16 = jnp.bfloat16
LOG2E = math.log2(math.e)
HBM = pl.BlockSpec(memory_space=pl.ANY)
STEP = 1024


def ring_order(count):
    wide = max(count // 4, 1)
    tall = count // wide
    path = [(row, 0) for row in range(tall)]
    for row in reversed(range(tall)):
        columns = list(range(1, wide))
        if (tall - 1 - row) % 2:
            columns.reverse()
        path += [(row, column) for column in columns]
    return [row * wide + column for row, column in path]


def order_table(order):
    count = len(order)
    rows = []
    for device in range(count):
        spot = order.index(device)
        rows.append(
            [order[(spot + i) % count] for i in range(count)]
            + [(order.index(i) - spot) % count for i in range(count)]
            + [device]
        )
    return rows


def ring_steps(order):
    onward = list(zip(order, order[1:] + order[:1]))
    return onward, [(target, source) for source, target in onward]


def after(value, *others):
    return lax.optimization_barrier((value, *others))[0] if others else value


def ring_gather(block, order, cut, waits=()):
    onward, backward = ring_steps(order)
    count = len(order)
    half = count // 2
    parts = [(0, 0, block)]
    left = right = block
    waits = dict(enumerate(waits, 2))
    for step in range(1, half):
        if step in waits:
            left, right = lax.optimization_barrier((left, right, *waits[step]))[:2]
        left = lax.ppermute(left, "fsdp", onward)
        right = lax.ppermute(right, "fsdp", backward)
        parts += [(count - step, 0, left), (step, 0, right)]
    if half in waits:
        left, right = lax.optimization_barrier((left, right, *waits[half]))[:2]
    parts.append((half, 0, lax.ppermute(left[:cut], "fsdp", onward)))
    if cut < block.shape[0]:
        parts.append((half, cut, lax.ppermute(right[cut:], "fsdp", backward)))
    return parts


class RingSum:
    def __init__(self, scalars, pieces, order, cut):
        self.scalars, self.pieces = scalars, pieces
        self.onward, self.backward = ring_steps(order)
        self.count, self.step = len(order), 1
        far = [part[self.count // 2] for part in pieces]
        if len(far) == 2 and far[0].shape[0] == cut:
            self.left, self.right = far
        else:
            far = jnp.concatenate(far)
            self.left, self.right = far[:cut], far[cut:]
        self.send()

    def send(self):
        self.left = lax.ppermute(self.left, "fsdp", self.onward)
        if self.right is not None and self.right.shape[0]:
            self.right = lax.ppermute(self.right, "fsdp", self.backward)
        else:
            self.right = None

    def advance(self, *waits):
        if self.step == self.count // 2:
            return []
        left = after(self.left, *waits)
        near, far = self.count // 2 - self.step, self.count // 2 + self.step
        self.left, self.right = merge(self.scalars, self.pieces, near, far, left, self.right)
        sent = [self.left, self.right]
        self.send()
        self.step += 1
        return sent

    def finish(self):
        while self.step < self.count // 2:
            self.advance()
        return merge(self.scalars, self.pieces, 0, None, self.left, self.right)


def swap(value, axis, count, bit):
    return lax.ppermute(value, axis, [(i, i ^ bit) for i in range(count)])


def spread(block, count):
    parts = {0: block}
    bit = count // 2
    while bit:
        parts.update({place | bit: swap(part, "seq", count, bit) for place, part in parts.items()})
        bit //= 2
    return [parts[place] for place in range(count)]


def fold(kept, sent, count):
    addends, sends = [kept], [sent]
    bit = 1
    while True:
        addends.append(swap(sends[-1], "seq", count, bit))
        bit *= 2
        if bit == count:
            return addends, sends
        sends.append(sum(part[1::2].astype(F32) for part in addends).astype(BF16))
        addends = [part[0::2] for part in addends]


def run(kernel, outs, *, grid, scalars, specs, arrays, out_specs, scratch=(), flops=0, vmem=20, kept=None):
    return pl.pallas_call(
        kernel,
        out_shape=[jax.ShapeDtypeStruct(o.shape, o.dtype) for o in outs],
        grid_spec=pltpu.PrefetchScalarGridSpec(
            num_scalar_prefetch=1,
            grid=grid,
            in_specs=specs,
            out_specs=out_specs,
            scratch_shapes=list(scratch),
        ),
        input_output_aliases=kept or {},
        compiler_params=pltpu.CompilerParams(vmem_limit_bytes=vmem * MIB),
        cost_estimate=pl.CostEstimate(flops=0, bytes_accessed=1024, transcendentals=0),
    )(scalars, *arrays)


def shape(dims, dtype=BF16):
    return jax.ShapeDtypeStruct(dims, dtype)


def whole(dims):
    return pl.BlockSpec(dims, lambda *_: (0,) * len(dims))


def dot(left, right):
    return jnp.dot(left, right, preferred_element_type=F32)


def dot_nt(left, right):
    return lax.dot_general(left, right, (((1,), (1,)), ((), ())), preferred_element_type=F32)


def dot_tn(left, right):
    return lax.dot_general(left, right, (((0,), (0,)), ((), ())), preferred_element_type=F32)


def each(count, body):
    if count == 1:
        body(0)
    else:
        lax.fori_loop(0, count, lambda number, carry: (body(number), carry)[1], 0)


def blocks_of(total, rows):
    return min(total, 1024) // rows


def standard(values):
    center = values - jnp.mean(values, axis=-1, keepdims=True)
    spread_of = jnp.mean(center * center, axis=-1, keepdims=True)
    inverse = lax.rsqrt(spread_of + EPSILON)
    return center * inverse, inverse


def norm_pull(grad, gain, unit, inverse):
    slope = grad * gain
    first = jnp.mean(slope, axis=-1, keepdims=True)
    second = jnp.mean(slope * unit, axis=-1, keepdims=True)
    return inverse * (slope - first - unit * second)


def column_sum(values):
    return jnp.sum(values, axis=0, keepdims=True)


def landing(parts, refs, fields, places, sems):
    height = sum(part.shape[0] for distance, _, part in parts if distance == 0)
    copies = []
    for (distance, start, part), ref in zip(parts, refs):
        for (low, high), columns, target in fields:
            high = high or height
            begin, end = max(low, start), min(high, start + part.shape[0])
            if begin >= end:
                continue
            offset = places[distance] * (high - low) + (begin - low)
            source = ref.at[pl.ds(begin - start, end - begin)]
            if columns is not None:
                source = ref.at[pl.ds(begin - start, end - begin), pl.ds(*columns)]
            target = target.at[pl.ds(pl.multiple_of(offset, 16), end - begin)]
            copies.append(pltpu.make_async_copy(source, target, sems.at[len(copies)]))
    return copies


def landings(parts, fields):
    return len(parts) * fields


def wait_all(copies):
    for copy in copies:
        copy.start()
    for copy in copies:
        copy.wait()


def merge(scalars, pieces, near, far, left, right):
    heights = [part.shape[1] for part in pieces]
    height, width = sum(heights), pieces[0].shape[2]
    arrays, specs = [], []
    for distance in (near,) if far is None else (near, far):
        for part, rows in zip(pieces, heights):
            arrays.append(part)
            specs.append(pl.BlockSpec((1, rows, width), lambda i, _, d=distance: (d, 0, 0)))
    sums = [part for part in (left, right) if part is not None]

    def kernel(_, *refs):
        held = refs[: len(arrays)]
        sums_refs = list(refs[len(arrays) : len(arrays) + len(sums)])
        outs = refs[len(arrays) + len(sums) :]
        first = left.shape[0]
        for side, out in enumerate(outs):
            start = 0
            for ref, rows in zip(held[side * len(pieces) :], heights):
                own = ref[0].astype(F32)
                span = slice(start, start + rows)
                if far is None:
                    for part in sums_refs:
                        own = own + part[span, :].astype(F32)
                    out[span, :] = own.astype(BF16)
                elif side < len(sums) and sums[side].shape[0] == height:
                    out[span, :] = (own + sums_refs[side][span, :].astype(F32)).astype(BF16)
                else:
                    out[span, :] = own.astype(BF16)
                start += rows
            if far is not None and side < len(sums) and sums[side].shape[0] < height:
                base = 0 if side == 0 else first
                rows = sums[side].shape[0]
                span = slice(base, base + rows)
                total = out[span, :].astype(F32) + sums_refs[side][...].astype(F32)
                out[span, :] = total.astype(BF16)

    whole_out = whole((height, width))
    count = 1 if far is None else 2
    outs = run(
        kernel,
        [shape((height, width))] * count,
        grid=(1,),
        scalars=scalars,
        specs=specs + [whole(part.shape) for part in sums],
        arrays=arrays + sums,
        out_specs=[whole_out] * count,
    )
    return outs[0] if far is None else outs


def select(scalars, arrays, starts, columns, fields=()):
    rows = arrays[0].shape[0]
    own = scalars.shape[0] - 1
    width = len(starts) * columns
    height = rows + (16 if fields else 0)
    if columns % 128:
        pick = lambda array, start, size: lax.dynamic_slice_in_dim(
            array, (start + scalars[own]) * size, size, 1
        )
        parts = [pick(array, start, columns) for array, start in zip(arrays, starts)]
        parts = jnp.concatenate(parts, axis=1)
        if not fields:
            return parts
        line = lax.dynamic_slice_in_dim(fields[-1], scalars[own], 1, 0)
        below = jnp.concatenate([*fields[:-1], line], axis=1)
        below = jnp.pad(below, ((0, 0), (0, 16 * width - below.shape[1])))
        return jnp.concatenate([parts, below.reshape(16, width)])

    def kernel(_, *refs):
        held = refs[: len(arrays) + len(fields)]
        out, sems, *lines = refs[len(held) :]
        mine = lax.axis_index("seq")
        copies = []
        for number, (ref, start) in enumerate(zip(held, starts)):
            begin = pl.multiple_of((start + mine) * columns, 128)
            target = out.at[pl.ds(0, rows), pl.ds(number * columns, columns)]
            copies.append((ref.at[:, pl.ds(begin, columns)], target))
        for number, ref in enumerate(held[len(arrays) :]):
            copies.append((ref, lines[number]))
        wait_all(
            [
                pltpu.make_async_copy(source, target, sems.at[number])
                for number, (source, target) in enumerate(copies)
            ]
        )
        if not fields:
            return
        size = lines[0].shape[1]
        per = width // size
        row = lax.broadcasted_iota(jnp.int32, (16, size), 0)
        values = [line[...].astype(F32) for line in lines]
        chosen = lax.broadcasted_iota(jnp.int32, values[-1].shape, 0) == mine
        values[-1] = column_sum(jnp.where(chosen, values[-1], 0.0))
        for start in range(per):
            value = jnp.zeros(row.shape, F32)
            for number in range(start, len(lines), per):
                value = jnp.where(row == number // per, values[number], value)
            out[rows:, start * size : (start + 1) * size] = value.astype(BF16)

    return run(
        kernel,
        [shape((height, width))],
        grid=(1,),
        scalars=jnp.zeros((1,), jnp.int32),
        specs=[pl.BlockSpec(memory_space=pltpu.HBM)] * (len(arrays) + len(fields)),
        arrays=[*arrays, *fields],
        out_specs=[whole((height, width))],
        scratch=[pltpu.SemaphoreType.DMA((len(arrays) + len(fields),))]
        + [pltpu.VMEM(field.shape, BF16) for field in fields],
        vmem=60 if fields else 20,
    )[0]


def tables(scalars, lengths, key_mask, along):
    total = key_mask.shape[1]
    rows = total // along
    scenes = lengths.shape[1]
    own = scalars.shape[0] - 1

    def kernel(places, lengths_ref, mask_ref, query_table, key_table):
        row = lax.broadcasted_iota(jnp.int32, (HEAD_DIM, rows), 0)
        for number in range(along):
            start = pl.multiple_of((places[own] ^ number) * rows, 128)
            spot = start + lax.broadcasted_iota(jnp.int32, (1, rows), 1)
            keep = mask_ref[:, pl.ds(start, rows)] == 1
            keep = jnp.where(keep, 1.0, 0.0)
            scene = jnp.zeros((1, rows), jnp.int32)
            edge = 0
            for part in range(scenes):
                keep = jnp.where(spot == edge, 1.0, keep)
                edge = edge + lengths_ref[0, part]
                scene = scene + jnp.where(spot >= edge, 1, 0)
            same = jnp.where(row == scene, 1.0, 0.0)
            keys = jnp.where(same * keep > 0.5, 0.0, MASKED)
            keys = jnp.where(row < scenes, keys, jnp.where(row < scenes + 3, -1.0, 0.0))
            span = slice(number * rows, (number + 1) * rows)
            query_table[span, :] = same.T.astype(BF16)
            key_table[span, :] = keys.T.astype(BF16)

    return run(
        kernel,
        [shape((total, HEAD_DIM))] * 2,
        grid=(1,),
        scalars=scalars,
        specs=[pl.BlockSpec(memory_space=pltpu.SMEM), whole(key_mask.shape)],
        arrays=[lengths, key_mask],
        out_specs=[whole((total, HEAD_DIM))] * 2,
    )


def standardize(scalars, tokens):
    rows, width = tokens[0].shape
    total = rows * len(tokens)

    def kernel(_, *refs):
        parts, (unit, joined) = refs[: len(tokens)], refs[len(tokens) :]
        for number, part in enumerate(parts):
            span = slice(number * rows, (number + 1) * rows)
            joined[span, :] = part[...]
            unit[span, :], _ = standard(part[...].astype(F32))

    return run(
        kernel,
        [shape((total, width), F32), shape((total, width))],
        grid=(1,),
        scalars=scalars,
        specs=[whole((rows, width))] * len(tokens),
        arrays=tokens,
        out_specs=[whole((total, width))] * 2,
    )


def field_at(number, strip, columns):
    per = columns // strip
    return number // per, number % per * strip


def project(scalars, unit, parts, rows, strip, unit_strip):
    total, width = unit.shape
    columns = parts[0][2].shape[1]
    share = columns // 4
    groups = width // strip
    count = landings(parts, 3)
    blocks = blocks_of(total, rows)

    def kernel(places, unit_ref, *refs):
        held = refs[: len(parts)]
        normed, query, keys, values, weight, out_weight, vectors, tail, extra, sems, *joint = refs[
            len(parts) :
        ]

        @pl.when(pl.program_id(0) == 0)
        def _():
            fields = [((strip, strip + 16), None, extra)]
            if joint:
                fields.append(((0, strip), None, joint[0]))
            else:
                fields.append(((0, strip), (0, 3 * share), weight))
                fields.append(((0, strip), (3 * share, share), out_weight))
            wait_all(landing(parts, held, fields, places, sems))
            if joint:
                weight[...] = joint[0][:, : 3 * share]
                out_weight[...] = joint[0][:, 3 * share :]
            for number in range(groups):
                block = extra[number * 16 : (number + 1) * 16, :].astype(F32)
                for field in range(7):
                    row, start = field_at(field, strip, columns)
                    part = block[row : row + 1, start : start + strip]
                    vectors[field : field + 1, number * strip : (number + 1) * strip] = part
                tail[:, number * unit_strip : (number + 1) * unit_strip] = part[:, :unit_strip]

        def block(number):
            span = pl.ds(pl.multiple_of(number * rows, rows), rows)
            part = (unit_ref[span, :] * vectors[0:1, :] + vectors[1:2, :]).astype(BF16)
            normed[span, :] = part
            mixed = dot(part, weight[...]).astype(BF16)
            query[span, :] = mixed[:, :share]
            keys[span, :] = mixed[:, share : 2 * share]
            values[span, :] = mixed[:, 2 * share :]

        each(blocks, block)

    by_rows = lambda w: pl.BlockSpec((rows * blocks, w), lambda i, _: (i, 0))
    return run(
        kernel,
        [shape((total, width))]
        + [shape((total, share))] * 3
        + [shape((width, 3 * share)), shape((width, share))]
        + [shape((8, width), F32), shape((1, groups * unit_strip), F32)],
        grid=(total // rows // blocks,),
        scalars=scalars,
        specs=[by_rows(width)] + [HBM] * len(parts),
        arrays=[unit] + [part for _, _, part in parts],
        out_specs=[by_rows(width)]
        + [by_rows(share)] * 3
        + [whole((width, 3 * share)), whole((width, share))]
        + [whole((8, width)), whole((1, groups * unit_strip))],
        scratch=[pltpu.VMEM((groups * 16, columns), BF16), pltpu.SemaphoreType.DMA((count,))]
        + [pltpu.VMEM((width, columns), BF16)] * (share % 128 > 0),
        flops=2 * total * width * 3 * share,
    )


def split_three(values):
    high = values.astype(BF16)
    rest = values - high.astype(F32)
    middle = rest.astype(BF16)
    return high, middle, (rest - middle.astype(F32)).astype(BF16)


def head_pairs(share):
    wide = min(share, 2 * HEAD_DIM)
    return share // wide, wide


def attend(scalars, query, keys, values, query_mask, key_mask, pair, before=()):
    total, share = query.shape
    wide = head_pairs(share)[1]
    rows = min(total, 512 * STEP // total)
    heads = wide // HEAD_DIM
    scale = HEAD_DIM**-0.5

    def kernel(_, q_ref, k_ref, v_ref, qm_ref, km_ref, *refs):
        attended, extra, k_held, v_held = refs[len(before) :]
        ones = jnp.ones((total, HEAD_DIM), BF16)
        place = lax.broadcasted_iota(jnp.int32, (rows, HEAD_DIM), 1)
        for head in range(heads):
            lanes = slice(head * HEAD_DIM, (head + 1) * HEAD_DIM)
            k_held[head] = jnp.concatenate([k_ref[:, lanes], km_ref[...]], axis=1)
            v_held[head] = jnp.concatenate([v_ref[:, lanes], ones], axis=1)

        def block(number):
            span = pl.ds(pl.multiple_of(number * rows, rows), rows)
            mask = qm_ref[span, :]
            outs, extras = [], []
            for head in range(heads):
                lanes = slice(head * HEAD_DIM, (head + 1) * HEAD_DIM)
                q = jnp.concatenate([q_ref[span, lanes], mask], axis=1)
                scores = dot_nt(q, k_held[head])
                top = jnp.max(scores, axis=1, keepdims=True)
                weights = jnp.exp2((scores - top) * (LOG2E * scale)).astype(BF16)
                summed = dot(weights, v_held[head])
                amount = summed[:, HEAD_DIM : HEAD_DIM + 1]
                outs.append(summed[:, :HEAD_DIM] / amount)
                high, middle, low = split_three(top + jnp.log(amount) / scale)
                tail = jnp.where(place == 4, middle, jnp.where(place == 5, low, mask))
                extras.append(jnp.where(place == 3, high, tail))
            attended[span, :] = jnp.concatenate(outs, axis=1).astype(BF16)
            extra[span, :] = jnp.concatenate(extras, axis=1)

        each(total // rows, block)

    fixed = pl.BlockSpec((total, wide), lambda i, _: (0, pair))
    table = whole((total, HEAD_DIM))
    return run(
        kernel,
        [shape((total, share))] * 2,
        grid=(1,),
        scalars=scalars,
        specs=[fixed, fixed, fixed, table, table] + [HBM] * len(before),
        arrays=[query, keys, values, query_mask, key_mask, *before],
        out_specs=[fixed, fixed],
        scratch=[pltpu.VMEM((heads, total, 2 * HEAD_DIM), BF16)] * 2,
        kept={6 + number: number for number in range(len(before))},
        flops=4 * 4 * total * total * wide,
    )


def column_copies(places, refs, target, sems, rows):
    own = places.shape[0] - 1
    if len(refs) == 1:
        return [pltpu.make_async_copy(refs[0].at[rows], target, sems.at[0])]
    columns = refs[0].shape[1]
    return [
        pltpu.make_async_copy(
            ref.at[rows],
            target.at[:, pl.ds(pl.multiple_of((places[own] ^ place) * columns, 128), columns)],
            sems.at[place],
        )
        for place, ref in enumerate(refs)
    ]


def attend_out(scalars, attended, tokens, vectors, outs, rows):
    places_along = len(attended)
    total, width = tokens.shape
    share = attended[0].shape[1]
    own = scalars.shape[0] - 1

    def kernel(places, *refs):
        attended_refs, refs = refs[:places_along], refs[places_along:]
        tokens_ref, vectors_ref = refs[:2]
        held, (gathered, normed, middle_own, out_ref, sems) = (
            refs[2 : 2 + len(outs)],
            refs[2 + len(outs) :],
        )
        step = pl.program_id(0)

        @pl.when(step == 0)
        def _():
            wait_all(column_copies(places, held, out_ref, sems, pl.ds(0, width)))

        for place, ref in enumerate(attended_refs):
            gathered[:, place * share : (place + 1) * share] = ref[...]
        branch = vectors_ref[2:3, :]
        for place in range(places_along):
            start = pl.multiple_of((places[own] ^ place) * share, share)
            branch = branch + dot(attended_refs[place][...], out_ref[pl.ds(start, share), :])
        middle = tokens_ref[...].astype(F32) + branch

        @pl.when(step == 0)
        def _():
            middle_own[...] = middle

        unit, _ = standard(middle)
        normed[...] = (unit * vectors_ref[3:4, :] + vectors_ref[4:5, :]).astype(BF16)

    by_rows = pl.BlockSpec((rows, width), lambda i, _: (i, 0))
    part_of = lambda x: pl.BlockSpec((rows, share), lambda i, _: (i ^ x, 0))
    return run(
        kernel,
        [shape((total, width)), shape((total, width)), shape((rows, width), F32)],
        grid=(places_along,),
        scalars=scalars,
        specs=[part_of(x) for x in range(places_along)]
        + [by_rows, whole(vectors.shape)]
        + [HBM] * len(outs),
        arrays=[*attended, tokens, vectors, *outs],
        out_specs=[by_rows, by_rows, whole((rows, width))],
        scratch=[pltpu.VMEM((width, width), BF16), pltpu.SemaphoreType.DMA((len(outs),))],
        flops=2 * total * width * width,
    )


def feed(scalars, normed, cotangent, up_shift, rings, rows, strip):
    total, width = normed.shape
    units = up_shift.shape[1]
    steps, blocks = total // rows, blocks_of(total, rows)
    parts = [part for ring in rings for part in ring]
    signals = 2 * len(parts)

    def kernel(places, *refs):
        normed_ref, cot_ref, shift_ref = refs[:3]
        held = refs[3 : 3 + len(parts)]
        active, grad_hidden, kept, sent, grad_shift, down, up, sems = refs[3 + len(parts) :]
        step = pl.program_id(0)

        @pl.when(step == 0)
        def _():
            if len(rings) == 1:
                fields = [((0, strip), None, up), ((strip, None), None, down)]
                copies = landing(rings[0], held, fields, places, sems)
            else:
                first, second = held[: len(rings[0])], held[len(rings[0]) :]
                copies = landing(rings[0], first, [((0, None), None, up)], places, sems)
                left = sems.at[pl.ds(len(copies), signals - len(copies))]
                copies += landing(rings[1], second, [((0, None), None, down)], places, left)
            wait_all(copies)
            grad_shift[...] = jnp.zeros_like(grad_shift)

        def pair(number):
            for half, out in enumerate((kept, sent)):
                span = pl.ds(pl.multiple_of((2 * number + half) * rows, rows), rows)
                hidden = dot(normed_ref[span, :], up[...]) + shift_ref[...]
                share_of = 0.5 + 0.5 * lax.erf(hidden * (0.5**0.5))
                active[span, :] = (hidden * share_of).astype(BF16)
                slope = share_of + hidden * (
                    jnp.exp2(hidden * hidden * (-0.5 * LOG2E)) * ((2 * math.pi) ** -0.5)
                )
                grad = (slope * dot_nt(cot_ref[span, :], down[...])).astype(BF16)
                grad_hidden[span, :] = grad
                grad_shift[...] += column_sum(grad.astype(F32))
                out[step * (blocks // 2) + number] = dot_nt(grad, up[...]).astype(BF16)

        each(blocks // 2, pair)

    by_rows = lambda w: pl.BlockSpec((rows * blocks, w), lambda i, _: (i, 0))
    halves = (steps // 2, rows, width)
    return run(
        kernel,
        [
            shape((total, units)),
            shape((total, units)),
            shape(halves),
            shape(halves),
            shape((1, units), F32),
            shape((units, width)),
        ],
        grid=(steps // blocks,),
        scalars=scalars,
        specs=[by_rows(width), by_rows(width), whole(up_shift.shape)] + [HBM] * len(parts),
        arrays=[normed, cotangent, up_shift] + [part for _, _, part in parts],
        out_specs=[
            by_rows(units),
            by_rows(units),
            whole(halves),
            whole(halves),
            whole((1, units)),
            whole((units, width)),
        ],
        scratch=[pltpu.VMEM((width, units), BF16), pltpu.SemaphoreType.DMA((signals,))],
        flops=6 * total * width * units,
        vmem=32,
    )


def descend(scalars, active, down, rows):
    total, units = active.shape
    width = down.shape[1]

    blocks = blocks_of(total, rows)

    def kernel(_, active_ref, down_ref, kept, sent):
        def pair(number):
            for half, out in enumerate((kept, sent)):
                span = pl.ds(pl.multiple_of((2 * number + half) * rows, rows), rows)
                part = dot(active_ref[span, :], down_ref[...]).astype(BF16)
                out[pl.program_id(0) * (blocks // 2) + number] = part

        each(blocks // 2, pair)

    halves = (total // rows // 2, rows, width)
    return run(
        kernel,
        [shape(halves)] * 2,
        grid=(total // rows // blocks,),
        scalars=scalars,
        specs=[pl.BlockSpec((rows * blocks, units), lambda i, _: (i, 0)), whole(down.shape)],
        arrays=[active, down],
        out_specs=[whole(halves)] * 2,
        flops=2 * total * units * width,
    )


def outer(scalars, left, right, count):
    total, height = left.shape
    width = right.shape[1]
    rows = min(height, 512)
    piece = height // count

    def kernel(places, left_ref, right_ref, out):
        def block(number):
            start = pl.multiple_of(number * rows, rows)
            product = dot_tn(left_ref[:, pl.ds(start, rows)], right_ref[...]).astype(BF16)
            for part in range(rows // piece):
                target = places[count + number * (rows // piece) + part]
                out[target] = product[part * piece : (part + 1) * piece]

        each(height // rows, block)

    return run(
        kernel,
        [shape((count, piece, width))],
        grid=(1,),
        scalars=scalars,
        specs=[whole(left.shape), whole(right.shape)],
        arrays=[left, right],
        out_specs=[whole((count, piece, width))],
        flops=2 * total * height * width,
    )[0]


def middle_back(scalars, addends, middle, cotangent, vectors):
    rows, width = middle.shape
    block = min(rows, 128)

    def kernel(_, *refs):
        parts = refs[: len(addends)]
        middle_ref, cot_ref, vectors_ref, grad_middle, grad_branch, sums = refs[len(addends) :]
        grad = sum(part[0].astype(F32) for part in parts)
        cot = cot_ref[...].astype(F32)
        unit, inverse = standard(middle_ref[...])
        total = cot + norm_pull(grad, vectors_ref[3:4, :], unit, inverse)
        grad_middle[...] = total
        branch = total.astype(BF16)
        grad_branch[...] = branch

        @pl.when(pl.program_id(0) == 0)
        def _():
            sums[...] = jnp.zeros_like(sums)

        sums[0:1, :] += column_sum(branch.astype(F32))
        sums[1:2, :] += column_sum(grad * unit)
        sums[2:3, :] += column_sum(grad)
        sums[3:4, :] += column_sum(cot)

    by_rows = pl.BlockSpec((block, width), lambda i, _: (i, 0))
    return run(
        kernel,
        [shape((rows, width), F32), shape((rows, width)), shape((8, width), F32)],
        grid=(rows // block,),
        scalars=scalars,
        specs=[pl.BlockSpec((1, block, width), lambda i, _: (0, i, 0))] * len(addends)
        + [by_rows, by_rows, whole(vectors.shape)],
        arrays=[*addends, middle, cotangent, vectors],
        out_specs=[by_rows, by_rows, whole((8, width))],
    )


def attended_back(scalars, branches, outs, attended):
    count = len(branches)
    total, share = attended.shape
    rows, width = branches[0].shape
    own = scalars.shape[0] - 1

    def kernel(places, *refs):
        parts, held = refs[:count], refs[count : count + len(outs)]
        attended_ref, grads, extras, out_ref, sems = refs[count + len(outs) :]
        start = pl.multiple_of(places[own] * share, 16)
        wait_all(column_copies(places, held, out_ref, sems, pl.ds(start, share)))
        line = lax.broadcasted_iota(jnp.int32, (share, share), 0) // HEAD_DIM
        lane = lax.broadcasted_iota(jnp.int32, (share, share), 1) // HEAD_DIM
        over_head = jnp.where(line == lane, 1.0, 0.0).astype(BF16)
        place = lax.broadcasted_iota(jnp.int32, (rows, share), 1) % HEAD_DIM
        for number, part in enumerate(parts):
            span = slice(number * rows, (number + 1) * rows)
            grad = dot_nt(part[...], out_ref[...]).astype(BF16)
            grads[span, :] = grad
            product = grad.astype(F32) * attended_ref[span, :].astype(F32)
            delta = sum(dot(piece, over_head) for piece in split_three(product))
            high, middle, low = (piece.astype(F32) for piece in split_three(delta))
            extra = jnp.where(place == 4, middle, jnp.where(place == 5, low, 0.0))
            extras[span, :] = jnp.where(place == 3, high, extra).astype(BF16)

    return run(
        kernel,
        [shape((total, share))] * 2,
        grid=(1,),
        scalars=scalars,
        specs=[whole((rows, width))] * count
        + [HBM] * len(outs)
        + [whole((total, share))],
        arrays=[*branches, *outs, attended],
        out_specs=[whole((total, share))] * 2,
        scratch=[pltpu.VMEM((share, width), BF16), pltpu.SemaphoreType.DMA((len(outs),))],
        flops=2 * total * width * share,
    )


def attend_back(scalars, query, extra, keys, key_mask, values, grads, grad_extra, pair, before=()):
    total, share = query.shape
    wide = head_pairs(share)[1]
    rows = min(total, 256 * STEP // total)
    heads = wide // HEAD_DIM
    scale = HEAD_DIM**-0.5

    def kernel(_, q_ref, qx_ref, k_ref, km_ref, v_ref, g_ref, gx_ref, *refs):
        dq_ref, dk_ref, dv_ref, held, q_held, g_held = refs[len(before) :]
        held[...] = jnp.zeros_like(held)
        for head in range(heads):
            lanes = slice(head * HEAD_DIM, (head + 1) * HEAD_DIM)
            q_held[head] = jnp.concatenate([q_ref[:, lanes], qx_ref[:, lanes]], axis=1)
            g_held[head] = jnp.concatenate([g_ref[:, lanes], gx_ref[:, lanes]], axis=1)

        def block(number):
            span = pl.ds(pl.multiple_of(number * rows, rows), rows)
            mask = km_ref[span, :]
            grad_keys, grad_values = [], []
            for head in range(heads):
                lanes = slice(head * HEAD_DIM, (head + 1) * HEAD_DIM)
                key_part = k_ref[span, lanes]
                k = jnp.concatenate([key_part, mask], axis=1)
                v = jnp.concatenate([v_ref[span, lanes], jnp.maximum(mask, -1.0)], axis=1)
                shares = jnp.exp2(dot_nt(k, q_held[head]) * (LOG2E * scale))
                grad_scores = (shares * dot_nt(v, g_held[head])).astype(BF16)
                grad_values.append(dot(shares.astype(BF16), g_ref[:, lanes]))
                grad_keys.append(dot(grad_scores, q_ref[:, lanes]) * scale)
                held[lanes, :] += dot_tn(key_part, grad_scores) * scale
            dk_ref[span, :] = jnp.concatenate(grad_keys, axis=1).astype(BF16)
            dv_ref[span, :] = jnp.concatenate(grad_values, axis=1).astype(BF16)

        each(total // rows, block)
        dq_ref[...] = held[...].T.astype(BF16)

    fixed = pl.BlockSpec((total, wide), lambda i, _: (0, pair))
    return run(
        kernel,
        [shape((total, share))] * 3,
        grid=(1,),
        scalars=scalars,
        specs=[fixed, fixed, fixed, whole((total, HEAD_DIM)), fixed, fixed, fixed]
        + [HBM] * len(before),
        arrays=[query, extra, keys, key_mask, values, grads, grad_extra, *before],
        out_specs=[fixed, fixed, fixed],
        scratch=[pltpu.VMEM((wide, total), F32)]
        + [pltpu.VMEM((heads, total, 2 * HEAD_DIM), BF16)] * 2,
        kept={8 + number: number for number in range(len(before))},
        flops=10 * 4 * total * total * wide,
    )


def projection_grads(
    scalars, normed, mixed, gathered, branches, weight, vectors, middle_sums, up_sums, count
):
    total, width = normed.shape
    share = mixed[0].shape[1]
    rows = max(min(width, 512 * STEP // total), 128)
    piece = width // count
    units = up_sums.shape[1] // count
    block_rows = branches[0].shape[0]
    own = scalars.shape[0] - 1
    per = share // piece
    column = pl.BlockSpec((block_rows, share), lambda i, w: (0, w[own]))
    if share % 128:
        column = whole((block_rows, share))
        branches = [
            lax.dynamic_slice_in_dim(part, scalars[own] * share, share, 1) for part in branches
        ]

    def to_row(values):
        if values.shape[1] % 128 == 0:
            values = sum(
                values[:, start : start + 128] for start in range(0, values.shape[1], 128)
            )
        return jnp.sum(values.T, axis=0, keepdims=True)

    def kernel(places, normed_ref, gathered_ref, weight_ref, vectors_ref, sums_ref, up_ref, *refs):
        mixed_refs, parts = refs[:3], refs[3 : 3 + len(branches)]
        out, totals, fields = refs[3 + len(branches) :]
        for place, ref in enumerate(mixed_refs):
            totals[place : place + 1, :] = column_sum(ref[...].astype(F32))
        for number in range(count):
            span = slice(number * piece, (number + 1) * piece)
            fields[number, 2:6, :] = sums_ref[0:4, span]
            fields[number, 6:7, :units] = up_ref[:, number * units : (number + 1) * units]

        def block(step):
            begin = pl.ds(pl.multiple_of(step * rows, 128), rows)
            left = normed_ref[:, begin]
            products, gain, shift = [], 0.0, 0.0
            for place, ref in enumerate(mixed_refs):
                product = dot_tn(left, ref[...])
                products.append(product.astype(BF16))
                part = weight_ref[begin, place * share : (place + 1) * share].astype(F32)
                gain = gain + to_row(product * part)
                shift = shift + to_row(part * totals[place : place + 1, :])
            gain = (gain - vectors_ref[1:2, begin] * shift) / vectors_ref[0:1, begin]
            branch = 0.0
            for number, part in enumerate(parts):
                held = gathered_ref[number * block_rows : (number + 1) * block_rows, begin]
                branch = branch + dot_tn(held, part[...])
            branch = branch.astype(BF16)
            for part in range(rows // piece):
                span = slice(part * piece, (part + 1) * piece)
                number = step * (rows // piece) + part
                target = places[count + number]
                for place, product in enumerate(products):
                    out[target, :piece, place * share : (place + 1) * share] = product[span]
                held = fields[number]
                entries = [gain[:, span], shift[:, span]] + [held[i : i + 1] for i in range(2, 7)]
                row = lax.broadcasted_iota(jnp.int32, (16, piece), 0)
                spots = [field_at(number, piece, 4 * share) for number in range(7)]
                for start in range(0, 4 * share, piece):
                    value = jnp.zeros((16, piece), F32)
                    for entry, (line, first) in zip(entries, spots):
                        if first == start:
                            value = jnp.where(row == line, entry, value)
                    out[target, piece:, start : start + piece] = value.astype(BF16)
                natural = ((number // per) ^ places[own]) * per + number % per
                out[places[count + natural], :piece, 3 * share :] = branch[span]

        each(width // rows, block)

    return run(
        kernel,
        [shape((count, piece + 16, 4 * share))],
        grid=(1,),
        scalars=scalars,
        specs=[whole((total, width))] * 2
        + [whole(weight.shape), whole(vectors.shape)]
        + [whole(middle_sums.shape), whole(up_sums.shape)]
        + [whole((total, share))] * 3
        + [column] * len(branches),
        arrays=[normed, gathered, weight, vectors, middle_sums, up_sums, *mixed, *branches],
        out_specs=[whole((count, piece + 16, 4 * share))],
        scratch=[pltpu.VMEM((8, share), F32), pltpu.VMEM((count, 8, piece), F32)],
        flops=2 * total * width * 4 * share,
        vmem=40 if total > STEP else 24,
    )[0]


def normed_back(scalars, mixed, weight, rows):
    total, share = mixed[0].shape
    width = weight.shape[0]

    blocks = blocks_of(total, rows)

    def kernel(_, q_ref, k_ref, v_ref, weight_ref, kept, sent):
        def pair(number):
            for half, out in enumerate((kept, sent)):
                span = pl.ds(pl.multiple_of((2 * number + half) * rows, rows), rows)
                grad = 0.0
                for place, ref in enumerate((q_ref, k_ref, v_ref)):
                    lanes = slice(place * share, (place + 1) * share)
                    grad = grad + dot_nt(ref[span, :], weight_ref[:, lanes])
                out[pl.program_id(0) * (blocks // 2) + number] = grad.astype(BF16)

        each(blocks // 2, pair)

    by_rows = pl.BlockSpec((rows * blocks, share), lambda i, _: (i, 0))
    halves = (total // rows // 2, rows, width)
    return run(
        kernel,
        [shape(halves), shape(halves)],
        grid=(total // rows // blocks,),
        scalars=scalars,
        specs=[by_rows] * 3 + [whole(weight.shape)],
        arrays=[*mixed, weight],
        out_specs=[whole(halves), whole(halves)],
        flops=2 * total * width * 3 * share,
    )


def tokens_back(scalars, addends, tokens, grad_middle, vectors):
    rows, width = tokens.shape
    block = min(rows, 128)

    def kernel(_, *refs):
        parts = refs[: len(addends)]
        tokens_ref, middle_ref, vectors_ref, out = refs[len(addends) :]
        grad = sum(part[0].astype(F32) for part in parts)
        unit, inverse = standard(tokens_ref[...].astype(F32))
        pulled = norm_pull(grad, vectors_ref[0:1, :], unit, inverse)
        out[...] = (middle_ref[...] + pulled).astype(BF16)

    by_rows = pl.BlockSpec((block, width), lambda i, _: (i, 0))
    return run(
        kernel,
        [shape((rows, width))],
        grid=(rows // block,),
        scalars=scalars,
        specs=[pl.BlockSpec((1, block, width), lambda i, _: (0, i, 0))] * len(addends)
        + [by_rows, by_rows, whole(vectors.shape)],
        arrays=[*addends, tokens, grad_middle, vectors],
        out_specs=[by_rows],
    )[0]


def place_attention(scalars, parts, strip, unit_strip):
    columns = parts[0].shape[1]
    share = columns // 4
    along = len(parts)
    own = scalars.shape[0] - 1

    def kernel(places, *refs):
        held, grad_in, grad_out, small, tail = refs[:along], *refs[along : along + 2], *refs[-2:]
        total = 0.0
        for number, ref in enumerate(held):
            spot = places[own] ^ number
            for place in range(4):
                part = ref[:strip, place * share : (place + 1) * share].astype(F32)
                target = grad_out if place == 3 else grad_in
                start = pl.multiple_of((place % 3 * along + spot) * share, 128)
                target[:, pl.ds(start, share)] = part
            extra = ref[strip:, :].astype(F32)
            total = total + extra
            row, start = field_at(6, strip, columns)
            target = pl.multiple_of(spot * unit_strip, 128)
            tail[:, pl.ds(target, unit_strip)] = extra[row : row + 1, start : start + unit_strip]
        for field in range(6):
            row, start = field_at(field, strip, columns)
            small[field : field + 1, :] = total[row : row + 1, start : start + strip]

    outs = [(strip, 3 * share * along), (strip, share * along), (8, strip), (1, along * unit_strip)]
    return run(
        kernel,
        [shape(out, F32) for out in outs],
        grid=(1,),
        scalars=scalars,
        specs=[whole(part.shape) for part in parts],
        arrays=parts,
        out_specs=[whole(out) for out in outs],
    )


def place_feed(scalars, parts, strip, unit_strip, groups):
    width = parts[0].shape[1]
    along = len(parts)
    own = scalars.shape[0] - 1

    def kernel(places, *refs):
        held, (grad_up, grad_down) = refs[:along], refs[along:]
        for number, ref in enumerate(held):
            spot = places[own] ^ number
            for group in range(groups):
                start = pl.multiple_of((group * along + spot) * unit_strip, 128)
                lanes = slice(group * unit_strip, (group + 1) * unit_strip)
                grad_up[:, pl.ds(start, unit_strip)] = ref[:strip, lanes].astype(F32)
            start = pl.multiple_of(spot * unit_strip, 16)
            grad_down[pl.ds(start, unit_strip), :] = ref[strip:, :].astype(F32)

    outs = [(strip, groups * along * unit_strip), (along * unit_strip, width)]
    return run(
        kernel,
        [shape(out, F32) for out in outs],
        grid=(1,),
        scalars=scalars,
        specs=[whole(part.shape) for part in parts],
        arrays=parts,
        out_specs=[whole(out) for out in outs],
    )


def natural(parts, mine):
    return jnp.take(jnp.stack(parts), mine ^ jnp.arange(len(parts)), axis=0)


def local(
    groups,
    along,
    tokens,
    cotangent,
    scene_lengths,
    key_mask,
    project_in,
    project_out,
    up_weight,
    down_weight,
    in_gain,
    in_shift,
    out_shift,
    mid_gain,
    mid_shift,
    up_shift,
    down_shift,
):
    rows, width = tokens.shape[1:]
    total = rows * along
    hidden_units = up_weight.shape[1]
    strip = width // groups
    share = width // along
    unit_strip = hidden_units // groups // along
    units = unit_strip * groups
    mine, group = lax.axis_index("seq"), lax.axis_index("fsdp")
    order = ring_order(groups)
    rings = []
    for device in order_table(order):
        rings += [[*device, place] for place in range(along)]
    scalars = lax.dynamic_index_in_dim(
        jnp.array(rings, jnp.int32), group * along + mine, 0, keepdims=False
    )
    cut = max(unit_strip // 2 // 16, 1) * 16
    own_tokens = tokens[0]
    own_cot = cotangent[0]

    fields = [in_gain, in_shift, out_shift, mid_gain, mid_shift, down_shift]
    in_part = select(
        scalars,
        [project_in] * 3 + [project_out],
        [0, along, 2 * along, 0],
        share,
        [field.reshape(1, strip) for field in fields] + [up_shift.reshape(along, -1)],
    )
    token_parts = spread(after(own_tokens, in_part), along)
    unit, all_tokens = standardize(scalars, token_parts)
    in_parts = ring_gather(in_part, order, strip // 2, [[], [*token_parts[1 : along - 1]]])
    hops = [[part for d, _, part in in_parts if d in (i, groups - i)] for i in range(1, groups // 2 + 1)]

    cot_parts = spread(after(own_cot, token_parts[-2], *hops[2]), along)
    up_weight, down_weight, key_mask = lax.optimization_barrier(
        (up_weight, down_weight, key_mask, *hops[0])
    )[:3]
    up_part = select(scalars, [up_weight] * groups, [along * i for i in range(groups)], unit_strip)
    down_part = lax.dynamic_slice_in_dim(down_weight, mine * unit_strip, unit_strip, 0)
    query_mask, key_table = tables(scalars, scene_lengths, key_mask, along)
    up_part = after(up_part, key_table)
    all_cot = jnp.concatenate(cot_parts)
    joined = up_part.shape[1] == down_part.shape[1]
    normed, query, keys, values, in_weight, out_columns, vectors, up_shift_all = project(
        scalars, unit, in_parts, rows, strip, unit_strip
    )
    outs = spread(out_columns, along)
    pairs = head_pairs(share)[0]
    attended = attend(scalars, query, keys, values, query_mask, key_table, 0)
    if joined:
        feed_part = after(jnp.concatenate([up_part, down_part]), *hops[-1])
        rings = [ring_gather(feed_part, order, strip, [[attended[0]]])]
    else:
        rings = [ring_gather(up_part, order, strip // 2), ring_gather(down_part, order, cut)]
    first_hop = [part for d, _, part in rings[0] if d in (1, groups - 1)]
    for pair in range(1, pairs):
        query = after(query, outs[1], attended[0], all_cot, *first_hop)
        attended = attend(scalars, query, keys, values, query_mask, key_table, pair, attended)
    attended, extra = attended
    all_attended = spread(attended, along)
    if share % 128:
        outs = [jnp.transpose(natural(outs, mine), (1, 0, 2)).reshape(width, width)]

    gathered, normed_mid, middle = attend_out(
        scalars, all_attended, all_tokens, vectors, outs, rows
    )
    active, grad_hidden, kept, sent, grad_up_shift, down_all = feed(
        scalars, normed_mid, all_cot, up_shift_all, rings, rows, strip
    )
    addends, sends = fold(kept, sent, along)
    active, normed_mid = lax.optimization_barrier((active, normed_mid, sends[-1]))[:2]
    up_pieces = outer(scalars, normed_mid, grad_hidden, groups)
    down_pieces = outer(scalars, active, all_cot, groups)
    if joined:
        sums = [RingSum(scalars, [up_pieces, down_pieces], order, strip)]
    else:
        sums = [
            RingSum(scalars, [up_pieces], order, strip // 2),
            RingSum(scalars, [down_pieces], order, cut),
        ]
    feed_sum = sums[0]
    grad_middle, grad_branch, middle_sums = middle_back(
        scalars, addends, middle, own_cot, vectors
    )
    branches = spread(grad_branch, along)
    active = after(active, *feed_sum.advance(grad_branch))
    result_addends, result_sends = fold(*descend(scalars, active, down_all, rows), along)
    ready = after(attended, *feed_sum.advance())
    grads, grad_extra = attended_back(scalars, branches, outs, ready)
    mixed = ()
    for pair in range(pairs):
        mixed = attend_back(
            scalars, query, extra, keys, key_table, values, grads, grad_extra, pair, mixed
        )
        if pair == 0:
            grads = after(grads, result_sends[-1], *feed_sum.advance(mixed[0]))
    pieces = projection_grads(
        scalars,
        after(normed, result_addends[-1]),
        mixed,
        gathered,
        branches,
        in_weight,
        vectors,
        middle_sums,
        grad_up_shift,
        groups,
    )
    feed_grads = [ring.finish() for ring in sums]
    pieces = after(pieces, feed_grads[0])
    attention_sum = RingSum(scalars, [pieces], order, strip // 2)
    feed_parts = spread(feed_grads[0], along)
    mixed = lax.optimization_barrier((*mixed, *attention_sum.advance(feed_parts[-2])))[:3]
    addends, sends = fold(*normed_back(scalars, mixed, in_weight, rows), along)
    fits = joined and not (share % 128 or unit_strip % 128)
    result = middle + vectors[5:6] + sum(part[0].astype(F32) for part in result_addends)
    result = result.astype(BF16)
    done = [result]
    if fits:
        grad_up, grad_down = place_feed(scalars, feed_parts, strip, unit_strip, groups)
        done += [grad_up, grad_down]
    attention_sum.advance(sends[-1], *done)
    grad_tokens = tokens_back(scalars, addends, own_tokens, grad_middle, vectors)
    attention_grads = after(attention_sum.finish(), grad_tokens)

    parts = spread(attention_grads, along)
    if fits:
        grad_in, grad_out, small, tail = place_attention(scalars, parts, strip, unit_strip)
    else:
        both = natural(parts, mine).astype(F32)
        grad_in = jnp.transpose(
            both[:, :strip, : 3 * share].reshape(along, strip, 3, share), (1, 2, 0, 3)
        ).reshape(strip, 3 * width)
        grad_out = jnp.transpose(both[:, :strip, 3 * share :], (1, 0, 2)).reshape(strip, width)
        small = jnp.sum(both[:, strip:], axis=0).reshape(-1, strip)
        tail = both[:, strip:].reshape(along, -1, strip)[:, 6, :unit_strip]
        ups = natural(feed_parts, mine).astype(F32)
        ups = ups.reshape(along, strip, groups, unit_strip)
        grad_up = jnp.transpose(ups, (1, 2, 0, 3)).reshape(strip, hidden_units)
        grad_down = natural(spread(feed_grads[1], along), mine).astype(F32)
        grad_down = grad_down.reshape(along * unit_strip, width)
    small = [small[i] for i in range(6)]
    return (
        result[None],
        grad_tokens[None],
        grad_in,
        grad_out,
        grad_up,
        grad_down,
        small[0],
        small[1],
        small[2],
        small[3],
        small[4],
        tail.reshape(-1),
        small[5],
    )


def solution(mesh):
    by_token = P("fsdp", "seq", None)
    by_row, by_part = P("fsdp", None), P("fsdp")
    return jax.shard_map(
        functools.partial(local, mesh.shape["fsdp"], mesh.shape["seq"]),
        mesh=mesh,
        in_specs=(by_token,) * 2 + (by_row,) * 6 + (by_part,) * 7,
        out_specs=(by_token,) * 2 + (by_row,) * 4 + (by_part,) * 7,
        check_vma=False,
    )
```

```python
import functools
import math

import jax
import jax.numpy as jnp
from jax import lax
from jax.experimental import pallas as pl
from jax.experimental.pallas import tpu as pltpu
from jax.sharding import PartitionSpec as P


HEADS = 16
HEAD_DIM = 64
EPSILON = 1e-05
MASKED = -1e30
MIB = 1 << 20
F32 = jnp.float32
BF16 = jnp.bfloat16
LOG2E = math.log2(math.e)
HBM = pl.BlockSpec(memory_space=pl.ANY)
STEP = 1024


def ring_order(count):
    wide = max(count // 4, 1)
    tall = count // wide
    path = [(row, 0) for row in range(tall)]
    for row in reversed(range(tall)):
        columns = list(range(1, wide))
        if (tall - 1 - row) % 2:
            columns.reverse()
        path += [(row, column) for column in columns]
    return [row * wide + column for row, column in path]


def order_table(order):
    count = len(order)
    rows = []
    for device in range(count):
        spot = order.index(device)
        rows.append(
            [order[(spot + i) % count] for i in range(count)]
            + [(order.index(i) - spot) % count for i in range(count)]
            + [device]
        )
    return rows


def ring_steps(order):
    onward = list(zip(order, order[1:] + order[:1]))
    return onward, [(target, source) for source, target in onward]


def after(value, *others):
    return lax.optimization_barrier((value, *others))[0] if others else value


def ring_gather(block, order, cut, waits=()):
    onward, backward = ring_steps(order)
    count = len(order)
    half = count // 2
    parts = [(0, 0, block)]
    left = right = block
    waits = dict(enumerate(waits, 2))
    for step in range(1, half):
        if step in waits:
            left, right = lax.optimization_barrier((left, right, *waits[step]))[:2]
        left = lax.ppermute(left, "fsdp", onward)
        right = lax.ppermute(right, "fsdp", backward)
        parts += [(count - step, 0, left), (step, 0, right)]
    if half in waits:
        left, right = lax.optimization_barrier((left, right, *waits[half]))[:2]
    parts.append((half, 0, lax.ppermute(left[:cut], "fsdp", onward)))
    if cut < block.shape[0]:
        parts.append((half, cut, lax.ppermute(right[cut:], "fsdp", backward)))
    return parts


class RingSum:
    def __init__(self, scalars, pieces, order, cut):
        self.scalars, self.pieces = scalars, pieces
        self.onward, self.backward = ring_steps(order)
        self.count, self.step = len(order), 1
        far = [part[self.count // 2] for part in pieces]
        if len(far) == 2 and far[0].shape[0] == cut:
            self.left, self.right = far
        else:
            far = jnp.concatenate(far)
            self.left, self.right = far[:cut], far[cut:]
        self.send()

    def send(self):
        self.left = lax.ppermute(self.left, "fsdp", self.onward)
        if self.right is not None and self.right.shape[0]:
            self.right = lax.ppermute(self.right, "fsdp", self.backward)
        else:
            self.right = None

    def advance(self, *waits):
        if self.step == self.count // 2:
            return []
        left = after(self.left, *waits)
        near, far = self.count // 2 - self.step, self.count // 2 + self.step
        self.left, self.right = merge(self.scalars, self.pieces, near, far, left, self.right)
        sent = [self.left, self.right]
        self.send()
        self.step += 1
        return sent

    def finish(self):
        while self.step < self.count // 2:
            self.advance()
        return merge(self.scalars, self.pieces, 0, None, self.left, self.right)


def swap(value, axis, count, bit):
    return lax.ppermute(value, axis, [(i, i ^ bit) for i in range(count)])


def spread(block, count):
    parts = {0: block}
    bit = count // 2
    while bit:
        parts.update({place | bit: swap(part, "seq", count, bit) for place, part in parts.items()})
        bit //= 2
    return [parts[place] for place in range(count)]


def fold(kept, sent, count):
    addends, sends = [kept], [sent]
    bit = 1
    while True:
        addends.append(swap(sends[-1], "seq", count, bit))
        bit *= 2
        if bit == count:
            return addends, sends
        sends.append(sum(part[1::2].astype(F32) for part in addends).astype(BF16))
        addends = [part[0::2] for part in addends]


def run(kernel, outs, *, grid, scalars, specs, arrays, out_specs, scratch=(), flops=0, vmem=20, kept=None):
    return pl.pallas_call(
        kernel,
        out_shape=[jax.ShapeDtypeStruct(o.shape, o.dtype) for o in outs],
        grid_spec=pltpu.PrefetchScalarGridSpec(
            num_scalar_prefetch=1,
            grid=grid,
            in_specs=specs,
            out_specs=out_specs,
            scratch_shapes=list(scratch),
        ),
        input_output_aliases=kept or {},
        compiler_params=pltpu.CompilerParams(vmem_limit_bytes=vmem * MIB),
        cost_estimate=pl.CostEstimate(flops=0, bytes_accessed=1024, transcendentals=0),
    )(scalars, *arrays)


def shape(dims, dtype=BF16):
    return jax.ShapeDtypeStruct(dims, dtype)


def whole(dims):
    return pl.BlockSpec(dims, lambda *_: (0,) * len(dims))


def dot(left, right):
    return jnp.dot(left, right, preferred_element_type=F32)


def dot_nt(left, right):
    return lax.dot_general(left, right, (((1,), (1,)), ((), ())), preferred_element_type=F32)


def dot_tn(left, right):
    return lax.dot_general(left, right, (((0,), (0,)), ((), ())), preferred_element_type=F32)


def each(count, body):
    if count == 1:
        body(0)
    else:
        lax.fori_loop(0, count, lambda number, carry: (body(number), carry)[1], 0)


def blocks_of(total, rows):
    return min(total, 1024) // rows


def standard(values):
    center = values - jnp.mean(values, axis=-1, keepdims=True)
    spread_of = jnp.mean(center * center, axis=-1, keepdims=True)
    inverse = lax.rsqrt(spread_of + EPSILON)
    return center * inverse, inverse


def norm_pull(grad, gain, unit, inverse):
    slope = grad * gain
    first = jnp.mean(slope, axis=-1, keepdims=True)
    second = jnp.mean(slope * unit, axis=-1, keepdims=True)
    return inverse * (slope - first - unit * second)


def column_sum(values):
    return jnp.sum(values, axis=0, keepdims=True)


def landing(parts, refs, fields, places, sems):
    height = sum(part.shape[0] for distance, _, part in parts if distance == 0)
    copies = []
    for (distance, start, part), ref in zip(parts, refs):
        for (low, high), columns, target in fields:
            high = high or height
            begin, end = max(low, start), min(high, start + part.shape[0])
            if begin >= end:
                continue
            offset = places[distance] * (high - low) + (begin - low)
            source = ref.at[pl.ds(begin - start, end - begin)]
            if columns is not None:
                source = ref.at[pl.ds(begin - start, end - begin), pl.ds(*columns)]
            target = target.at[pl.ds(pl.multiple_of(offset, 16), end - begin)]
            copies.append(pltpu.make_async_copy(source, target, sems.at[len(copies)]))
    return copies


def landings(parts, fields):
    return len(parts) * fields


def wait_all(copies):
    for copy in copies:
        copy.start()
    for copy in copies:
        copy.wait()


def merge(scalars, pieces, near, far, left, right):
    heights = [part.shape[1] for part in pieces]
    height, width = sum(heights), pieces[0].shape[2]
    arrays, specs = [], []
    for distance in (near,) if far is None else (near, far):
        for part, rows in zip(pieces, heights):
            arrays.append(part)
            specs.append(pl.BlockSpec((1, rows, width), lambda i, _, d=distance: (d, 0, 0)))
    sums = [part for part in (left, right) if part is not None]

    def kernel(_, *refs):
        held = refs[: len(arrays)]
        sums_refs = list(refs[len(arrays) : len(arrays) + len(sums)])
        outs = refs[len(arrays) + len(sums) :]
        first = left.shape[0]
        for side, out in enumerate(outs):
            start = 0
            for ref, rows in zip(held[side * len(pieces) :], heights):
                own = ref[0].astype(F32)
                span = slice(start, start + rows)
                if far is None:
                    for part in sums_refs:
                        own = own + part[span, :].astype(F32)
                    out[span, :] = own.astype(BF16)
                elif side < len(sums) and sums[side].shape[0] == height:
                    out[span, :] = (own + sums_refs[side][span, :].astype(F32)).astype(BF16)
                else:
                    out[span, :] = own.astype(BF16)
                start += rows
            if far is not None and side < len(sums) and sums[side].shape[0] < height:
                base = 0 if side == 0 else first
                rows = sums[side].shape[0]
                span = slice(base, base + rows)
                total = out[span, :].astype(F32) + sums_refs[side][...].astype(F32)
                out[span, :] = total.astype(BF16)

    whole_out = whole((height, width))
    count = 1 if far is None else 2
    outs = run(
        kernel,
        [shape((height, width))] * count,
        grid=(1,),
        scalars=scalars,
        specs=specs + [whole(part.shape) for part in sums],
        arrays=arrays + sums,
        out_specs=[whole_out] * count,
    )
    return outs[0] if far is None else outs


def select(scalars, arrays, starts, columns, fields=()):
    rows = arrays[0].shape[0]
    own = scalars.shape[0] - 1
    width = len(starts) * columns
    height = rows + (16 if fields else 0)
    if columns % 128:
        pick = lambda array, start, size: lax.dynamic_slice_in_dim(
            array, (start + scalars[own]) * size, size, 1
        )
        parts = [pick(array, start, columns) for array, start in zip(arrays, starts)]
        parts = jnp.concatenate(parts, axis=1)
        if not fields:
            return parts
        line = lax.dynamic_slice_in_dim(fields[-1], scalars[own], 1, 0)
        below = jnp.concatenate([*fields[:-1], line], axis=1)
        below = jnp.pad(below, ((0, 0), (0, 16 * width - below.shape[1])))
        return jnp.concatenate([parts, below.reshape(16, width)])

    def kernel(_, *refs):
        held = refs[: len(arrays) + len(fields)]
        out, sems, *lines = refs[len(held) :]
        mine = lax.axis_index("seq")
        copies = []
        for number, (ref, start) in enumerate(zip(held, starts)):
            begin = pl.multiple_of((start + mine) * columns, 128)
            target = out.at[pl.ds(0, rows), pl.ds(number * columns, columns)]
            copies.append((ref.at[:, pl.ds(begin, columns)], target))
        for number, ref in enumerate(held[len(arrays) :]):
            copies.append((ref, lines[number]))
        wait_all(
            [
                pltpu.make_async_copy(source, target, sems.at[number])
                for number, (source, target) in enumerate(copies)
            ]
        )
        if not fields:
            return
        size = lines[0].shape[1]
        per = width // size
        row = lax.broadcasted_iota(jnp.int32, (16, size), 0)
        values = [line[...].astype(F32) for line in lines]
        chosen = lax.broadcasted_iota(jnp.int32, values[-1].shape, 0) == mine
        values[-1] = column_sum(jnp.where(chosen, values[-1], 0.0))
        for start in range(per):
            value = jnp.zeros(row.shape, F32)
            for number in range(start, len(lines), per):
                value = jnp.where(row == number // per, values[number], value)
            out[rows:, start * size : (start + 1) * size] = value.astype(BF16)

    return run(
        kernel,
        [shape((height, width))],
        grid=(1,),
        scalars=jnp.zeros((1,), jnp.int32),
        specs=[pl.BlockSpec(memory_space=pltpu.HBM)] * (len(arrays) + len(fields)),
        arrays=[*arrays, *fields],
        out_specs=[whole((height, width))],
        scratch=[pltpu.SemaphoreType.DMA((len(arrays) + len(fields),))]
        + [pltpu.VMEM(field.shape, BF16) for field in fields],
        vmem=60 if fields else 20,
    )[0]


def tables(scalars, lengths, key_mask, along):
    total = key_mask.shape[1]
    rows = total // along
    scenes = lengths.shape[1]
    own = scalars.shape[0] - 1

    def kernel(places, lengths_ref, mask_ref, query_table, key_table):
        row = lax.broadcasted_iota(jnp.int32, (HEAD_DIM, rows), 0)
        for number in range(along):
            start = pl.multiple_of((places[own] ^ number) * rows, 128)
            spot = start + lax.broadcasted_iota(jnp.int32, (1, rows), 1)
            keep = mask_ref[:, pl.ds(start, rows)] == 1
            keep = jnp.where(keep, 1.0, 0.0)
            scene = jnp.zeros((1, rows), jnp.int32)
            edge = 0
            for part in range(scenes):
                keep = jnp.where(spot == edge, 1.0, keep)
                edge = edge + lengths_ref[0, part]
                scene = scene + jnp.where(spot >= edge, 1, 0)
            same = jnp.where(row == scene, 1.0, 0.0)
            keys = jnp.where(same * keep > 0.5, 0.0, MASKED)
            keys = jnp.where(row < scenes, keys, jnp.where(row < scenes + 3, -1.0, 0.0))
            span = slice(number * rows, (number + 1) * rows)
            query_table[span, :] = same.T.astype(BF16)
            key_table[span, :] = keys.T.astype(BF16)

    return run(
        kernel,
        [shape((total, HEAD_DIM))] * 2,
        grid=(1,),
        scalars=scalars,
        specs=[pl.BlockSpec(memory_space=pltpu.SMEM), whole(key_mask.shape)],
        arrays=[lengths, key_mask],
        out_specs=[whole((total, HEAD_DIM))] * 2,
    )


def standardize(scalars, tokens):
    rows, width = tokens[0].shape
    total = rows * len(tokens)

    def kernel(_, *refs):
        parts, (unit, joined) = refs[: len(tokens)], refs[len(tokens) :]
        for number, part in enumerate(parts):
            span = slice(number * rows, (number + 1) * rows)
            joined[span, :] = part[...]
            unit[span, :], _ = standard(part[...].astype(F32))

    return run(
        kernel,
        [shape((total, width), F32), shape((total, width))],
        grid=(1,),
        scalars=scalars,
        specs=[whole((rows, width))] * len(tokens),
        arrays=tokens,
        out_specs=[whole((total, width))] * 2,
    )


def field_at(number, strip, columns):
    per = columns // strip
    return number // per, number % per * strip


def project(scalars, unit, parts, rows, strip, unit_strip):
    total, width = unit.shape
    columns = parts[0][2].shape[1]
    share = columns // 4
    groups = width // strip
    count = landings(parts, 3)
    blocks = blocks_of(total, rows)

    def kernel(places, unit_ref, *refs):
        held = refs[: len(parts)]
        normed, query, keys, values, weight, out_weight, vectors, tail, extra, sems, *joint = refs[
            len(parts) :
        ]

        @pl.when(pl.program_id(0) == 0)
        def _():
            fields = [((strip, strip + 16), None, extra)]
            if joint:
                fields.append(((0, strip), None, joint[0]))
            else:
                fields.append(((0, strip), (0, 3 * share), weight))
                fields.append(((0, strip), (3 * share, share), out_weight))
            wait_all(landing(parts, held, fields, places, sems))
            if joint:
                weight[...] = joint[0][:, : 3 * share]
                out_weight[...] = joint[0][:, 3 * share :]
            for number in range(groups):
                block = extra[number * 16 : (number + 1) * 16, :].astype(F32)
                for field in range(7):
                    row, start = field_at(field, strip, columns)
                    part = block[row : row + 1, start : start + strip]
                    vectors[field : field + 1, number * strip : (number + 1) * strip] = part
                tail[:, number * unit_strip : (number + 1) * unit_strip] = part[:, :unit_strip]

        def block(number):
            span = pl.ds(pl.multiple_of(number * rows, rows), rows)
            part = (unit_ref[span, :] * vectors[0:1, :] + vectors[1:2, :]).astype(BF16)
            normed[span, :] = part
            mixed = dot(part, weight[...]).astype(BF16)
            query[span, :] = mixed[:, :share]
            keys[span, :] = mixed[:, share : 2 * share]
            values[span, :] = mixed[:, 2 * share :]

        each(blocks, block)

    by_rows = lambda w: pl.BlockSpec((rows * blocks, w), lambda i, _: (i, 0))
    return run(
        kernel,
        [shape((total, width))]
        + [shape((total, share))] * 3
        + [shape((width, 3 * share)), shape((width, share))]
        + [shape((8, width), F32), shape((1, groups * unit_strip), F32)],
        grid=(total // rows // blocks,),
        scalars=scalars,
        specs=[by_rows(width)] + [HBM] * len(parts),
        arrays=[unit] + [part for _, _, part in parts],
        out_specs=[by_rows(width)]
        + [by_rows(share)] * 3
        + [whole((width, 3 * share)), whole((width, share))]
        + [whole((8, width)), whole((1, groups * unit_strip))],
        scratch=[pltpu.VMEM((groups * 16, columns), BF16), pltpu.SemaphoreType.DMA((count,))]
        + [pltpu.VMEM((width, columns), BF16)] * (share % 128 > 0),
        flops=2 * total * width * 3 * share,
    )


def split_three(values):
    high = values.astype(BF16)
    rest = values - high.astype(F32)
    middle = rest.astype(BF16)
    return high, middle, (rest - middle.astype(F32)).astype(BF16)


def head_pairs(share):
    wide = min(share, 2 * HEAD_DIM)
    return share // wide, wide


def attend(scalars, query, keys, values, query_mask, key_mask, pair, before=()):
    total, share = query.shape
    wide = head_pairs(share)[1]
    rows = min(total, 512 * STEP // total)
    heads = wide // HEAD_DIM
    scale = HEAD_DIM**-0.5

    def kernel(_, q_ref, k_ref, v_ref, qm_ref, km_ref, *refs):
        attended, extra, k_held, v_held = refs[len(before) :]
        ones = jnp.ones((total, HEAD_DIM), BF16)
        place = lax.broadcasted_iota(jnp.int32, (rows, HEAD_DIM), 1)
        for head in range(heads):
            lanes = slice(head * HEAD_DIM, (head + 1) * HEAD_DIM)
            k_held[head] = jnp.concatenate([k_ref[:, lanes], km_ref[...]], axis=1)
            v_held[head] = jnp.concatenate([v_ref[:, lanes], ones], axis=1)

        def block(number):
            span = pl.ds(pl.multiple_of(number * rows, rows), rows)
            mask = qm_ref[span, :]
            outs, extras = [], []
            for head in range(heads):
                lanes = slice(head * HEAD_DIM, (head + 1) * HEAD_DIM)
                q = jnp.concatenate([q_ref[span, lanes], mask], axis=1)
                scores = dot_nt(q, k_held[head])
                top = jnp.max(scores, axis=1, keepdims=True)
                weights = jnp.exp2((scores - top) * (LOG2E * scale)).astype(BF16)
                summed = dot(weights, v_held[head])
                amount = summed[:, HEAD_DIM : HEAD_DIM + 1]
                outs.append(summed[:, :HEAD_DIM] / amount)
                high, middle, low = split_three(top + jnp.log(amount) / scale)
                tail = jnp.where(place == 4, middle, jnp.where(place == 5, low, mask))
                extras.append(jnp.where(place == 3, high, tail))
            attended[span, :] = jnp.concatenate(outs, axis=1).astype(BF16)
            extra[span, :] = jnp.concatenate(extras, axis=1)

        each(total // rows, block)

    fixed = pl.BlockSpec((total, wide), lambda i, _: (0, pair))
    table = whole((total, HEAD_DIM))
    return run(
        kernel,
        [shape((total, share))] * 2,
        grid=(1,),
        scalars=scalars,
        specs=[fixed, fixed, fixed, table, table] + [HBM] * len(before),
        arrays=[query, keys, values, query_mask, key_mask, *before],
        out_specs=[fixed, fixed],
        scratch=[pltpu.VMEM((heads, total, 2 * HEAD_DIM), BF16)] * 2,
        kept={6 + number: number for number in range(len(before))},
        flops=4 * 4 * total * total * wide,
    )


def column_copies(places, refs, target, sems, rows):
    own = places.shape[0] - 1
    if len(refs) == 1:
        return [pltpu.make_async_copy(refs[0].at[rows], target, sems.at[0])]
    columns = refs[0].shape[1]
    return [
        pltpu.make_async_copy(
            ref.at[rows],
            target.at[:, pl.ds(pl.multiple_of((places[own] ^ place) * columns, 128), columns)],
            sems.at[place],
        )
        for place, ref in enumerate(refs)
    ]


def attend_out(scalars, attended, tokens, vectors, outs, rows):
    places_along = len(attended)
    total, width = tokens.shape
    share = attended[0].shape[1]
    own = scalars.shape[0] - 1

    def kernel(places, *refs):
        attended_refs, refs = refs[:places_along], refs[places_along:]
        tokens_ref, vectors_ref = refs[:2]
        held, (gathered, normed, middle_own, out_ref, sems) = (
            refs[2 : 2 + len(outs)],
            refs[2 + len(outs) :],
        )
        step = pl.program_id(0)

        @pl.when(step == 0)
        def _():
            wait_all(column_copies(places, held, out_ref, sems, pl.ds(0, width)))

        for place, ref in enumerate(attended_refs):
            gathered[:, place * share : (place + 1) * share] = ref[...]
        branch = vectors_ref[2:3, :]
        for place in range(places_along):
            start = pl.multiple_of((places[own] ^ place) * share, share)
            branch = branch + dot(attended_refs[place][...], out_ref[pl.ds(start, share), :])
        middle = tokens_ref[...].astype(F32) + branch

        @pl.when(step == 0)
        def _():
            middle_own[...] = middle

        unit, _ = standard(middle)
        normed[...] = (unit * vectors_ref[3:4, :] + vectors_ref[4:5, :]).astype(BF16)

    by_rows = pl.BlockSpec((rows, width), lambda i, _: (i, 0))
    part_of = lambda x: pl.BlockSpec((rows, share), lambda i, _: (i ^ x, 0))
    return run(
        kernel,
        [shape((total, width)), shape((total, width)), shape((rows, width), F32)],
        grid=(places_along,),
        scalars=scalars,
        specs=[part_of(x) for x in range(places_along)]
        + [by_rows, whole(vectors.shape)]
        + [HBM] * len(outs),
        arrays=[*attended, tokens, vectors, *outs],
        out_specs=[by_rows, by_rows, whole((rows, width))],
        scratch=[pltpu.VMEM((width, width), BF16), pltpu.SemaphoreType.DMA((len(outs),))],
        flops=2 * total * width * width,
    )


def feed(scalars, normed, cotangent, up_shift, rings, rows, strip):
    total, width = normed.shape
    units = up_shift.shape[1]
    steps, blocks = total // rows, blocks_of(total, rows)
    parts = [part for ring in rings for part in ring]
    signals = 2 * len(parts)

    def kernel(places, *refs):
        normed_ref, cot_ref, shift_ref = refs[:3]
        held = refs[3 : 3 + len(parts)]
        active, grad_hidden, kept, sent, grad_shift, down, up, sems = refs[3 + len(parts) :]
        step = pl.program_id(0)

        @pl.when(step == 0)
        def _():
            if len(rings) == 1:
                fields = [((0, strip), None, up), ((strip, None), None, down)]
                copies = landing(rings[0], held, fields, places, sems)
            else:
                first, second = held[: len(rings[0])], held[len(rings[0]) :]
                copies = landing(rings[0], first, [((0, None), None, up)], places, sems)
                left = sems.at[pl.ds(len(copies), signals - len(copies))]
                copies += landing(rings[1], second, [((0, None), None, down)], places, left)
            wait_all(copies)
            grad_shift[...] = jnp.zeros_like(grad_shift)

        def pair(number):
            for half, out in enumerate((kept, sent)):
                span = pl.ds(pl.multiple_of((2 * number + half) * rows, rows), rows)
                hidden = dot(normed_ref[span, :], up[...]) + shift_ref[...]
                share_of = 0.5 + 0.5 * lax.erf(hidden * (0.5**0.5))
                active[span, :] = (hidden * share_of).astype(BF16)
                slope = share_of + hidden * (
                    jnp.exp2(hidden * hidden * (-0.5 * LOG2E)) * ((2 * math.pi) ** -0.5)
                )
                grad = (slope * dot_nt(cot_ref[span, :], down[...])).astype(BF16)
                grad_hidden[span, :] = grad
                grad_shift[...] += column_sum(grad.astype(F32))
                out[step * (blocks // 2) + number] = dot_nt(grad, up[...]).astype(BF16)

        each(blocks // 2, pair)

    by_rows = lambda w: pl.BlockSpec((rows * blocks, w), lambda i, _: (i, 0))
    halves = (steps // 2, rows, width)
    return run(
        kernel,
        [
            shape((total, units)),
            shape((total, units)),
            shape(halves),
            shape(halves),
            shape((1, units), F32),
            shape((units, width)),
        ],
        grid=(steps // blocks,),
        scalars=scalars,
        specs=[by_rows(width), by_rows(width), whole(up_shift.shape)] + [HBM] * len(parts),
        arrays=[normed, cotangent, up_shift] + [part for _, _, part in parts],
        out_specs=[
            by_rows(units),
            by_rows(units),
            whole(halves),
            whole(halves),
            whole((1, units)),
            whole((units, width)),
        ],
        scratch=[pltpu.VMEM((width, units), BF16), pltpu.SemaphoreType.DMA((signals,))],
        flops=6 * total * width * units,
        vmem=32,
    )


def descend(scalars, active, down, rows):
    total, units = active.shape
    width = down.shape[1]

    blocks = blocks_of(total, rows)

    def kernel(_, active_ref, down_ref, kept, sent):
        def pair(number):
            for half, out in enumerate((kept, sent)):
                span = pl.ds(pl.multiple_of((2 * number + half) * rows, rows), rows)
                part = dot(active_ref[span, :], down_ref[...]).astype(BF16)
                out[pl.program_id(0) * (blocks // 2) + number] = part

        each(blocks // 2, pair)

    halves = (total // rows // 2, rows, width)
    return run(
        kernel,
        [shape(halves)] * 2,
        grid=(total // rows // blocks,),
        scalars=scalars,
        specs=[pl.BlockSpec((rows * blocks, units), lambda i, _: (i, 0)), whole(down.shape)],
        arrays=[active, down],
        out_specs=[whole(halves)] * 2,
        flops=2 * total * units * width,
    )


def outer(scalars, left, right, count):
    total, height = left.shape
    width = right.shape[1]
    rows = min(height, 512)
    piece = height // count

    def kernel(places, left_ref, right_ref, out):
        def block(number):
            start = pl.multiple_of(number * rows, rows)
            product = dot_tn(left_ref[:, pl.ds(start, rows)], right_ref[...]).astype(BF16)
            for part in range(rows // piece):
                target = places[count + number * (rows // piece) + part]
                out[target] = product[part * piece : (part + 1) * piece]

        each(height // rows, block)

    return run(
        kernel,
        [shape((count, piece, width))],
        grid=(1,),
        scalars=scalars,
        specs=[whole(left.shape), whole(right.shape)],
        arrays=[left, right],
        out_specs=[whole((count, piece, width))],
        flops=2 * total * height * width,
    )[0]


def middle_back(scalars, addends, middle, cotangent, vectors):
    rows, width = middle.shape
    block = min(rows, 128)

    def kernel(_, *refs):
        parts = refs[: len(addends)]
        middle_ref, cot_ref, vectors_ref, grad_middle, grad_branch, sums = refs[len(addends) :]
        grad = sum(part[0].astype(F32) for part in parts)
        cot = cot_ref[...].astype(F32)
        unit, inverse = standard(middle_ref[...])
        total = cot + norm_pull(grad, vectors_ref[3:4, :], unit, inverse)
        grad_middle[...] = total
        branch = total.astype(BF16)
        grad_branch[...] = branch

        @pl.when(pl.program_id(0) == 0)
        def _():
            sums[...] = jnp.zeros_like(sums)

        sums[0:1, :] += column_sum(branch.astype(F32))
        sums[1:2, :] += column_sum(grad * unit)
        sums[2:3, :] += column_sum(grad)
        sums[3:4, :] += column_sum(cot)

    by_rows = pl.BlockSpec((block, width), lambda i, _: (i, 0))
    return run(
        kernel,
        [shape((rows, width), F32), shape((rows, width)), shape((8, width), F32)],
        grid=(rows // block,),
        scalars=scalars,
        specs=[pl.BlockSpec((1, block, width), lambda i, _: (0, i, 0))] * len(addends)
        + [by_rows, by_rows, whole(vectors.shape)],
        arrays=[*addends, middle, cotangent, vectors],
        out_specs=[by_rows, by_rows, whole((8, width))],
    )


def attended_back(scalars, branches, outs, attended):
    count = len(branches)
    total, share = attended.shape
    rows, width = branches[0].shape
    own = scalars.shape[0] - 1

    def kernel(places, *refs):
        parts, held = refs[:count], refs[count : count + len(outs)]
        attended_ref, grads, extras, out_ref, sems = refs[count + len(outs) :]
        start = pl.multiple_of(places[own] * share, 16)
        wait_all(column_copies(places, held, out_ref, sems, pl.ds(start, share)))
        line = lax.broadcasted_iota(jnp.int32, (share, share), 0) // HEAD_DIM
        lane = lax.broadcasted_iota(jnp.int32, (share, share), 1) // HEAD_DIM
        over_head = jnp.where(line == lane, 1.0, 0.0).astype(BF16)
        place = lax.broadcasted_iota(jnp.int32, (rows, share), 1) % HEAD_DIM
        for number, part in enumerate(parts):
            span = slice(number * rows, (number + 1) * rows)
            grad = dot_nt(part[...], out_ref[...]).astype(BF16)
            grads[span, :] = grad
            product = grad.astype(F32) * attended_ref[span, :].astype(F32)
            delta = sum(dot(piece, over_head) for piece in split_three(product))
            high, middle, low = (piece.astype(F32) for piece in split_three(delta))
            extra = jnp.where(place == 4, middle, jnp.where(place == 5, low, 0.0))
            extras[span, :] = jnp.where(place == 3, high, extra).astype(BF16)

    return run(
        kernel,
        [shape((total, share))] * 2,
        grid=(1,),
        scalars=scalars,
        specs=[whole((rows, width))] * count
        + [HBM] * len(outs)
        + [whole((total, share))],
        arrays=[*branches, *outs, attended],
        out_specs=[whole((total, share))] * 2,
        scratch=[pltpu.VMEM((share, width), BF16), pltpu.SemaphoreType.DMA((len(outs),))],
        flops=2 * total * width * share,
    )


def attend_back(scalars, query, extra, keys, key_mask, values, grads, grad_extra, pair, before=()):
    total, share = query.shape
    wide = head_pairs(share)[1]
    rows = min(total, 256 * STEP // total)
    heads = wide // HEAD_DIM
    scale = HEAD_DIM**-0.5

    def kernel(_, q_ref, qx_ref, k_ref, km_ref, v_ref, g_ref, gx_ref, *refs):
        dq_ref, dk_ref, dv_ref, held, q_held, g_held = refs[len(before) :]
        held[...] = jnp.zeros_like(held)
        for head in range(heads):
            lanes = slice(head * HEAD_DIM, (head + 1) * HEAD_DIM)
            q_held[head] = jnp.concatenate([q_ref[:, lanes], qx_ref[:, lanes]], axis=1)
            g_held[head] = jnp.concatenate([g_ref[:, lanes], gx_ref[:, lanes]], axis=1)

        def block(number):
            span = pl.ds(pl.multiple_of(number * rows, rows), rows)
            mask = km_ref[span, :]
            grad_keys, grad_values = [], []
            for head in range(heads):
                lanes = slice(head * HEAD_DIM, (head + 1) * HEAD_DIM)
                key_part = k_ref[span, lanes]
                k = jnp.concatenate([key_part, mask], axis=1)
                v = jnp.concatenate([v_ref[span, lanes], jnp.maximum(mask, -1.0)], axis=1)
                shares = jnp.exp2(dot_nt(k, q_held[head]) * (LOG2E * scale))
                grad_scores = (shares * dot_nt(v, g_held[head])).astype(BF16)
                grad_values.append(dot(shares.astype(BF16), g_ref[:, lanes]))
                grad_keys.append(dot(grad_scores, q_ref[:, lanes]) * scale)
                held[lanes, :] += dot_tn(key_part, grad_scores) * scale
            dk_ref[span, :] = jnp.concatenate(grad_keys, axis=1).astype(BF16)
            dv_ref[span, :] = jnp.concatenate(grad_values, axis=1).astype(BF16)

        each(total // rows, block)
        dq_ref[...] = held[...].T.astype(BF16)

    fixed = pl.BlockSpec((total, wide), lambda i, _: (0, pair))
    return run(
        kernel,
        [shape((total, share))] * 3,
        grid=(1,),
        scalars=scalars,
        specs=[fixed, fixed, fixed, whole((total, HEAD_DIM)), fixed, fixed, fixed]
        + [HBM] * len(before),
        arrays=[query, extra, keys, key_mask, values, grads, grad_extra, *before],
        out_specs=[fixed, fixed, fixed],
        scratch=[pltpu.VMEM((wide, total), F32)]
        + [pltpu.VMEM((heads, total, 2 * HEAD_DIM), BF16)] * 2,
        kept={8 + number: number for number in range(len(before))},
        flops=10 * 4 * total * total * wide,
    )


def projection_grads(
    scalars, normed, mixed, gathered, branches, weight, vectors, middle_sums, up_sums, count
):
    total, width = normed.shape
    share = mixed[0].shape[1]
    rows = max(min(width, 512 * STEP // total), 128)
    piece = width // count
    units = up_sums.shape[1] // count
    block_rows = branches[0].shape[0]
    own = scalars.shape[0] - 1
    per = share // piece
    column = pl.BlockSpec((block_rows, share), lambda i, w: (0, w[own]))
    if share % 128:
        column = whole((block_rows, share))
        branches = [
            lax.dynamic_slice_in_dim(part, scalars[own] * share, share, 1) for part in branches
        ]

    def to_row(values):
        if values.shape[1] % 128 == 0:
            values = sum(
                values[:, start : start + 128] for start in range(0, values.shape[1], 128)
            )
        return jnp.sum(values.T, axis=0, keepdims=True)

    def kernel(places, normed_ref, gathered_ref, weight_ref, vectors_ref, sums_ref, up_ref, *refs):
        mixed_refs, parts = refs[:3], refs[3 : 3 + len(branches)]
        out, totals, fields = refs[3 + len(branches) :]
        for place, ref in enumerate(mixed_refs):
            totals[place : place + 1, :] = column_sum(ref[...].astype(F32))
        for number in range(count):
            span = slice(number * piece, (number + 1) * piece)
            fields[number, 2:6, :] = sums_ref[0:4, span]
            fields[number, 6:7, :units] = up_ref[:, number * units : (number + 1) * units]

        def block(step):
            begin = pl.ds(pl.multiple_of(step * rows, 128), rows)
            left = normed_ref[:, begin]
            products, gain, shift = [], 0.0, 0.0
            for place, ref in enumerate(mixed_refs):
                product = dot_tn(left, ref[...])
                products.append(product.astype(BF16))
                part = weight_ref[begin, place * share : (place + 1) * share].astype(F32)
                gain = gain + to_row(product * part)
                shift = shift + to_row(part * totals[place : place + 1, :])
            gain = (gain - vectors_ref[1:2, begin] * shift) / vectors_ref[0:1, begin]
            branch = 0.0
            for number, part in enumerate(parts):
                held = gathered_ref[number * block_rows : (number + 1) * block_rows, begin]
                branch = branch + dot_tn(held, part[...])
            branch = branch.astype(BF16)
            for part in range(rows // piece):
                span = slice(part * piece, (part + 1) * piece)
                number = step * (rows // piece) + part
                target = places[count + number]
                for place, product in enumerate(products):
                    out[target, :piece, place * share : (place + 1) * share] = product[span]
                held = fields[number]
                entries = [gain[:, span], shift[:, span]] + [held[i : i + 1] for i in range(2, 7)]
                row = lax.broadcasted_iota(jnp.int32, (16, piece), 0)
                spots = [field_at(number, piece, 4 * share) for number in range(7)]
                for start in range(0, 4 * share, piece):
                    value = jnp.zeros((16, piece), F32)
                    for entry, (line, first) in zip(entries, spots):
                        if first == start:
                            value = jnp.where(row == line, entry, value)
                    out[target, piece:, start : start + piece] = value.astype(BF16)
                natural = ((number // per) ^ places[own]) * per + number % per
                out[places[count + natural], :piece, 3 * share :] = branch[span]

        each(width // rows, block)

    return run(
        kernel,
        [shape((count, piece + 16, 4 * share))],
        grid=(1,),
        scalars=scalars,
        specs=[whole((total, width))] * 2
        + [whole(weight.shape), whole(vectors.shape)]
        + [whole(middle_sums.shape), whole(up_sums.shape)]
        + [whole((total, share))] * 3
        + [column] * len(branches),
        arrays=[normed, gathered, weight, vectors, middle_sums, up_sums, *mixed, *branches],
        out_specs=[whole((count, piece + 16, 4 * share))],
        scratch=[pltpu.VMEM((8, share), F32), pltpu.VMEM((count, 8, piece), F32)],
        flops=2 * total * width * 4 * share,
        vmem=40 if total > STEP else 24,
    )[0]


def normed_back(scalars, mixed, weight, rows):
    total, share = mixed[0].shape
    width = weight.shape[0]

    blocks = blocks_of(total, rows)

    def kernel(_, q_ref, k_ref, v_ref, weight_ref, kept, sent):
        def pair(number):
            for half, out in enumerate((kept, sent)):
                span = pl.ds(pl.multiple_of((2 * number + half) * rows, rows), rows)
                grad = 0.0
                for place, ref in enumerate((q_ref, k_ref, v_ref)):
                    lanes = slice(place * share, (place + 1) * share)
                    grad = grad + dot_nt(ref[span, :], weight_ref[:, lanes])
                out[pl.program_id(0) * (blocks // 2) + number] = grad.astype(BF16)

        each(blocks // 2, pair)

    by_rows = pl.BlockSpec((rows * blocks, share), lambda i, _: (i, 0))
    halves = (total // rows // 2, rows, width)
    return run(
        kernel,
        [shape(halves), shape(halves)],
        grid=(total // rows // blocks,),
        scalars=scalars,
        specs=[by_rows] * 3 + [whole(weight.shape)],
        arrays=[*mixed, weight],
        out_specs=[whole(halves), whole(halves)],
        flops=2 * total * width * 3 * share,
    )


def tokens_back(scalars, addends, tokens, grad_middle, vectors):
    rows, width = tokens.shape
    block = min(rows, 128)

    def kernel(_, *refs):
        parts = refs[: len(addends)]
        tokens_ref, middle_ref, vectors_ref, out = refs[len(addends) :]
        grad = sum(part[0].astype(F32) for part in parts)
        unit, inverse = standard(tokens_ref[...].astype(F32))
        pulled = norm_pull(grad, vectors_ref[0:1, :], unit, inverse)
        out[...] = (middle_ref[...] + pulled).astype(BF16)

    by_rows = pl.BlockSpec((block, width), lambda i, _: (i, 0))
    return run(
        kernel,
        [shape((rows, width))],
        grid=(rows // block,),
        scalars=scalars,
        specs=[pl.BlockSpec((1, block, width), lambda i, _: (0, i, 0))] * len(addends)
        + [by_rows, by_rows, whole(vectors.shape)],
        arrays=[*addends, tokens, grad_middle, vectors],
        out_specs=[by_rows],
    )[0]


def place_attention(scalars, parts, strip, unit_strip):
    columns = parts[0].shape[1]
    share = columns // 4
    along = len(parts)
    own = scalars.shape[0] - 1

    def kernel(places, *refs):
        held, grad_in, grad_out, small, tail = refs[:along], *refs[along : along + 2], *refs[-2:]
        total = 0.0
        for number, ref in enumerate(held):
            spot = places[own] ^ number
            for place in range(4):
                part = ref[:strip, place * share : (place + 1) * share].astype(F32)
                target = grad_out if place == 3 else grad_in
                start = pl.multiple_of((place % 3 * along + spot) * share, 128)
                target[:, pl.ds(start, share)] = part
            extra = ref[strip:, :].astype(F32)
            total = total + extra
            row, start = field_at(6, strip, columns)
            target = pl.multiple_of(spot * unit_strip, 128)
            tail[:, pl.ds(target, unit_strip)] = extra[row : row + 1, start : start + unit_strip]
        for field in range(6):
            row, start = field_at(field, strip, columns)
            small[field : field + 1, :] = total[row : row + 1, start : start + strip]

    outs = [(strip, 3 * share * along), (strip, share * along), (8, strip), (1, along * unit_strip)]
    return run(
        kernel,
        [shape(out, F32) for out in outs],
        grid=(1,),
        scalars=scalars,
        specs=[whole(part.shape) for part in parts],
        arrays=parts,
        out_specs=[whole(out) for out in outs],
    )


def place_feed(scalars, parts, strip, unit_strip, groups):
    width = parts[0].shape[1]
    along = len(parts)
    own = scalars.shape[0] - 1

    def kernel(places, *refs):
        held, (grad_up, grad_down) = refs[:along], refs[along:]
        for number, ref in enumerate(held):
            spot = places[own] ^ number
            for group in range(groups):
                start = pl.multiple_of((group * along + spot) * unit_strip, 128)
                lanes = slice(group * unit_strip, (group + 1) * unit_strip)
                grad_up[:, pl.ds(start, unit_strip)] = ref[:strip, lanes].astype(F32)
            start = pl.multiple_of(spot * unit_strip, 16)
            grad_down[pl.ds(start, unit_strip), :] = ref[strip:, :].astype(F32)

    outs = [(strip, groups * along * unit_strip), (along * unit_strip, width)]
    return run(
        kernel,
        [shape(out, F32) for out in outs],
        grid=(1,),
        scalars=scalars,
        specs=[whole(part.shape) for part in parts],
        arrays=parts,
        out_specs=[whole(out) for out in outs],
    )


def natural(parts, mine):
    return jnp.take(jnp.stack(parts), mine ^ jnp.arange(len(parts)), axis=0)


def local(
    groups,
    along,
    tokens,
    cotangent,
    scene_lengths,
    key_mask,
    project_in,
    project_out,
    up_weight,
    down_weight,
    in_gain,
    in_shift,
    out_shift,
    mid_gain,
    mid_shift,
    up_shift,
    down_shift,
):
    rows, width = tokens.shape[1:]
    total = rows * along
    hidden_units = up_weight.shape[1]
    strip = width // groups
    share = width // along
    unit_strip = hidden_units // groups // along
    units = unit_strip * groups
    mine, group = lax.axis_index("seq"), lax.axis_index("fsdp")
    order = ring_order(groups)
    rings = []
    for device in order_table(order):
        rings += [[*device, place] for place in range(along)]
    scalars = lax.dynamic_index_in_dim(
        jnp.array(rings, jnp.int32), group * along + mine, 0, keepdims=False
    )
    cut = max(unit_strip // 2 // 16, 1) * 16
    own_tokens = tokens[0]
    own_cot = cotangent[0]

    fields = [in_gain, in_shift, out_shift, mid_gain, mid_shift, down_shift]
    in_part = select(
        scalars,
        [project_in] * 3 + [project_out],
        [0, along, 2 * along, 0],
        share,
        [field.reshape(1, strip) for field in fields] + [up_shift.reshape(along, -1)],
    )
    token_parts = spread(after(own_tokens, in_part), along)
    unit, all_tokens = standardize(scalars, token_parts)
    in_parts = ring_gather(in_part, order, strip // 2, [[], [*token_parts[1 : along - 1]]])
    hops = [[part for d, _, part in in_parts if d in (i, groups - i)] for i in range(1, groups // 2 + 1)]

    cot_parts = spread(after(own_cot, token_parts[-2], *hops[2]), along)
    up_weight, down_weight, key_mask = lax.optimization_barrier(
        (up_weight, down_weight, key_mask, *hops[0])
    )[:3]
    up_part = select(scalars, [up_weight] * groups, [along * i for i in range(groups)], unit_strip)
    down_part = lax.dynamic_slice_in_dim(down_weight, mine * unit_strip, unit_strip, 0)
    query_mask, key_table = tables(scalars, scene_lengths, key_mask, along)
    up_part = after(up_part, key_table)
    all_cot = jnp.concatenate(cot_parts)
    joined = up_part.shape[1] == down_part.shape[1]
    normed, query, keys, values, in_weight, out_columns, vectors, up_shift_all = project(
        scalars, unit, in_parts, rows, strip, unit_strip
    )
    outs = spread(out_columns, along)
    pairs = head_pairs(share)[0]
    attended = attend(scalars, query, keys, values, query_mask, key_table, 0)
    if joined:
        feed_part = after(jnp.concatenate([up_part, down_part]), *hops[-1])
        rings = [ring_gather(feed_part, order, strip, [[attended[0]]])]
    else:
        rings = [ring_gather(up_part, order, strip // 2), ring_gather(down_part, order, cut)]
    first_hop = [part for d, _, part in rings[0] if d in (1, groups - 1)]
    for pair in range(1, pairs):
        query = after(query, outs[1], attended[0], all_cot, *first_hop)
        attended = attend(scalars, query, keys, values, query_mask, key_table, pair, attended)
    attended, extra = attended
    all_attended = spread(attended, along)
    if share % 128:
        outs = [jnp.transpose(natural(outs, mine), (1, 0, 2)).reshape(width, width)]

    gathered, normed_mid, middle = attend_out(
        scalars, all_attended, all_tokens, vectors, outs, rows
    )
    active, grad_hidden, kept, sent, grad_up_shift, down_all = feed(
        scalars, normed_mid, all_cot, up_shift_all, rings, rows, strip
    )
    addends, sends = fold(kept, sent, along)
    active, normed_mid = lax.optimization_barrier((active, normed_mid, sends[-1]))[:2]
    up_pieces = outer(scalars, normed_mid, grad_hidden, groups)
    down_pieces = outer(scalars, active, all_cot, groups)
    if joined:
        sums = [RingSum(scalars, [up_pieces, down_pieces], order, strip)]
    else:
        sums = [
            RingSum(scalars, [up_pieces], order, strip // 2),
            RingSum(scalars, [down_pieces], order, cut),
        ]
    feed_sum = sums[0]
    grad_middle, grad_branch, middle_sums = middle_back(
        scalars, addends, middle, own_cot, vectors
    )
    branches = spread(grad_branch, along)
    active = after(active, *feed_sum.advance(grad_branch))
    result_addends, result_sends = fold(*descend(scalars, active, down_all, rows), along)
    ready = after(attended, *feed_sum.advance())
    grads, grad_extra = attended_back(scalars, branches, outs, ready)
    mixed = ()
    for pair in range(pairs):
        mixed = attend_back(
            scalars, query, extra, keys, key_table, values, grads, grad_extra, pair, mixed
        )
        if pair == 0:
            grads = after(grads, result_sends[-1], *feed_sum.advance(mixed[0]))
    pieces = projection_grads(
        scalars,
        after(normed, result_addends[-1]),
        mixed,
        gathered,
        branches,
        in_weight,
        vectors,
        middle_sums,
        grad_up_shift,
        groups,
    )
    feed_grads = [ring.finish() for ring in sums]
    pieces = after(pieces, feed_grads[0])
    attention_sum = RingSum(scalars, [pieces], order, strip // 2)
    feed_parts = spread(feed_grads[0], along)
    mixed = lax.optimization_barrier((*mixed, *attention_sum.advance(feed_parts[-2])))[:3]
    addends, sends = fold(*normed_back(scalars, mixed, in_weight, rows), along)
    fits = joined and not (share % 128 or unit_strip % 128)
    result = middle + vectors[5:6] + sum(part[0].astype(F32) for part in result_addends)
    result = result.astype(BF16)
    done = [result]
    if fits:
        grad_up, grad_down = place_feed(scalars, feed_parts, strip, unit_strip, groups)
        done += [grad_up, grad_down]
    attention_sum.advance(sends[-1], *done[:1])
    attention_sum.advance(*done[1:])
    grad_tokens = tokens_back(scalars, addends, own_tokens, grad_middle, vectors)
    attention_grads = after(attention_sum.finish(), grad_tokens)

    parts = spread(attention_grads, along)
    if fits:
        grad_in, grad_out, small, tail = place_attention(scalars, parts, strip, unit_strip)
    else:
        both = natural(parts, mine).astype(F32)
        grad_in = jnp.transpose(
            both[:, :strip, : 3 * share].reshape(along, strip, 3, share), (1, 2, 0, 3)
        ).reshape(strip, 3 * width)
        grad_out = jnp.transpose(both[:, :strip, 3 * share :], (1, 0, 2)).reshape(strip, width)
        small = jnp.sum(both[:, strip:], axis=0).reshape(-1, strip)
        tail = both[:, strip:].reshape(along, -1, strip)[:, 6, :unit_strip]
        ups = natural(feed_parts, mine).astype(F32)
        ups = ups.reshape(along, strip, groups, unit_strip)
        grad_up = jnp.transpose(ups, (1, 2, 0, 3)).reshape(strip, hidden_units)
        grad_down = natural(spread(feed_grads[1], along), mine).astype(F32)
        grad_down = grad_down.reshape(along * unit_strip, width)
    small = [small[i] for i in range(6)]
    return (
        result[None],
        grad_tokens[None],
        grad_in,
        grad_out,
        grad_up,
        grad_down,
        small[0],
        small[1],
        small[2],
        small[3],
        small[4],
        tail.reshape(-1),
        small[5],
    )


def solution(mesh):
    by_token = P("fsdp", "seq", None)
    by_row, by_part = P("fsdp", None), P("fsdp")
    return jax.shard_map(
        functools.partial(local, mesh.shape["fsdp"], mesh.shape["seq"]),
        mesh=mesh,
        in_specs=(by_token,) * 2 + (by_row,) * 6 + (by_part,) * 7,
        out_specs=(by_token,) * 2 + (by_row,) * 4 + (by_part,) * 7,
        check_vma=False,
    )
```
